32 devices in a mesh: layer: 8 (over z, y), dp: 4 (over x, core).
Axes of the slice: x: 2, y: 2, z: 4, core: 2. Of those that a mesh axis runs over, the one named last changes fastest.
Arguments:
- states: float32 [8, 4, 256, 512], P('layer', 'dp'), may hold values from -6 to 6
- target: float32 [4, 256, 512], P('dp'), may hold values from -6 to 6
- lengths: int32 [4], P('dp'), may hold values from 64 to 256, as said below
- qkv_weight: bfloat16 [16, 512, 1536], P('layer'), may hold values from -0.25 to 0.25
- out_weight: bfloat16 [16, 512, 512], P('layer'), may hold values from -0.25 to 0.25
- up_weight: bfloat16 [16, 512, 1024], P('layer'), may hold values from -0.25 to 0.25
- down_weight: bfloat16 [16, 1024, 512], P('layer'), may hold values from -0.1875 to 0.1875
Outputs:
- block_ends: float32 [8, 4, 256, 512], P('layer', 'dp')
- adjoint_starts: float32 [8, 4, 256, 512], P('layer', 'dp')
- grad_qkv: float32 [16, 512, 1536], P('layer')
- grad_out: float32 [16, 512, 512], P('layer')
- grad_up: float32 [16, 512, 1024], P('layer')
- grad_down: float32 [16, 1024, 512], P('layer')
The draws below stay inside these ranges and needn't reach their ends.
Inputs may be any that keep to these rules, and one draw needn't show every extreme that they name: A sequence's valid tokens are its first lengths entries; in every draw some sequence has all 256.
All inputs are finite; a program needn't handle non-finite values.
Results may differ from the reference program's by a relative error of at most 0.024.
Values sent between devices are 32-bit elements; how exact they have to be, the bound alone decides.
No kernel may reach another device: no remote copies, remote signals or barrier semaphores. Data moves between devices by JAX's collectives and lax.ppermute only.
A program may use at most 192 MiB of HBM per device.

```python
import math
import jax
import jax.numpy as jnp
from jax import lax

D = 512
HEADS = 8
FF = 1024
LEN = 256
BLOCKS = 8
LAYERS = 16
SEQ = 4
N_DP = 4


def draw_lengths(key, part):
    key = jax.random.fold_in(key, 7)
    base_key, pick_key = jax.random.split(key)
    draw_values = jax.random.randint(base_key, (SEQ,), LEN // 4, LEN + 1)
    chosen = jax.random.randint(pick_key, (), 0, SEQ)
    return jnp.where(jnp.arange(SEQ) == chosen, LEN, draw_values).astype(jnp.int32)


def level_of(rng, extent, cuts, least, largest):
    factor_of = 1.0
    for position, blocks in cuts:
        draws = jax.random.uniform(jax.random.fold_in(jax.random.fold_in(rng, 6), position), (blocks,), jnp.float32, least / len(cuts), largest / len(cuts))
        factor_of = factor_of * jnp.repeat(jnp.exp(draws), extent[position] // blocks).reshape((-1,) + (1,) * (len(extent) - 1 - position))
    return factor_of


def gaussian(stream_key, shape, width, most, pieces=(), kind=jnp.bfloat16):
    gain = level_of(stream_key, shape, pieces, -0.22, 0.18) if pieces else 1.0
    result = jax.random.normal(stream_key, shape, jnp.float32) * width * gain
    return jnp.minimum(jnp.maximum(result, -most), most).astype(kind)


def setup_inputs(seed: int = 0) -> dict:
    key_list = jax.random.split(jax.random.key(seed), 8)
    states = gaussian(key_list[0], (BLOCKS, SEQ, LEN, D), 1.0, 6.0, ((0, 8), (1, 4)), jnp.float32)
    target = gaussian(key_list[1], (SEQ, LEN, D), 1.0, 6.0, ((0, 4),), jnp.float32)
    lengths = draw_lengths(jax.random.fold_in(key_list[7], 71), 0)
    qkv_weight = gaussian(key_list[3], (LAYERS, D, 3 * D), D ** -0.5, 0.25, ((0, 8),))
    out_weight = gaussian(key_list[4], (LAYERS, D, D), D ** -0.5, 0.25, ((0, 8),))
    up_weight = gaussian(key_list[5], (LAYERS, D, FF), D ** -0.5, 0.25, ((0, 8),))
    down_weight = gaussian(key_list[6], (LAYERS, FF, D), FF ** -0.5, 0.1875, ((0, 8),))
    return {"states": states, "target": target, "lengths": lengths, "qkv_weight": qkv_weight, "out_weight": out_weight, "up_weight": up_weight, "down_weight": down_weight}


STEP = 0.125

def layer_fn(inputs, weight_set, lengths):
    qkv_w, out_w, up_w, down_w = weight_set
    batch_size, seq_len, model_width = inputs.shape
    head_dim = model_width // HEADS
    normed = (inputs * lax.rsqrt(lax.optimization_barrier(jnp.mean(inputs * inputs, axis=-1, keepdims=True)) + 1e-06)).astype(jnp.bfloat16)
    flat = normed.reshape(batch_size * seq_len, model_width)
    packed = jnp.dot(flat, qkv_w, preferred_element_type=jnp.float32).astype(jnp.bfloat16)
    packed = packed.reshape(batch_size, seq_len, 3, HEADS, head_dim).astype(jnp.float32)
    scores = jnp.einsum('bqhd,bkhd->bhqk', packed[:, :, 0], packed[:, :, 1]) * head_dim ** (-0.5)
    positions = jnp.arange(seq_len)
    causal = (positions[None, :] <= positions[:, None])[None, None]
    inside = (positions[None, :] < lengths[:, None])[:, None, None, :]
    scores = jnp.where(causal & inside, scores, -jnp.inf)
    attn_probs = jax.nn.softmax(scores, axis=-1).astype(jnp.bfloat16).astype(jnp.float32)
    context = jnp.einsum('bhqk,bkhd->bqhd', attn_probs, packed[:, :, 2]).astype(jnp.bfloat16)
    context = context.reshape(batch_size * seq_len, model_width)
    attn_out = jnp.dot(context, out_w, preferred_element_type=jnp.float32)
    hidden = jax.nn.gelu(jnp.dot(flat, up_w, preferred_element_type=jnp.float32)).astype(jnp.bfloat16)
    ffn_out = jnp.dot(hidden, down_w, preferred_element_type=jnp.float32)
    return (attn_out + ffn_out).reshape(batch_size, seq_len, model_width)

def advance(inputs, weight_set, lengths):
    return inputs + STEP * layer_fn(inputs, weight_set, lengths)

def adjoint_step(inputs, cotangent, weight_set, lengths):
    _, pullback = jax.vjp(lambda moved: layer_fn(moved, weight_set, lengths), inputs)
    return cotangent + STEP * pullback(cotangent)[0]

def adjoint_with_weights(inputs, cotangent, weight_set, lengths):
    _, pullback = jax.vjp(lambda moved, params: layer_fn(moved, params, lengths), inputs, weight_set)
    back_state, back_params = pullback(cotangent)
    grads = tuple((STEP * param_grad.astype(jnp.float32) for param_grad in back_params))
    return (cotangent + STEP * back_state, grads)

def run_group(starts, target_g, lengths_g, even_w, odd_w):
    forward_map = jax.vmap(advance, in_axes=(0, 0, None))
    layer_map = jax.vmap(layer_fn, in_axes=(0, 0, None))
    back_map = jax.vmap(adjoint_step, in_axes=(0, 0, 0, None))
    final_map = jax.vmap(adjoint_with_weights, in_axes=(0, 0, 0, None))
    first_mid = forward_map(starts, even_w, lengths_g)
    first_end = forward_map(first_mid, odd_w, lengths_g)
    relaxed = jnp.concatenate([starts[:1], first_end[:-1]], axis=0)
    layer_out = layer_map(relaxed, even_w, lengths_g)
    fine_mid = relaxed + STEP * layer_out
    fine_end = forward_map(fine_mid, odd_w, lengths_g)
    defect = fine_end - (relaxed + 2.0 * STEP * layer_out)

    def coarse_forward(current, inputs_j):
        weight_set, defect_j = inputs_j
        value = layer_fn(current, weight_set, lengths_g)
        following = current + 2.0 * STEP * value + defect_j
        return (following, (current, current + STEP * value, following))
    _, (corrected, middles, block_ends) = lax.scan(coarse_forward, starts[0], (even_w, defect))
    valid = (jnp.arange(starts.shape[2])[None, :] < lengths_g[:, None]).astype(jnp.float32)[:, :, None]
    guess = valid[None] * (block_ends - target_g[None])
    terminal = guess[-1]
    first_back = back_map(corrected, back_map(middles, guess, odd_w, lengths_g), even_w, lengths_g)
    relaxed_adj = jnp.concatenate([first_back[1:], terminal[None]], axis=0)
    fine_back = back_map(corrected, back_map(middles, relaxed_adj, odd_w, lengths_g), even_w, lengths_g)

    def coarse_backward(current, inputs_j):
        state_j, weight_set, relaxed_j, fine_j = inputs_j
        _, pullback = jax.vjp(lambda moved: layer_fn(moved, weight_set, lengths_g), state_j)
        gap = current - relaxed_j
        value = fine_j + (gap + 2.0 * STEP * pullback(gap)[0])
        return (value, (current, value))
    _, (adjoint_ends, adjoint_starts) = lax.scan(coarse_backward, terminal, (corrected, even_w, relaxed_adj, fine_back), reverse=True)
    odd_final, odd_grads = final_map(middles, adjoint_ends, odd_w, lengths_g)
    _, even_grads = final_map(corrected, odd_final, even_w, lengths_g)
    partial_grads = tuple((jnp.stack([even_g, odd_g], axis=1).reshape((2 * even_g.shape[0],) + even_g.shape[1:]) for even_g, odd_g in zip(even_grads, odd_grads)))
    return (block_ends, adjoint_starts, partial_grads)

def reference(states, target, lengths, qkv_weight, out_weight, up_weight, down_weight):
    weight_list = (qkv_weight, out_weight, up_weight, down_weight)
    even_w = tuple((weight[0::2] for weight in weight_list))
    odd_w = tuple((weight[1::2] for weight in weight_list))
    block_count, seq_total, seq_len, model_width = states.shape
    group_size = seq_total // N_DP
    grouped_states = jnp.moveaxis(states.reshape(block_count, N_DP, group_size, seq_len, model_width), 1, 0)
    grouped_target = target.reshape(N_DP, group_size, seq_len, model_width)
    grouped_lengths = lengths.reshape(N_DP, group_size)

    def group_step(totals, group_in):
        starts, target_g, lengths_g = group_in
        ends, adj_starts, partial_grads = run_group(starts, target_g, lengths_g, even_w, odd_w)
        totals = tuple((total + part_grad for total, part_grad in zip(totals, partial_grads)))
        return (totals, (ends, adj_starts))
    zero_totals = tuple((jnp.zeros(weight.shape, jnp.float32) for weight in weight_list))
    totals, (ends, adj_starts) = lax.scan(group_step, zero_totals, (grouped_states, grouped_target, grouped_lengths))
    block_ends = jnp.moveaxis(ends, 0, 1).reshape(block_count, seq_total, seq_len, model_width)
    adjoint_starts = jnp.moveaxis(adj_starts, 0, 1).reshape(block_count, seq_total, seq_len, model_width)
    count = float(sum((math.prod(weight.shape[1:]) for weight in weight_list)))
    square = sum((lax.optimization_barrier(jnp.sum(total * total, axis=(1, 2))) for total in totals))
    scale = jnp.sqrt(square / count + 1e-06)[:, None, None]
    results = tuple((total / scale for total in totals))
    return (block_ends, adjoint_starts, results[0], results[1], results[2], results[3])
```

```python
import math

import jax
import jax.numpy as jnp
from jax import lax
from jax.sharding import PartitionSpec as P

HEADS = 8


STEP = 0.125


def shifted(block, axis, distance):
    devices = range(lax.axis_size(axis))
    route = [(i - distance, i) for i in devices if i - distance in devices]
    return lax.ppermute(block, axis, route)


def layer_rows(inputs, weight_set, lengths):
    qkv_w, out_w, up_w, down_w = weight_set
    batch_size, row_count, model_width = inputs.shape
    head_dim = model_width // HEADS
    normed = (inputs * lax.rsqrt(jnp.mean(inputs * inputs, axis=-1, keepdims=True) + 1e-06)).astype(
        jnp.bfloat16
    )
    flat = normed.reshape(batch_size * row_count, model_width)
    packed = jnp.dot(flat, qkv_w, preferred_element_type=jnp.float32).astype(jnp.bfloat16)
    packed = packed.reshape(batch_size, row_count, 3, HEADS, head_dim)
    queries = packed[:, :, 0]
    new_keys = packed[:, :, 1]
    new_vals = packed[:, :, 2]
    scores = jnp.einsum(
        "bqhd,bkhd->bhqk", queries, new_keys, preferred_element_type=jnp.float32
    ) * head_dim ** (-0.5)
    query_pos = jnp.arange(row_count)
    key_pos = jnp.arange(new_keys.shape[1])
    causal = (key_pos[None, :] <= query_pos[:, None])[None, None]
    inside = (key_pos[None, :] < lengths[:, None])[:, None, None, :]
    scores = jnp.where(causal & inside, scores, -jnp.inf)
    attn_probs = jax.nn.softmax(scores, axis=-1).astype(jnp.bfloat16)
    context = jnp.einsum(
        "bhqk,bkhd->bqhd", attn_probs, new_vals, preferred_element_type=jnp.float32
    ).astype(jnp.bfloat16)
    context = context.reshape(batch_size * row_count, model_width)
    attn_out = jnp.dot(context, out_w, preferred_element_type=jnp.float32)
    hidden = jax.nn.gelu(jnp.dot(flat, up_w, preferred_element_type=jnp.float32)).astype(
        jnp.bfloat16
    )
    ffn_out = jnp.dot(hidden, down_w, preferred_element_type=jnp.float32)
    return ((attn_out + ffn_out).reshape(batch_size, row_count, model_width), new_keys, new_vals)


def on_device(states, target, lengths, qkv_weight, out_weight, up_weight, down_weight):
    layer_count = lax.axis_size("layer")
    device = lax.axis_index("layer")
    weight_list = (qkv_weight, out_weight, up_weight, down_weight)
    even_set = tuple((weight[0] for weight in weight_list))
    odd_set = tuple((weight[1] for weight in weight_list))
    starts = states[0]

    def apply_full(inputs, weight_set):
        return layer_rows(inputs, weight_set, lengths)[0]

    first_mid = starts + STEP * apply_full(starts, even_set)
    first_end = first_mid + STEP * apply_full(first_mid, odd_set)
    received = shifted(first_end, "layer", 1)
    corrected = jnp.where(device == 0, starts, received)
    layer_out = apply_full(corrected, even_set)
    middles = corrected + STEP * layer_out
    ends = middles + STEP * apply_full(middles, odd_set)
    defect = ends - (corrected + 2.0 * STEP * layer_out)

    def active_whole(current):
        value = apply_full(current, even_set)
        return (current, current + STEP * value, current + 2.0 * STEP * value + defect)

    for block in range(2, layer_count):
        incoming = lax.ppermute(ends, "layer", [(block - 1, block)])
        corrected, middles, ends = lax.cond(
            device == block,
            lambda: active_whole(incoming),
            lambda: (corrected, middles, ends),
        )
    all_lengths = lax.all_gather(lengths, "dp", tiled=True)
    all_corrected = lax.all_gather(corrected, "dp", tiled=True)
    valid = (jnp.arange(starts.shape[1])[None, :] < lengths[:, None]).astype(jnp.float32)[
        :, :, None
    ]
    guess = valid * (ends - target)

    def linearize(inputs, weight_set, sizes):
        _, pullback = jax.vjp(
            lambda moved, params: layer_rows(moved, params, sizes)[0], inputs, weight_set
        )
        return pullback

    odd_pull = linearize(middles, odd_set, lengths)
    even_pull = linearize(corrected, even_set, lengths)

    def odd_back(cotangent):
        return cotangent + STEP * odd_pull(cotangent)[0]

    def even_back(cotangent):
        return cotangent + STEP * even_pull(cotangent)[0]

    received_adj = shifted(even_back(odd_back(guess)), "layer", -1)
    relaxed_adj = jnp.where(device == layer_count - 1, guess, received_adj)
    fine_back = even_back(odd_back(relaxed_adj))
    adjoint_ends, adjoint_out = relaxed_adj, fine_back

    def adjoint_value(current):
        gap = current - relaxed_adj
        return (current, fine_back + (gap + 2.0 * STEP * even_pull(gap)[0]))

    for block in range(layer_count - 3, -1, -1):
        incoming = lax.ppermute(adjoint_out, "layer", [(block + 1, block)])
        adjoint_ends, adjoint_out = lax.cond(
            device == block,
            lambda: adjoint_value(incoming),
            lambda: (adjoint_ends, adjoint_out),
        )
    all_adjoint = lax.all_gather(adjoint_ends, "dp", tiled=True)
    all_middles = all_corrected + STEP * layer_rows(all_corrected, even_set, all_lengths)[0]
    odd_state, odd_grads = linearize(all_middles, odd_set, all_lengths)(all_adjoint)
    odd_final = all_adjoint + STEP * odd_state
    even_grads = linearize(all_corrected, even_set, all_lengths)(odd_final)[1]
    totals = tuple(
        (
            jnp.stack([STEP * even_g.astype(jnp.float32), STEP * odd_g.astype(jnp.float32)])
            for even_g, odd_g in zip(even_grads, odd_grads)
        )
    )
    count = float(sum((math.prod(weight.shape[1:]) for weight in weight_list)))
    square = sum((jnp.sum(total * total, axis=(1, 2)) for total in totals))
    scale = jnp.sqrt(square / count + 1e-06)[:, None, None]
    results = tuple((total / scale for total in totals))
    return (ends[None], adjoint_out[None], results[0], results[1], results[2], results[3])


def solution(mesh):
    in_specs = (
        P("layer", "dp", None, None),
        P("dp", None, None),
        P("dp"),
        P("layer", None, None),
        P("layer", None, None),
        P("layer", None, None),
        P("layer", None, None),
    )
    out_specs = (
        P("layer", "dp", None, None),
        P("layer", "dp", None, None),
        P("layer", None, None),
        P("layer", None, None),
        P("layer", None, None),
        P("layer", None, None),
    )
    return jax.shard_map(
        on_device, mesh=mesh, in_specs=in_specs, out_specs=out_specs, check_vma=False
    )
```

```python
import functools
import math

import jax
import jax.numpy as jnp
from jax import lax
from jax.experimental import pallas as pl
from jax.experimental.pallas import tpu as pltpu
from jax.sharding import PartitionSpec as P

HEADS = 8
STEP = 0.125
CHUNKS = 2
PAIR = 128
VMEM_LIMIT = 56 * 1024 * 1024

BF = jnp.bfloat16
F32 = jnp.float32
NN = ((1,), (0,))
NT = ((1,), (1,))
TN = ((0,), (0,))
GELU_A = math.sqrt(2.0 / math.pi)
GELU_B = 0.044715


def dot(a, b, dims=NN):
    return lax.dot_general(a, b, (dims, ((), ())), preferred_element_type=F32)


def norm_scale(u):
    return lax.rsqrt(jnp.mean(u * u, axis=-1, keepdims=True) + 1e-06)


def half_masks(value):
    lane = lax.broadcasted_iota(jnp.int32, (1, PAIR), 1)
    first = jnp.where(lane < PAIR // 2, value, 0.0).astype(BF)
    second = jnp.where(lane < PAIR // 2, 0.0, value).astype(BF)
    return (first, second)


def first_half(shape):
    return lax.broadcasted_iota(jnp.int32, shape, 1) < PAIR // 2


def gelu_parts(x):
    inner = jnp.tanh(GELU_A * (x + GELU_B * (x * x * x)))
    return 0.5 * (1.0 + inner), inner


def forward_rows(u, weights, length, row0, old_keys=None, old_vals=None):
    qkv_w, out_w, up_w, down_w = weights
    rows, width = u.shape
    head = width // HEADS
    normed = (u * norm_scale(u)).astype(BF)
    packed = dot(normed, qkv_w[...]).astype(BF)
    queries, new_keys, new_vals = (packed[:, i * width : (i + 1) * width] for i in range(3))
    keys = new_keys if old_keys is None else jnp.concatenate([old_keys, new_keys], axis=0)
    vals = new_vals if old_vals is None else jnp.concatenate([old_vals, new_vals], axis=0)
    shape = (rows, keys.shape[0])
    key_pos = lax.broadcasted_iota(jnp.int32, shape, 1)
    query_pos = lax.broadcasted_iota(jnp.int32, shape, 0) + row0
    seen = (key_pos <= query_pos) & (key_pos < length)
    masks = half_masks(head**-0.5)
    parts = []
    for pair in range(width // PAIR):
        cols = slice(pair * PAIR, (pair + 1) * PAIR)
        outs = []
        for mask in masks:
            scores = dot(queries[:, cols] * mask, keys[:, cols], NT)
            scores = jnp.where(seen, scores, -jnp.inf)
            weight = jnp.exp(scores - jnp.max(scores, axis=-1, keepdims=True))
            probs = (weight * (1.0 / jnp.sum(weight, axis=-1, keepdims=True))).astype(BF)
            outs.append(dot(probs, vals[:, cols]))
        parts.append(jnp.where(first_half((rows, PAIR)), outs[0], outs[1]).astype(BF))
    context = jnp.concatenate(parts, axis=1)
    up = dot(normed, up_w[...])
    hidden = (up * gelu_parts(up)[0]).astype(BF)
    return dot(context, out_w[...]) + dot(hidden, down_w[...]), new_keys, new_vals


def linearize_rows(u, weights, length, packed_ref, probs_ref, slope_ref, factors=None):
    qkv_w, _, up_w, _ = weights
    rows, width = u.shape
    head = width // HEADS
    normed = (u * norm_scale(u)).astype(BF)
    packed = dot(normed, qkv_w[...]).astype(BF)
    packed_ref[...] = packed
    up = dot(normed, up_w[...])
    gate, inner = gelu_parts(up)
    slope = gate + 0.5 * up * (1.0 - inner * inner) * (GELU_A + 3.0 * GELU_A * GELU_B * up * up)
    slope_ref[...] = slope.astype(BF)
    key_pos = lax.broadcasted_iota(jnp.int32, (rows, rows), 0)
    query_pos = lax.broadcasted_iota(jnp.int32, (rows, rows), 1)
    seen = (key_pos <= query_pos) & (key_pos < length)
    masks = half_masks(head**-0.5)
    parts = []
    for pair in range(width // PAIR):
        cols = slice(pair * PAIR, (pair + 1) * PAIR)
        queries = packed[:, cols]
        keys = packed[:, width + pair * PAIR : width + (pair + 1) * PAIR]
        vals = packed[:, 2 * width + pair * PAIR : 2 * width + (pair + 1) * PAIR]
        outs = []
        for half, mask in enumerate(masks):
            scores = dot(keys, queries * mask, NT)
            scores = jnp.where(seen, scores, -jnp.inf)
            weight = jnp.exp(scores - jnp.max(scores, axis=0, keepdims=True))
            probs = (weight * (1.0 / jnp.sum(weight, axis=0, keepdims=True))).astype(BF)
            probs_ref[2 * pair + half] = probs
            if factors is not None:
                outs.append(dot(probs, vals, TN))
        if factors is not None:
            parts.append(jnp.where(first_half((rows, PAIR)), outs[0], outs[1]).astype(BF))
    if factors is not None:
        normed_ref, context_ref, hidden_ref = factors
        normed_ref[...] = normed
        context_ref[...] = jnp.concatenate(parts, axis=1)
        hidden_ref[...] = (up * gate).astype(BF)


def backward_rows(ct, u, weights, packed_ref, probs_ref, slope_ref, row0, later=None):
    qkv_w, out_w, up_w, down_w = weights
    rows, width = ct.shape
    head = width // HEADS
    end = row0 + rows
    low = ct.astype(BF)
    d_context = dot(low, out_w[...], NT).astype(BF)
    d_hidden = dot(low, down_w[...], NT)
    d_up = (d_hidden * slope_ref[row0:end, :].astype(F32)).astype(BF)
    ones = half_masks(1.0)
    d_queries, d_keys, d_vals = [], [], []
    for pair in range(width // PAIR):
        lo = pair * PAIR
        queries = packed_ref[row0:end, lo : lo + PAIR]
        keys = packed_ref[0:end, width + lo : width + lo + PAIR]
        vals = packed_ref[0:end, 2 * width + lo : 2 * width + lo + PAIR]
        d_pair = d_context[:, lo : lo + PAIR]
        dq, dk, dv = [], [], []
        for half, mask in enumerate(ones):
            probs = probs_ref[2 * pair + half, 0:end, row0:end]
            wide = probs.astype(F32)
            d_probs = dot(vals, d_pair * mask, NT)
            mean = jnp.sum(wide * d_probs, axis=0, keepdims=True)
            d_scores = (wide * (d_probs - mean) * head**-0.5).astype(BF)
            dq.append(dot(d_scores, keys, TN))
            dk.append(dot(d_scores, queries))
            dv.append(dot(probs, d_pair))
        d_queries.append(jnp.where(first_half((rows, PAIR)), dq[0], dq[1]))
        d_keys.append(jnp.where(first_half((end, PAIR)), dk[0], dk[1]))
        d_vals.append(jnp.where(first_half((end, PAIR)), dv[0], dv[1]))
    d_keys = jnp.concatenate(d_keys, axis=1)
    d_vals = jnp.concatenate(d_vals, axis=1)
    if later is not None:
        d_keys = d_keys + later[0:end, 0:width]
        d_vals = d_vals + later[0:end, width : 2 * width]
    d_packed = jnp.concatenate([*d_queries, d_keys[row0:end], d_vals[row0:end]], axis=1).astype(BF)
    d_normed = dot(d_packed, qkv_w[...], NT) + dot(d_up, up_w[...], NT)
    scale = norm_scale(u)
    unit = u * scale
    d_state = scale * (d_normed - unit * jnp.mean(unit * d_normed, axis=-1, keepdims=True))
    earlier = None
    if row0 > 0:
        earlier = jnp.concatenate([d_keys[0:row0], d_vals[0:row0]], axis=1)
    return d_state, earlier, (d_packed, d_up, low)


def relax_kernel(length, starts, *refs):
    even, odd, out = refs[0:4], refs[4:8], refs[8]
    state = starts[...]
    state = state + STEP * forward_rows(state, even, length[0], 0)[0]
    out[...] = state + STEP * forward_rows(state, odd, length[0], 0)[0]


def fine_kernel(length, relaxed, *refs):
    even, odd = refs[0:4], refs[4:8]
    middles, ends, defect = refs[8:]
    state = relaxed[...]
    value = forward_rows(state, even, length[0], 0)[0]
    middle = state + STEP * value
    end = middle + STEP * forward_rows(middle, odd, length[0], 0)[0]
    middles[...] = middle
    ends[...] = end
    defect[...] = end - (state + 2.0 * STEP * value)


def coarse_kernel(chunk, length, state, defect, *refs):
    weights, refs = refs[0:4], refs[4:]
    old_keys = old_vals = None
    if chunk > 0:
        old = refs[0][...]
        refs = refs[1:]
        width = state.shape[1]
        old_keys, old_vals = old[:, 0:width], old[:, width : 2 * width]
    ends, middles = refs[0:2]
    current = state[...]
    rows = current.shape[0]
    value, keys, vals = forward_rows(
        current, weights, length[0], chunk * rows, old_keys, old_vals
    )
    middles[...] = current + STEP * value
    ends[...] = current + 2.0 * STEP * value + defect[...]
    if len(refs) > 2:
        both = jnp.concatenate([keys, vals], axis=1)
        refs[2][...] = both if chunk == 0 else jnp.concatenate([old, both], axis=0)


def turn_kernel(length, corrected, middles, ends, target, *refs):
    even, odd = refs[0:4], refs[4:8]
    even_saved, odd_saved, guess_ref, out = refs[8:11], refs[11:14], refs[14], refs[15]
    rows, width = ends.shape
    position = lax.broadcasted_iota(jnp.int32, (rows, width), 0)
    guess = jnp.where(position < length[0], ends[...] - target[...], 0.0)
    guess_ref[...] = guess
    linearize_rows(middles[...], odd, length[0], *odd_saved)
    linearize_rows(corrected[...], even, length[0], *even_saved)
    state = guess + STEP * backward_rows(guess, middles[...], odd, *odd_saved, 0)[0]
    out[...] = state + STEP * backward_rows(state, corrected[...], even, *even_saved, 0)[0]


def back_kernel(adjoint, corrected, middles, *refs):
    even, odd = refs[0:4], refs[4:8]
    even_saved, odd_saved, out = refs[8:11], refs[11:14], refs[14]
    state = adjoint[...]
    state = state + STEP * backward_rows(state, middles[...], odd, *odd_saved, 0)[0]
    out[...] = state + STEP * backward_rows(state, corrected[...], even, *even_saved, 0)[0]


def adjoint_kernel(chunk, chunks, incoming, relaxed, fine, corrected, *refs):
    weights, saved, refs = refs[0:4], refs[4:7], refs[7:]
    later = None
    if chunk < chunks - 1:
        later = refs[0][...]
        refs = refs[1:]
    rows = incoming.shape[0]
    gap = incoming[...] - relaxed[...]
    change, earlier, _ = backward_rows(
        gap, corrected[...], weights, *saved, chunk * rows, later
    )
    refs[0][...] = fine[...] + (gap + 2.0 * STEP * change)
    if chunk > 0:
        refs[1][...] = earlier


def all_linear_kernel(order, lengths, corrected, *refs):
    even, odd = refs[0:4], refs[4:8]
    middles = refs[8]
    even_saved, odd_saved = refs[9:12], refs[12:15]
    even_factors, odd_factors = refs[15:18], refs[18:21]
    length = lengths[order[pl.program_id(0)]]
    state = corrected[...]
    linearize_rows(state, even, length, *even_saved, even_factors)
    value = dot(even_factors[1][...], even[1][...]) + dot(even_factors[2][...], even[3][...])
    middle = state + STEP * value
    middles[...] = middle
    linearize_rows(middle, odd, length, *odd_saved, odd_factors)


def all_back_kernel(order, adjoint, corrected, *refs):
    even, odd = refs[0:4], refs[4:8]
    middles, even_saved, odd_saved = refs[8], refs[9:12], refs[12:15]
    outs = refs[15:]
    state = adjoint[...]
    change, _, right = backward_rows(state, middles[...], odd, *odd_saved, 0)
    for ref, value in zip(outs[3:6], right):
        ref[...] = value
    state = state + STEP * change
    _, _, right = backward_rows(state, corrected[...], even, *even_saved, 0)
    for ref, value in zip(outs[0:3], right):
        ref[...] = value


def call(kernel, outs, smem, *args):
    specs = [pl.BlockSpec(memory_space=pltpu.SMEM)] * len(smem)
    specs += [pl.BlockSpec(memory_space=pltpu.VMEM)] * len(args)
    return pl.pallas_call(
        kernel,
        out_shape=tuple(jax.ShapeDtypeStruct(shape, kind) for shape, kind in outs),
        in_specs=specs,
        out_specs=tuple(pl.BlockSpec(memory_space=pltpu.VMEM) for _ in outs),
        compiler_params=pltpu.CompilerParams(vmem_limit_bytes=VMEM_LIMIT),
    )(*smem, *args)


def call_each(kernel, outs, order, smem, gathered, fixed, moving=()):
    def block(shape):
        rest = (0,) * (len(shape) - 1)
        return pl.BlockSpec((None, *shape[1:]), lambda i, order: (i, *rest))

    def placed(shape):
        rest = (0,) * (len(shape) - 1)
        return pl.BlockSpec((None, *shape[1:]), lambda i, order: (order[i], *rest))

    def whole(shape):
        rest = (0,) * len(shape)
        return pl.BlockSpec(shape, lambda i, order: rest)

    return pl.pallas_call(
        kernel,
        grid_spec=pltpu.PrefetchScalarGridSpec(
            num_scalar_prefetch=1,
            grid=order.shape,
            in_specs=[pl.BlockSpec(memory_space=pltpu.SMEM)] * len(smem)
            + [placed(x.shape) for x in gathered]
            + [whole(x.shape) for x in fixed]
            + [block(x.shape) for x in moving],
            out_specs=tuple(block(shape) for shape, _ in outs),
        ),
        out_shape=tuple(jax.ShapeDtypeStruct(shape, kind) for shape, kind in outs),
        compiler_params=pltpu.CompilerParams(vmem_limit_bytes=VMEM_LIMIT),
    )(order, *smem, *gathered, *fixed, *moving)


def gather_dp(block):
    count = lax.axis_size("dp")
    if count == 1:
        return block[None]
    mine = [block]
    for turn in range(1, count // 2):
        route = [(i, (i + 2 * turn) % count) for i in range(count)]
        mine.append(lax.ppermute(block, "dp", route))
    mine = jnp.stack(mine)
    theirs = lax.ppermute(mine, "dp", [(i, i ^ 1) for i in range(count)])
    both = jnp.stack([mine, theirs], axis=1)
    return both.reshape(count, *block.shape)


def gathered_order():
    count = lax.axis_size("dp")
    place = lax.axis_index("dp")
    other = jnp.arange(count, dtype=jnp.int32)
    turn = (place // 2 - other // 2) % max(count // 2, 1)
    return (2 * turn + (place + other) % 2).astype(jnp.int32) if count > 1 else other


def on_device(states, target, lengths, qkv_weight, out_weight, up_weight, down_weight):
    layer_count = lax.axis_size("layer")
    device = lax.axis_index("layer")
    weight_list = (qkv_weight, out_weight, up_weight, down_weight)
    even = tuple((weight[0] for weight in weight_list))
    odd = tuple((weight[1] for weight in weight_list))
    starts, goal = states[0, 0], target[0]
    rows, width = starts.shape
    hidden = up_weight.shape[2]
    part = rows // CHUNKS
    full = ((rows, width), F32)
    piece = ((part, width), F32)
    saved = (((rows, 3 * width), BF), ((HEADS, rows, rows), BF), ((rows, hidden), BF))

    def pieces(array):
        return [array[c * part : (c + 1) * part] for c in range(CHUNKS)]

    (first_end,) = call(relax_kernel, (full,), (lengths,), starts, *even, *odd)
    received = lax.ppermute(
        first_end, "layer", [(i, i + 1) for i in range(layer_count - 1)]
    )
    corrected = jnp.where(device == 0, starts, received)
    middles, ends, defect = call(
        fine_kernel, (full, full, full), (lengths,), corrected, *even, *odd
    )
    corrected, middles, ends, defect = (
        pieces(array) for array in (corrected, middles, ends, defect)
    )
    stores = [jnp.zeros((c * part, 2 * width), BF) for c in range(1, CHUNKS)]
    for block in range(2, layer_count):
        incoming = [lax.ppermute(ends[c], "layer", [(block - 1, block)]) for c in range(CHUNKS)]
        for c in range(CHUNKS):
            outs = (piece, piece)
            if c < CHUNKS - 1:
                outs += (((((c + 1) * part), 2 * width), BF),)
            old = () if c == 0 else (stores[c - 1],)

            def active(state, defect_c, old, c=c, outs=outs):
                got = call(
                    functools.partial(coarse_kernel, c), outs, (lengths,), state, defect_c,
                    *even, *old
                )
                return (state, *got)

            kept = (corrected[c], ends[c], middles[c])
            if c < CHUNKS - 1:
                kept += (stores[c],)
            got = lax.cond(
                device == block,
                functools.partial(active, incoming[c], defect[c], old),
                lambda kept=kept: kept,
            )
            corrected[c], ends[c], middles[c] = got[0:3]
            if c < CHUNKS - 1:
                stores[c] = got[3]
    corrected, middles, ends = (
        jnp.concatenate(array, axis=0) for array in (corrected, middles, ends)
    )
    *kept, guess, turned = call(
        turn_kernel, (*saved, *saved, full, full), (lengths,), corrected, middles, ends, goal,
        *even, *odd
    )
    even_saved = kept[0:3]
    received = lax.ppermute(
        turned, "layer", [(i + 1, i) for i in range(layer_count - 1)]
    )
    relaxed = jnp.where(device == layer_count - 1, guess, received)
    (fine,) = call(back_kernel, (full,), (), relaxed, corrected, middles, *even, *odd, *kept)
    late, fine = lax.optimization_barrier((corrected, fine))
    every = gather_dp(late)
    sizes = gather_dp(lengths)[:, 0]
    count = every.shape[0]
    order = gathered_order()
    stack = lambda shapes: tuple(((count, *shape), kind) for shape, kind in shapes)
    factors = (((rows, width), BF), ((rows, width), BF), ((rows, hidden), BF))
    linear = call_each(
        all_linear_kernel, stack((full, *saved, *saved, *factors, *factors)), order,
        (sizes,), (every,), (*even, *odd)
    )
    adjoint_ends, adjoint_out = pieces(relaxed), pieces(fine)
    relaxed, fine, states_c = (pieces(array) for array in (relaxed, fine, corrected))
    carried = [jnp.zeros((c * part, 2 * width), F32) for c in range(1, CHUNKS)]
    for block in range(layer_count - 3, -1, -1):
        incoming = [
            lax.ppermute(adjoint_out[c], "layer", [(block + 1, block)])
            for c in range(CHUNKS - 1, -1, -1)
        ][::-1]
        if block == layer_count - 3:
            incoming, linear = lax.optimization_barrier((incoming, linear))
        for c in range(CHUNKS - 1, -1, -1):
            outs = (piece,)
            if c > 0:
                outs += (((c * part, 2 * width), F32),)
            later = () if c == CHUNKS - 1 else (carried[c],)

            def active(state, rest, later, c=c, outs=outs):
                got = call(
                    functools.partial(adjoint_kernel, c, CHUNKS), outs, (), state, *rest,
                    *even, *even_saved, *later
                )
                return (state, *got)

            old = (adjoint_ends[c], adjoint_out[c])
            if c > 0:
                old += (carried[c - 1],)
            got = lax.cond(
                device == block,
                functools.partial(active, incoming[c], (relaxed[c], fine[c], states_c[c]), later),
                lambda old=old: old,
            )
            adjoint_ends[c], adjoint_out[c] = got[0:2]
            if c > 0:
                carried[c - 1] = got[2]
    adjoint_ends, adjoint_out = (
        jnp.concatenate(array, axis=0) for array in (adjoint_ends, adjoint_out)
    )
    every_adjoint = gather_dp(adjoint_ends)
    lefts = (linear[7:10], linear[10:13])
    rights = (((rows, 3 * width), BF), ((rows, hidden), BF), ((rows, width), BF))
    got = call_each(
        all_back_kernel, stack((*rights, *rights)), order, (),
        (every_adjoint, every), (*even, *odd), (linear[0], *linear[1:7])
    )
    totals = [[], [], [], []]
    for left, right in zip(lefts, (got[0:3], got[3:6])):
        normed, context, gated = (x.reshape(count * rows, -1) for x in left)
        d_packed, d_up, d_out = (x.reshape(count * rows, -1) for x in right)
        for total, pair in zip(
            totals, ((normed, d_packed), (context, d_out), (normed, d_up), (gated, d_out))
        ):
            total.append(STEP * dot(*pair, TN))
    totals = tuple(jnp.stack(total) for total in totals)
    weight_count = float(sum((math.prod(weight.shape[1:]) for weight in weight_list)))
    square = sum((jnp.sum(total * total, axis=(1, 2)) for total in totals))
    scale = jnp.sqrt(square / weight_count + 1e-06)[:, None, None]
    results = tuple((total / scale for total in totals))
    return (ends[None, None], adjoint_out[None, None], *results)


def solution(mesh):
    in_specs = (
        P("layer", "dp", None, None),
        P("dp", None, None),
        P("dp"),
        P("layer", None, None),
        P("layer", None, None),
        P("layer", None, None),
        P("layer", None, None),
    )
    out_specs = (
        P("layer", "dp", None, None),
        P("layer", "dp", None, None),
        P("layer", None, None),
        P("layer", None, None),
        P("layer", None, None),
        P("layer", None, None),
    )
    return jax.shard_map(
        on_device, mesh=mesh, in_specs=in_specs, out_specs=out_specs, check_vma=False
    )
```

```python
import functools
import math

import jax
import jax.numpy as jnp
from jax import lax
from jax.experimental import pallas as pl
from jax.experimental.pallas import tpu as pltpu
from jax.sharding import PartitionSpec as P

HEADS = 8
STEP = 0.125
CHUNKS = 2
PAIR = 128
SMALL_LIMIT = 20 * 1024 * 1024
LARGE_LIMIT = 36 * 1024 * 1024

BF = jnp.bfloat16
F32 = jnp.float32
NN = ((1,), (0,))
NT = ((1,), (1,))
TN = ((0,), (0,))
GELU_A = math.sqrt(2.0 / math.pi)
GELU_B = 0.044715


def dot(a, b, dims=NN):
    return lax.dot_general(a, b, (dims, ((), ())), preferred_element_type=F32)


def norm_scale(u):
    return lax.rsqrt(jnp.mean(u * u, axis=-1, keepdims=True) + 1e-06)


def half_masks(value):
    lane = lax.broadcasted_iota(jnp.int32, (1, PAIR), 1)
    first = jnp.where(lane < PAIR // 2, value, 0.0).astype(BF)
    second = jnp.where(lane < PAIR // 2, 0.0, value).astype(BF)
    return (first, second)


def first_half(shape):
    return lax.broadcasted_iota(jnp.int32, shape, 1) < PAIR // 2


def gelu_parts(x):
    inner = jnp.tanh(GELU_A * (x + GELU_B * (x * x * x)))
    return 0.5 * (1.0 + inner), inner


def forward_rows(u, weights, length, row0, old_keys=None, old_vals=None):
    qkv_w, out_w, up_w, down_w = weights
    rows, width = u.shape
    head = width // HEADS
    normed = (u * norm_scale(u)).astype(BF)
    packed = dot(normed, qkv_w[...]).astype(BF)
    queries, new_keys, new_vals = (packed[:, i * width : (i + 1) * width] for i in range(3))
    keys = new_keys if old_keys is None else jnp.concatenate([old_keys, new_keys], axis=0)
    vals = new_vals if old_vals is None else jnp.concatenate([old_vals, new_vals], axis=0)
    shape = (rows, keys.shape[0])
    key_pos = lax.broadcasted_iota(jnp.int32, shape, 1)
    query_pos = lax.broadcasted_iota(jnp.int32, shape, 0) + row0
    seen = (key_pos <= query_pos) & (key_pos < length)
    masks = half_masks(head**-0.5)
    parts = []
    for pair in range(width // PAIR):
        cols = slice(pair * PAIR, (pair + 1) * PAIR)
        outs = []
        for mask in masks:
            scores = dot(queries[:, cols] * mask, keys[:, cols], NT)
            scores = jnp.where(seen, scores, -jnp.inf)
            weight = jnp.exp(scores - jnp.max(scores, axis=-1, keepdims=True))
            probs = (weight * (1.0 / jnp.sum(weight, axis=-1, keepdims=True))).astype(BF)
            outs.append(dot(probs, vals[:, cols]))
        parts.append(jnp.where(first_half((rows, PAIR)), outs[0], outs[1]).astype(BF))
    context = jnp.concatenate(parts, axis=1)
    up = dot(normed, up_w[...])
    hidden = (up * gelu_parts(up)[0]).astype(BF)
    return dot(context, out_w[...]) + dot(hidden, down_w[...]), new_keys, new_vals


def linearize_rows(u, weights, length, packed_ref, probs_ref, slope_ref, factors=None):
    qkv_w, _, up_w, _ = weights
    rows, width = u.shape
    head = width // HEADS
    normed = (u * norm_scale(u)).astype(BF)
    packed = dot(normed, qkv_w[...]).astype(BF)
    packed_ref[...] = packed
    up = dot(normed, up_w[...])
    gate, inner = gelu_parts(up)
    slope = gate + 0.5 * up * (1.0 - inner * inner) * (GELU_A + 3.0 * GELU_A * GELU_B * up * up)
    slope_ref[...] = slope.astype(BF)
    key_pos = lax.broadcasted_iota(jnp.int32, (rows, rows), 0)
    query_pos = lax.broadcasted_iota(jnp.int32, (rows, rows), 1)
    seen = (key_pos <= query_pos) & (key_pos < length)
    masks = half_masks(head**-0.5)
    parts = []
    for pair in range(width // PAIR):
        cols = slice(pair * PAIR, (pair + 1) * PAIR)
        queries = packed[:, cols]
        keys = packed[:, width + pair * PAIR : width + (pair + 1) * PAIR]
        vals = packed[:, 2 * width + pair * PAIR : 2 * width + (pair + 1) * PAIR]
        outs = []
        for half, mask in enumerate(masks):
            scores = dot(keys, queries * mask, NT)
            scores = jnp.where(seen, scores, -jnp.inf)
            weight = jnp.exp(scores - jnp.max(scores, axis=0, keepdims=True))
            probs = (weight * (1.0 / jnp.sum(weight, axis=0, keepdims=True))).astype(BF)
            probs_ref[2 * pair + half] = probs
            if factors is not None:
                outs.append(dot(probs, vals, TN))
        if factors is not None:
            parts.append(jnp.where(first_half((rows, PAIR)), outs[0], outs[1]).astype(BF))
    if factors is not None:
        normed_ref, context_ref, hidden_ref = factors
        normed_ref[...] = normed
        context_ref[...] = jnp.concatenate(parts, axis=1)
        hidden_ref[...] = (up * gate).astype(BF)


def backward_rows(ct, u, weights, packed_ref, probs_ref, slope_ref, row0, later=None):
    qkv_w, out_w, up_w, down_w = weights
    rows, width = ct.shape
    head = width // HEADS
    end = row0 + rows
    low = ct.astype(BF)
    d_context = dot(low, out_w[...], NT).astype(BF)
    d_hidden = dot(low, down_w[...], NT)
    d_up = (d_hidden * slope_ref[row0:end, :].astype(F32)).astype(BF)
    ones = half_masks(1.0)
    d_queries, d_keys, d_vals = [], [], []
    for pair in range(width // PAIR):
        lo = pair * PAIR
        queries = packed_ref[row0:end, lo : lo + PAIR]
        keys = packed_ref[0:end, width + lo : width + lo + PAIR]
        vals = packed_ref[0:end, 2 * width + lo : 2 * width + lo + PAIR]
        d_pair = d_context[:, lo : lo + PAIR]
        dq, dk, dv = [], [], []
        for half, mask in enumerate(ones):
            probs = probs_ref[2 * pair + half, 0:end, row0:end]
            wide = probs.astype(F32)
            d_probs = dot(vals, d_pair * mask, NT)
            mean = jnp.sum(wide * d_probs, axis=0, keepdims=True)
            d_scores = (wide * (d_probs - mean) * head**-0.5).astype(BF)
            dq.append(dot(d_scores, keys, TN))
            dk.append(dot(d_scores, queries))
            dv.append(dot(probs, d_pair))
        d_queries.append(jnp.where(first_half((rows, PAIR)), dq[0], dq[1]))
        d_keys.append(jnp.where(first_half((end, PAIR)), dk[0], dk[1]))
        d_vals.append(jnp.where(first_half((end, PAIR)), dv[0], dv[1]))
    d_keys = jnp.concatenate(d_keys, axis=1)
    d_vals = jnp.concatenate(d_vals, axis=1)
    if later is not None:
        d_keys = d_keys + later[0:end, 0:width]
        d_vals = d_vals + later[0:end, width : 2 * width]
    d_packed = jnp.concatenate([*d_queries, d_keys[row0:end], d_vals[row0:end]], axis=1).astype(BF)
    d_normed = dot(d_packed, qkv_w[...], NT) + dot(d_up, up_w[...], NT)
    scale = norm_scale(u)
    unit = u * scale
    d_state = scale * (d_normed - unit * jnp.mean(unit * d_normed, axis=-1, keepdims=True))
    earlier = None
    if row0 > 0:
        earlier = jnp.concatenate([d_keys[0:row0], d_vals[0:row0]], axis=1)
    return d_state, earlier, (d_packed, d_up, low)


def layers_of(refs):
    return [ref.at[0] for ref in refs], [ref.at[1] for ref in refs]


def whole(refs):
    return jnp.concatenate([ref[...] for ref in refs], axis=0)


def split(value, refs):
    rows = refs[0].shape[0]
    for c, ref in enumerate(refs):
        ref[...] = value[c * rows : (c + 1) * rows]


def relax_kernel(length, starts, *refs):
    even, odd = layers_of(refs[0:4])
    state = starts[...]
    state = state + STEP * forward_rows(state, even, length[0], 0)[0]
    refs[4][...] = state + STEP * forward_rows(state, odd, length[0], 0)[0]


def fine_kernel(length, first, starts, received, *refs):
    even, odd = layers_of(refs[0:4])
    outs = [refs[4 + i * CHUNKS : 4 + (i + 1) * CHUNKS] for i in range(4)]
    state = jnp.where(first[0] == 1, starts[...], received[...])
    value = forward_rows(state, even, length[0], 0)[0]
    middle = state + STEP * value
    end = middle + STEP * forward_rows(middle, odd, length[0], 0)[0]
    for array, out in zip((state, middle, end, end - (state + 2.0 * STEP * value)), outs):
        split(array, out)


def coarse_kernel(chunk, length, state, defect, *refs):
    weights, refs = layers_of(refs[0:4])[0], refs[4:]
    old_keys = old_vals = None
    if chunk > 0:
        old = refs[0][...]
        refs = refs[1:]
        width = state.shape[1]
        old_keys, old_vals = old[:, 0:width], old[:, width : 2 * width]
    corrected, middles, ends = refs[0:3]
    current = state[...]
    rows = current.shape[0]
    value, keys, vals = forward_rows(
        current, weights, length[0], chunk * rows, old_keys, old_vals
    )
    corrected[...] = current
    middles[...] = current + STEP * value
    ends[...] = current + 2.0 * STEP * value + defect[...]
    if len(refs) > 3:
        both = jnp.concatenate([keys, vals], axis=1)
        refs[3][...] = both if chunk == 0 else jnp.concatenate([old, both], axis=0)


def turn_kernel(length, *refs):
    corrected, middles, ends = (
        whole(refs[i * CHUNKS : (i + 1) * CHUNKS]) for i in range(3)
    )
    target, refs = refs[3 * CHUNKS], refs[3 * CHUNKS + 1 :]
    even, odd = layers_of(refs[0:4])
    even_saved, odd_saved = refs[4:7], refs[7:10]
    guess_ref, out, corrected_ref, middles_ref, ends_ref = refs[10:]
    corrected_ref[...] = corrected
    middles_ref[...] = middles
    ends_ref[...] = ends
    position = lax.broadcasted_iota(jnp.int32, ends.shape, 0)
    guess = jnp.where(position < length[0], ends - target[...], 0.0)
    guess_ref[...] = guess
    linearize_rows(middles, odd, length[0], *odd_saved)
    linearize_rows(corrected, even, length[0], *even_saved)
    state = guess + STEP * backward_rows(guess, middles, odd, *odd_saved, 0)[0]
    out[...] = state + STEP * backward_rows(state, corrected, even, *even_saved, 0)[0]


def back_kernel(last, guess, received, corrected, middles, *refs):
    even, odd = layers_of(refs[0:4])
    even_saved, odd_saved, outs = refs[4:7], refs[7:10], refs[10:]
    state = jnp.where(last[0] == 1, guess[...], received[...])
    split(state, outs[0:CHUNKS])
    state = state + STEP * backward_rows(state, middles[...], odd, *odd_saved, 0)[0]
    state = state + STEP * backward_rows(state, corrected[...], even, *even_saved, 0)[0]
    split(state, outs[CHUNKS : 2 * CHUNKS])


def adjoint_kernel(chunk, incoming, relaxed, fine, corrected, *refs):
    weights, saved, refs = layers_of(refs[0:4])[0], refs[4:7], refs[7:]
    later = None
    if chunk < CHUNKS - 1:
        later = refs[0][...]
        refs = refs[1:]
    rows = incoming.shape[0]
    current = incoming[...]
    gap = current - relaxed[...]
    state = corrected[chunk * rows : (chunk + 1) * rows, :]
    change, earlier, _ = backward_rows(gap, state, weights, *saved, chunk * rows, later)
    refs[0][...] = current
    refs[1][...] = fine[...] + (gap + 2.0 * STEP * change)
    if chunk > 0:
        refs[2][...] = earlier


def pick(order, blocks, held):
    place = order[pl.program_id(0)]
    for i, group in enumerate(blocks):

        @pl.when(place == i)
        def _(group=group):
            split_rows = 0
            for ref in group:
                held[split_rows : split_rows + ref.shape[0], :] = ref[...]
                split_rows += ref.shape[0]


def all_linear_kernel(count, order, lengths, *refs):
    held = refs[-1]
    pick(order, [refs[i : i + 1] for i in range(count)], held)
    refs = refs[count:-1]
    even, odd = layers_of(refs[0:4])
    corrected, middles = refs[4:6]
    even_saved, odd_saved = refs[6:9], refs[9:12]
    even_factors, odd_factors = refs[12:15], refs[15:18]
    length = lengths[order[pl.program_id(0)]]
    state = held[...]
    corrected[...] = state
    linearize_rows(state, even, length, *even_saved, even_factors)
    value = dot(even_factors[1][...], even[1][...]) + dot(even_factors[2][...], even[3][...])
    middle = state + STEP * value
    middles[...] = middle
    linearize_rows(middle, odd, length, *odd_saved, odd_factors)


def all_back_kernel(count, order, *refs):
    held = refs[-1]
    pick(order, [refs[i * CHUNKS : (i + 1) * CHUNKS] for i in range(count)], held)
    refs = refs[count * CHUNKS : -1]
    even, odd = layers_of(refs[0:4])
    corrected, middles, even_saved, odd_saved = refs[4], refs[5], refs[6:9], refs[9:12]
    outs = refs[12:]
    state = held[...]
    change, _, right = backward_rows(state, middles[...], odd, *odd_saved, 0)
    for ref, value in zip(outs[3:6], right):
        ref[...] = value
    state = state + STEP * change
    _, _, right = backward_rows(state, corrected[...], even, *even_saved, 0)
    for ref, value in zip(outs[0:3], right):
        ref[...] = value


def nothing_kernel(*refs):
    del refs


def in_vmem(arrays):
    return [pltpu.with_memory_space_constraint(array, pltpu.VMEM) for array in arrays]


def call(kernel, outs, smem, weights, before, after=()):
    args = (*before, *in_vmem(weights), *after)
    specs = [pl.BlockSpec(memory_space=pltpu.SMEM)] * len(smem)
    specs += [pl.BlockSpec(memory_space=pltpu.VMEM)] * len(args)
    return pl.pallas_call(
        kernel,
        out_shape=tuple(jax.ShapeDtypeStruct(shape, kind) for shape, kind in outs),
        in_specs=specs,
        out_specs=tuple(pl.BlockSpec(memory_space=pltpu.VMEM) for _ in outs),
        compiler_params=pltpu.CompilerParams(vmem_limit_bytes=SMALL_LIMIT),
    )(*smem, *args)


def call_each(kernel, outs, order, smem, gathered, weights, moving=()):
    def block(shape):
        rest = (0,) * (len(shape) - 1)
        return pl.BlockSpec((None, *shape[1:]), lambda i, order: (i, *rest))

    rows, width = moving[0].shape[1:] if moving else gathered[0].shape
    return pl.pallas_call(
        kernel,
        grid_spec=pltpu.PrefetchScalarGridSpec(
            num_scalar_prefetch=1,
            grid=order.shape,
            in_specs=[pl.BlockSpec(memory_space=pltpu.SMEM)] * len(smem)
            + [pl.BlockSpec(memory_space=pltpu.VMEM)] * (len(gathered) + len(weights))
            + [block(x.shape) for x in moving],
            out_specs=tuple(block(shape) for shape, _ in outs),
            scratch_shapes=[pltpu.VMEM((rows, width), F32)],
        ),
        out_shape=tuple(jax.ShapeDtypeStruct(shape, kind) for shape, kind in outs),
        compiler_params=pltpu.CompilerParams(vmem_limit_bytes=LARGE_LIMIT),
    )(order, *smem, *gathered, *in_vmem(weights), *moving)


def unwritten(outs):
    return pl.pallas_call(
        nothing_kernel,
        out_shape=tuple(jax.ShapeDtypeStruct(shape, kind) for shape, kind in outs),
        out_specs=tuple(pl.BlockSpec(memory_space=pl.ANY) for _ in outs),
    )()


def gather_dp(block):
    count = lax.axis_size("dp")
    return [block] + [
        lax.ppermute(block, "dp", [(i, (i + turn) % count) for i in range(count)])
        for turn in range(1, count)
    ]


def gathered_order():
    count = lax.axis_size("dp")
    others = jnp.arange(count, dtype=jnp.int32)
    return ((lax.axis_index("dp") - others) % count).astype(jnp.int32)


def on_device(states, target, lengths, qkv_weight, out_weight, up_weight, down_weight):
    layer_count = lax.axis_size("layer")
    device = lax.axis_index("layer")
    weights = (qkv_weight, out_weight, up_weight, down_weight)
    starts, goal = states[0, 0], target[0]
    rows, width = starts.shape
    hidden = up_weight.shape[2]
    part = rows // CHUNKS
    full = ((rows, width), F32)
    piece = ((part, width), F32)
    saved = (((rows, 3 * width), BF), ((HEADS, rows, rows), BF), ((rows, hidden), BF))
    sizes = jnp.concatenate(gather_dp(lengths))
    order = gathered_order()
    count = order.shape[0]
    is_first = (device == 0).astype(jnp.int32).reshape(1)
    is_last = (device == layer_count - 1).astype(jnp.int32).reshape(1)

    (first_end,) = call(relax_kernel, (full,), (lengths,), weights, (starts,))
    received = lax.ppermute(
        first_end, "layer", [(i, i + 1) for i in range(layer_count - 1)]
    )
    got = call(
        fine_kernel, (piece,) * (4 * CHUNKS), (lengths, is_first), weights, (starts, received)
    )
    corrected, middles, ends, defect = (
        list(got[i * CHUNKS : (i + 1) * CHUNKS]) for i in range(4)
    )
    stores = [jnp.zeros((c * part, 2 * width), BF) for c in range(1, CHUNKS)]
    for block in range(2, layer_count):
        incoming = [lax.ppermute(ends[c], "layer", [(block - 1, block)]) for c in range(CHUNKS)]
        for c in range(CHUNKS):
            outs = (piece, piece, piece)
            kept = (corrected[c], middles[c], ends[c])
            if c < CHUNKS - 1:
                outs += (((((c + 1) * part), 2 * width), BF),)
                kept += (stores[c],)
            old = () if c == 0 else (stores[c - 1],)
            got = lax.cond(
                device == block,
                functools.partial(
                    call, functools.partial(coarse_kernel, c), outs, (lengths,), weights,
                    (incoming[c], defect[c]), old,
                ),
                lambda kept=kept: kept,
            )
            corrected[c], middles[c], ends[c] = got[0:3]
            if c < CHUNKS - 1:
                stores[c] = got[3]
    *kept, guess, turned, corrected, middles, ends = call(
        turn_kernel, (*saved, *saved, full, full, full, full, full), (lengths,), weights,
        (*corrected, *middles, *ends, goal),
    )
    even_saved = kept[0:3]
    received = lax.ppermute(
        turned, "layer", [(i + 1, i) for i in range(layer_count - 1)]
    )
    stack = lambda shapes: tuple(((count, *shape), kind) for shape, kind in shapes)
    factors = (((rows, width), BF), ((rows, width), BF), ((rows, hidden), BF))
    linear_outs = stack((full, full, *saved, *saved, *factors, *factors))
    every = gather_dp(corrected)

    def all_linear():
        return tuple(
            call_each(
                functools.partial(all_linear_kernel, count), linear_outs, order, (sizes,), every,
                weights,
            )
        )

    linear = lax.cond(device < layer_count - 2, all_linear, lambda: tuple(unwritten(linear_outs)))
    received, linear = lax.optimization_barrier((received, linear))
    got = call(
        back_kernel, (piece,) * (2 * CHUNKS), (is_last,), weights,
        (guess, received, corrected, middles), kept,
    )
    relaxed, fine = got[0:CHUNKS], got[CHUNKS:]
    adjoint_ends, adjoint_out = list(relaxed), list(fine)
    carried = [jnp.zeros((c * part, 2 * width), F32) for c in range(1, CHUNKS)]
    for block in range(layer_count - 3, -1, -1):
        incoming = [
            lax.ppermute(adjoint_out[c], "layer", [(block + 1, block)])
            for c in range(CHUNKS - 1, -1, -1)
        ][::-1]
        for c in range(CHUNKS - 1, -1, -1):
            outs = (piece, piece)
            old = (adjoint_ends[c], adjoint_out[c])
            if c > 0:
                outs += (((c * part, 2 * width), F32),)
                old += (carried[c - 1],)
            later = () if c == CHUNKS - 1 else (carried[c],)
            got = lax.cond(
                device == block,
                functools.partial(
                    call, functools.partial(adjoint_kernel, c), outs, (), weights,
                    (incoming[c], relaxed[c], fine[c], corrected), (*even_saved, *later),
                ),
                lambda old=old: old,
            )
            adjoint_ends[c], adjoint_out[c] = got[0:2]
            if c > 0:
                carried[c - 1] = got[2]
    linear, adjoint_out = lax.optimization_barrier((linear, adjoint_out))
    linear = lax.cond(device < layer_count - 2, lambda: linear, all_linear)
    gathered = [gather_dp(adjoint_ends[c]) for c in range(CHUNKS - 1, -1, -1)][::-1]
    every_adjoint = [gathered[c][i] for i in range(count) for c in range(CHUNKS)]
    lefts = (linear[8:11], linear[11:14])
    rights = (((rows, 3 * width), BF), ((rows, hidden), BF), ((rows, width), BF))
    got = call_each(
        functools.partial(all_back_kernel, count), stack((*rights, *rights)), order, (),
        every_adjoint, weights, linear[0:8],
    )
    totals = [[], [], [], []]
    for left, right in zip(lefts, (got[0:3], got[3:6])):
        normed, context, gated = (x.reshape(count * rows, -1) for x in left)
        d_packed, d_up, d_out = (x.reshape(count * rows, -1) for x in right)
        for total, pair in zip(
            totals, ((normed, d_packed), (context, d_out), (normed, d_up), (gated, d_out))
        ):
            total.append(STEP * dot(*pair, TN))
    totals = tuple(jnp.stack(total) for total in totals)
    weight_count = float(sum((math.prod(weight.shape[1:]) for weight in weights)))
    square = sum((jnp.sum(total * total, axis=(1, 2)) for total in totals))
    scale = jnp.sqrt(square / weight_count + 1e-06)[:, None, None]
    results = tuple((total / scale for total in totals))
    adjoint_out = jnp.concatenate(adjoint_out, axis=0)
    return (ends[None, None], adjoint_out[None, None], *results)


def solution(mesh):
    in_specs = (
        P("layer", "dp", None, None),
        P("dp", None, None),
        P("dp"),
        P("layer", None, None),
        P("layer", None, None),
        P("layer", None, None),
        P("layer", None, None),
    )
    out_specs = (
        P("layer", "dp", None, None),
        P("layer", "dp", None, None),
        P("layer", None, None),
        P("layer", None, None),
        P("layer", None, None),
        P("layer", None, None),
    )
    return jax.shard_map(
        on_device, mesh=mesh, in_specs=in_specs, out_specs=out_specs, check_vma=False
    )
```

```python
import functools
import math
import types

import jax
import jax.numpy as jnp
from jax import lax
from jax.experimental import pallas as pl
from jax.experimental.pallas import tpu as pltpu
from jax.sharding import PartitionSpec as P

HEADS = 8
STEP = 0.125
CHUNKS = 2
PAIR = 128
TILE = 512
VMEM_LIMIT = 48 * 1024 * 1024

BF = jnp.bfloat16
F32 = jnp.float32
NN = ((1,), (0,))
NT = ((1,), (1,))
TN = ((0,), (0,))
GELU_A = math.sqrt(2.0 / math.pi)
GELU_B = 0.044715


def dot(a, b, dims=NN):
    return lax.dot_general(a, b, (dims, ((), ())), preferred_element_type=F32)


def norm_scale(u):
    return lax.rsqrt(jnp.mean(u * u, axis=-1, keepdims=True) + 1e-06)


def half_masks(value):
    lane = lax.broadcasted_iota(jnp.int32, (1, PAIR), 1)
    first = jnp.where(lane < PAIR // 2, value, 0.0).astype(BF)
    second = jnp.where(lane < PAIR // 2, 0.0, value).astype(BF)
    return (first, second)


def join(pair):
    lane = lax.broadcasted_iota(jnp.int32, pair[0].shape, 1)
    return jnp.where(lane < PAIR // 2, pair[0], pair[1])


def gelu_parts(x):
    inner = jnp.tanh(GELU_A * (x + GELU_B * (x * x * x)))
    return 0.5 * (1.0 + inner), inner


def at(i, size, base=0):
    return pl.ds(pl.multiple_of(base + i * size, size if base % size == 0 else PAIR), size)


def loop(count, body):
    lax.fori_loop(0, count, lambda i, carry: (body(i), carry)[1], 0)


class Layer:
    def __init__(self, index, sources, targets, sems, when=None):
        self.targets, self.when = targets, when
        self.copies = [
            pltpu.make_async_copy(source.at[index], target, sems.at[i])
            for i, (source, target) in enumerate(zip(sources, targets))
        ]
        self.waiting = [True] * len(targets)

    def do(self, action):
        if self.when is None:
            action()
        else:
            pl.when(self.when)(action)

    def start(self, order):
        for i in order:
            self.do(self.copies[i].start)

    def get(self, i):
        if self.waiting[i]:
            self.do(self.copies[i].wait)
            self.waiting[i] = False
        return self.targets[i]


QKV, OUT, UP, DOWN = range(4)
FORWARD = (QKV, UP, OUT, DOWN)
BACKWARD = (OUT, DOWN, QKV, UP)


def project(u, layer, work):
    width = u.shape[1]
    work.normed[...] = (u * norm_scale(u)).astype(BF)
    qkv_w = layer.get(QKV)

    def step(i):
        work.packed[:, at(i, TILE)] = dot(work.normed[...], qkv_w[:, at(i, TILE)]).astype(BF)

    loop(3 * width // TILE, step)


def forward_rows(u, layer, length, row0, work, old=None):
    rows, width = u.shape
    head = width // HEADS
    project(u, layer, work)
    shape = (rows, row0 + rows)
    key_pos = lax.broadcasted_iota(jnp.int32, shape, 1)
    query_pos = lax.broadcasted_iota(jnp.int32, shape, 0) + row0
    seen = (key_pos <= query_pos) & (key_pos < length)
    masks = half_masks(head**-0.5)

    def attend(pair):
        queries = work.packed[:, at(pair, PAIR)]
        keys = work.packed[:, at(pair, PAIR, width)]
        vals = work.packed[:, at(pair, PAIR, 2 * width)]
        if old is not None:
            keys = jnp.concatenate([old[:, at(pair, PAIR)], keys], axis=0)
            vals = jnp.concatenate([old[:, at(pair, PAIR, width)], vals], axis=0)
        outs = []
        for mask in masks:
            scores = dot(queries * mask, keys, NT)
            scores = jnp.where(seen, scores, -jnp.inf)
            weight = jnp.exp(scores - jnp.max(scores, axis=-1, keepdims=True))
            probs = (weight * (1.0 / jnp.sum(weight, axis=-1, keepdims=True))).astype(BF)
            outs.append(dot(probs, vals))
        work.context[:, at(pair, PAIR)] = join(outs).astype(BF)

    loop(width // PAIR, attend)
    up_w = layer.get(UP)

    def expand(i):
        up = dot(work.normed[...], up_w[:, at(i, TILE)])
        work.hidden[:, at(i, TILE)] = (up * gelu_parts(up)[0]).astype(BF)

    loop(work.hidden.shape[1] // TILE, expand)
    return contract(layer, work, work.context, work.hidden)


def contract(layer, work, context, hidden):
    out_w, down_w = layer.get(OUT), layer.get(DOWN)
    tile = TILE // 2

    def step(i):
        cols = at(i, tile)
        work.value[:, cols] = dot(context[...], out_w[:, cols]) + dot(hidden[...], down_w[:, cols])

    loop(work.value.shape[1] // tile, step)
    return work.value[...]


def linearize_rows(u, layer, length, saved, work, factors=None):
    packed_ref, probs_ref, slope_ref = saved
    rows, width = u.shape
    head = width // HEADS
    project(u, layer, work)
    packed_ref[...] = work.packed[...]
    key_pos = lax.broadcasted_iota(jnp.int32, (rows, rows), 0)
    query_pos = lax.broadcasted_iota(jnp.int32, (rows, rows), 1)
    seen = (key_pos <= query_pos) & (key_pos < length)
    masks = half_masks(head**-0.5)

    def attend(pair):
        queries = work.packed[:, at(pair, PAIR)]
        keys = work.packed[:, at(pair, PAIR, width)]
        vals = work.packed[:, at(pair, PAIR, 2 * width)]
        outs = []
        for half, mask in enumerate(masks):
            scores = dot(keys, queries * mask, NT)
            scores = jnp.where(seen, scores, -jnp.inf)
            weight = jnp.exp(scores - jnp.max(scores, axis=0, keepdims=True))
            probs = (weight * (1.0 / jnp.sum(weight, axis=0, keepdims=True))).astype(BF)
            probs_ref[2 * pair + half] = probs
            if factors is not None:
                outs.append(dot(probs, vals, TN))
        if factors is not None:
            factors[1][:, at(pair, PAIR)] = join(outs).astype(BF)

    loop(width // PAIR, attend)
    up_w = layer.get(UP)

    def expand(i):
        cols = at(i, TILE)
        up = dot(work.normed[...], up_w[:, cols])
        gate, inner = gelu_parts(up)
        rise = GELU_A + 3.0 * GELU_A * GELU_B * up * up
        slope_ref[:, cols] = (gate + 0.5 * up * (1.0 - inner * inner) * rise).astype(BF)
        if factors is not None:
            factors[2][:, cols] = (up * gate).astype(BF)

    loop(slope_ref.shape[1] // TILE, expand)
    if factors is not None:
        factors[0][...] = work.normed[...]


def backward_rows(ct, u, layer, saved, work, row0, later=None, earlier=None, right=None):
    packed_ref, probs_ref, slope_ref = saved
    rows, width = ct.shape
    head = width // HEADS
    end = row0 + rows
    d_packed, d_up, low = right if right is not None else (work.d_packed, work.d_up, work.low)
    low[...] = ct.astype(BF)
    out_w = layer.get(OUT)
    half_tile = TILE // 2

    def back_context(i):
        cols = at(i, half_tile)
        work.d_context[:, cols] = dot(low[...], out_w[cols, :], NT).astype(BF)

    loop(width // half_tile, back_context)
    ones = half_masks(1.0)

    def attend(pair):
        cols = at(pair, PAIR)
        queries = packed_ref[row0:end, cols]
        keys = packed_ref[0:end, at(pair, PAIR, width)]
        vals = packed_ref[0:end, at(pair, PAIR, 2 * width)]
        d_pair = work.d_context[:, cols]
        dq, dk, dv = [], [], []
        for half, mask in enumerate(ones):
            probs = probs_ref[2 * pair + half, 0:end, row0:end]
            wide = probs.astype(F32)
            d_probs = dot(vals, d_pair * mask, NT)
            mean = jnp.sum(wide * d_probs, axis=0, keepdims=True)
            d_scores = (wide * (d_probs - mean) * head**-0.5).astype(BF)
            dq.append(dot(d_scores, keys, TN))
            dk.append(dot(d_scores, queries))
            dv.append(dot(probs, d_pair))
        d_packed[:, cols] = join(dq).astype(BF)
        for place, value in ((width, join(dk)), (2 * width, join(dv))):
            if later is not None:
                value = value + later[0:end, at(pair, PAIR, place - width)]
            d_packed[:, at(pair, PAIR, place)] = value[row0:end].astype(BF)
            if earlier is not None:
                earlier[:, at(pair, PAIR, place - width)] = value[0:row0]

    loop(width // PAIR, attend)
    down_w = layer.get(DOWN)

    def back_hidden(i):
        cols = at(i, TILE)
        d_hidden = dot(low[...], down_w[cols, :], NT)
        d_up[:, cols] = (d_hidden * slope_ref[row0:end, cols].astype(F32)).astype(BF)

    loop(slope_ref.shape[1] // TILE, back_hidden)
    qkv_w, up_w = layer.get(QKV), layer.get(UP)

    def back_normed(i):
        cols = at(i, half_tile)
        work.value[:, cols] = dot(d_packed[...], qkv_w[cols, :], NT) + dot(d_up[...], up_w[cols, :], NT)

    loop(width // half_tile, back_normed)
    d_normed = work.value[...]
    scale = norm_scale(u)
    unit = u * scale
    return scale * (d_normed - unit * jnp.mean(unit * d_normed, axis=-1, keepdims=True))


def whole(refs):
    return jnp.concatenate([ref[...] for ref in refs], axis=0)


def split(value, refs):
    rows = refs[0].shape[0]
    for c, ref in enumerate(refs):
        ref[...] = value[c * rows : (c + 1) * rows]


def relax_kernel(smem, ins, outs, work, layers):
    even, odd = layers
    even.start(FORWARD)
    odd.start(FORWARD)
    length = smem[0][0]
    state = ins[0][...]
    state = state + STEP * forward_rows(state, even, length, 0, work)
    outs[0][...] = state + STEP * forward_rows(state, odd, length, 0, work)


def fine_kernel(smem, ins, outs, work, layers):
    even, odd = layers
    even.start(FORWARD)
    odd.start(FORWARD)
    length = smem[0][0]
    state = jnp.where(smem[1][0] == 1, ins[0][...], ins[1][...])
    value = forward_rows(state, even, length, 0, work)
    middle = state + STEP * value
    split(state, outs[0:CHUNKS])
    split(middle, outs[CHUNKS : 2 * CHUNKS])
    coarse = state + 2.0 * STEP * value
    end = middle + STEP * forward_rows(middle, odd, length, 0, work)
    split(end, outs[2 * CHUNKS : 3 * CHUNKS])
    split(end - coarse, outs[3 * CHUNKS : 4 * CHUNKS])


def coarse_kernel(chunk, smem, ins, outs, work, layers):
    (even,) = layers
    even.start(FORWARD)
    state, defect = ins[0:2]
    old = ins[2] if chunk > 0 else None
    current = state[...]
    rows, width = current.shape
    value = forward_rows(current, even, smem[0][0], chunk * rows, work, old)
    outs[0][...] = current
    outs[1][...] = current + STEP * value
    outs[2][...] = current + 2.0 * STEP * value + defect[...]
    if len(outs) > 3:
        if chunk > 0:
            outs[3][0 : chunk * rows, :] = old[...]
        outs[3][chunk * rows :, :] = work.packed[:, width:]


def turn_kernel(smem, ins, outs, work, layers):
    even, odd = layers
    odd.start(FORWARD)
    even.start(FORWARD)
    length = smem[0][0]
    corrected, middles, ends = (whole(ins[i * CHUNKS : (i + 1) * CHUNKS]) for i in range(3))
    target = ins[3 * CHUNKS]
    even_saved, odd_saved = outs[0:3], outs[3:6]
    guess_ref, out, corrected_ref, middles_ref, ends_ref = outs[6:]
    corrected_ref[...] = corrected
    middles_ref[...] = middles
    ends_ref[...] = ends
    position = lax.broadcasted_iota(jnp.int32, ends.shape, 0)
    guess_ref[...] = jnp.where(position < length, ends - target[...], 0.0)
    linearize_rows(middles_ref[...], odd, length, odd_saved, work)
    linearize_rows(corrected_ref[...], even, length, even_saved, work)
    state = guess_ref[...]
    state = state + STEP * backward_rows(state, middles_ref[...], odd, odd_saved, work, 0)
    out[...] = state + STEP * backward_rows(state, corrected_ref[...], even, even_saved, work, 0)


def back_kernel(smem, ins, outs, work, layers):
    even, odd = layers
    odd.start(BACKWARD)
    even.start(BACKWARD)
    guess, received, corrected, middles = ins[0:4]
    even_saved, odd_saved = ins[4:7], ins[7:10]
    state = jnp.where(smem[0][0] == 1, guess[...], received[...])
    split(state, outs[0:CHUNKS])
    state = state + STEP * backward_rows(state, middles[...], odd, odd_saved, work, 0)
    state = state + STEP * backward_rows(state, corrected[...], even, even_saved, work, 0)
    split(state, outs[CHUNKS : 2 * CHUNKS])


def adjoint_kernel(chunk, smem, ins, outs, work, layers):
    (even,) = layers
    even.start(BACKWARD)
    incoming, relaxed, fine, corrected = ins[0:4]
    saved = ins[4:7]
    later = ins[7] if chunk < CHUNKS - 1 else None
    rows = incoming.shape[0]
    current = incoming[...]
    gap = current - relaxed[...]
    state = corrected[chunk * rows : (chunk + 1) * rows, :]
    change = backward_rows(
        gap, state, even, saved, work, chunk * rows, later, outs[2] if chunk > 0 else None
    )
    outs[0][...] = current
    outs[1][...] = fine[...] + (gap + 2.0 * STEP * change)


def pick(order, blocks, held):
    place = order[pl.program_id(0)]
    for i, group in enumerate(blocks):

        @pl.when(place == i)
        def _(group=group):
            first = 0
            for ref in group:
                held[first : first + ref.shape[0], :] = ref[...]
                first += ref.shape[0]


def all_linear_kernel(order, smem, ins, moving, outs, work, layers, held):
    del moving
    pick(order, [ins[i : i + CHUNKS] for i in range(0, len(ins), CHUNKS)], held)
    even, odd = layers
    even.start(FORWARD)
    odd.start((QKV, UP))
    corrected, middles = outs[0:2]
    even_saved, odd_saved = outs[2:5], outs[5:8]
    even_factors, odd_factors = outs[8:11], outs[11:14]
    length = smem[0][order[pl.program_id(0)]]
    corrected[...] = held[...]
    linearize_rows(held[...], even, length, even_saved, work, even_factors)
    middles[...] = held[...] + STEP * contract(even, work, even_factors[1], even_factors[2])
    linearize_rows(middles[...], odd, length, odd_saved, work, odd_factors)


def all_back_kernel(order, smem, ins, moving, outs, work, layers, held):
    del smem
    pick(order, [ins[i : i + CHUNKS] for i in range(0, len(ins), CHUNKS)], held)
    even, odd = layers
    odd.start(BACKWARD)
    even.start(BACKWARD)
    corrected, middles, even_saved, odd_saved = moving[0], moving[1], moving[2:5], moving[5:8]
    state = held[...]
    change = backward_rows(state, middles[...], odd, odd_saved, work, 0, right=outs[3:6])
    held[...] = state + STEP * change
    backward_rows(held[...], corrected[...], even, even_saved, work, 0, right=outs[0:3])


def nothing_kernel(*refs):
    del refs


WORK = ("normed", "packed", "context", "hidden", "value", "low", "d_context", "d_packed", "d_up")


def scratch(rows, weights, layers):
    _, width, hidden = weights[UP].shape
    shapes = [
        pltpu.VMEM((rows, columns), F32 if name == "value" else BF)
        for name, columns in zip(
            WORK, (width, 3 * width, width, hidden, width, width, width, 3 * width, hidden)
        )
    ]
    shapes += [pltpu.VMEM(w.shape[1:], w.dtype) for _ in layers for w in weights]
    return shapes + [pltpu.SemaphoreType.DMA((len(layers), len(weights)))]


def unpack(refs, sources, layers, when=None):
    work = types.SimpleNamespace(**dict(zip(WORK, refs)))
    count = len(sources)
    refs, sems = refs[len(WORK) : -1], refs[-1]
    found = [
        Layer(index, sources, refs[i * count : (i + 1) * count], sems.at[i], when)
        for i, index in enumerate(layers)
    ]
    return work, found


def cost(rows, weights, layers):
    flops = 2 * rows * sum(math.prod(w.shape[1:]) for w in weights) * layers
    return pl.CostEstimate(flops=6 * flops, bytes_accessed=0, transcendentals=0)


def call(kernel, outs, smem, weights, layers, ins, rows, passes=1):
    counts = [len(smem), len(ins), len(weights), len(outs)]

    def body(*refs):
        cuts = [sum(counts[:i]) for i in range(5)]
        parts = [refs[cuts[i] : cuts[i + 1]] for i in range(4)]
        kernel(parts[0], parts[1], parts[3], *unpack(refs[cuts[4] :], parts[2], layers))

    return pl.pallas_call(
        body,
        out_shape=tuple(jax.ShapeDtypeStruct(shape, kind) for shape, kind in outs),
        in_specs=[pl.BlockSpec(memory_space=pltpu.SMEM)] * len(smem)
        + [pl.BlockSpec(memory_space=pltpu.VMEM)] * len(ins)
        + [pl.BlockSpec(memory_space=pl.ANY)] * len(weights),
        out_specs=tuple(pl.BlockSpec(memory_space=pltpu.VMEM) for _ in outs),
        scratch_shapes=scratch(rows, weights, layers),
        cost_estimate=cost(rows, weights, passes),
        compiler_params=pltpu.CompilerParams(vmem_limit_bytes=VMEM_LIMIT),
    )(*smem, *ins, *weights)


def call_each(kernel, outs, order, smem, gathered, weights, moving=()):
    rows, width = outs[0][0][1], weights[OUT].shape[1]
    counts = [len(smem), len(gathered), len(weights), len(moving), len(outs)]

    def block(shape):
        rest = (0,) * (len(shape) - 1)
        return pl.BlockSpec((None, *shape[1:]), lambda i, order: (i, *rest))

    def body(order_ref, *refs):
        cuts = [sum(counts[:i]) for i in range(6)]
        parts = [refs[cuts[i] : cuts[i + 1]] for i in range(5)]
        work, layers = unpack(refs[cuts[5] : -1], parts[2], (0, 1), pl.program_id(0) == 0)
        kernel(order_ref, parts[0], parts[1], parts[3], parts[4], work, layers, refs[-1])

    return pl.pallas_call(
        body,
        grid_spec=pltpu.PrefetchScalarGridSpec(
            num_scalar_prefetch=1,
            grid=order.shape,
            in_specs=[pl.BlockSpec(memory_space=pltpu.SMEM)] * len(smem)
            + [pl.BlockSpec(memory_space=pltpu.VMEM)] * len(gathered)
            + [pl.BlockSpec(memory_space=pl.ANY)] * len(weights)
            + [block(x.shape) for x in moving],
            out_specs=tuple(block(shape) for shape, _ in outs),
            scratch_shapes=scratch(rows, weights, (0, 1)) + [pltpu.VMEM((rows, width), F32)],
        ),
        out_shape=tuple(jax.ShapeDtypeStruct(shape, kind) for shape, kind in outs),
        cost_estimate=cost(rows, weights, 4 * order.shape[0]),
        compiler_params=pltpu.CompilerParams(vmem_limit_bytes=VMEM_LIMIT),
    )(order, *smem, *gathered, *weights, *moving)


def unwritten(outs):
    return pl.pallas_call(
        nothing_kernel,
        out_shape=tuple(jax.ShapeDtypeStruct(shape, kind) for shape, kind in outs),
        out_specs=tuple(pl.BlockSpec(memory_space=pl.ANY) for _ in outs),
    )()


def gather_dp(block, then=None):
    count = lax.axis_size("dp")
    if count == 1:
        return [block]
    swap = [(i, i ^ 1) for i in range(count)]
    mine = [block]
    for turn in range(1, count // 2):
        route = [(i, (i + 2 * turn) % count) for i in range(count)]
        mine.append(lax.ppermute(block, "dp", route))
    theirs = [lax.ppermute(block, "dp", swap)]
    if then is not None:
        mine, _ = lax.optimization_barrier((mine, then))
    theirs += [lax.ppermute(own, "dp", swap) for own in mine[1:]]
    return [x for pair in zip(mine, theirs) for x in pair]


def gathered_order():
    count = lax.axis_size("dp")
    place = lax.axis_index("dp")
    other = jnp.arange(count, dtype=jnp.int32)
    turn = (place // 2 - other // 2) % max(count // 2, 1)
    return (2 * turn + (place + other) % 2).astype(jnp.int32) if count > 1 else other


def on_device(states, target, lengths, qkv_weight, out_weight, up_weight, down_weight):
    layer_count = lax.axis_size("layer")
    device = lax.axis_index("layer")
    weights = (qkv_weight, out_weight, up_weight, down_weight)
    starts, goal = states[0, 0], target[0]
    rows, width = starts.shape
    hidden = up_weight.shape[2]
    part = rows // CHUNKS
    full = ((rows, width), F32)
    piece = ((part, width), F32)
    saved = (((rows, 3 * width), BF), ((HEADS, rows, rows), BF), ((rows, hidden), BF))
    sizes = jnp.concatenate(gather_dp(lengths))
    both, first_layer = (0, 1), (0,)
    order = gathered_order()
    count = order.shape[0]
    is_first = (device == 0).astype(jnp.int32).reshape(1)
    is_last = (device == layer_count - 1).astype(jnp.int32).reshape(1)

    (first_end,) = call(relax_kernel, (full,), (lengths,), weights, both, (starts,), rows, 2)
    received = lax.ppermute(
        first_end, "layer", [(i, i + 1) for i in range(layer_count - 1)]
    )
    received, sizes = lax.optimization_barrier((received, sizes))
    got = call(
        fine_kernel, (piece,) * (4 * CHUNKS), (lengths, is_first), weights, both,
        (starts, received), rows, 2,
    )
    corrected, middles, ends, defect = (
        list(got[i * CHUNKS : (i + 1) * CHUNKS]) for i in range(4)
    )
    stores = [jnp.zeros((c * part, 2 * width), BF) for c in range(1, CHUNKS)]
    for block in range(2, layer_count):
        incoming = [lax.ppermute(ends[c], "layer", [(block - 1, block)]) for c in range(CHUNKS)]
        for c in range(CHUNKS):
            outs = (piece, piece, piece)
            kept = (corrected[c], middles[c], ends[c])
            if c < CHUNKS - 1:
                outs += (((((c + 1) * part), 2 * width), BF),)
                kept += (stores[c],)
            old = () if c == 0 else (stores[c - 1],)
            got = lax.cond(
                device == block,
                functools.partial(
                    call, functools.partial(coarse_kernel, c), outs, (lengths,), weights,
                    first_layer, (incoming[c], defect[c], *old), part,
                ),
                lambda kept=kept: kept,
            )
            corrected[c], middles[c], ends[c] = got[0:3]
            if c < CHUNKS - 1:
                stores[c] = got[3]
    chunks = corrected
    *kept, guess, turned, corrected, middles, ends = call(
        turn_kernel, (*saved, *saved, full, full, full, full, full), (lengths,), weights, both,
        (*corrected, *middles, *ends, goal), rows, 6,
    )
    even_saved = kept[0:3]
    received = lax.ppermute(
        turned, "layer", [(i + 1, i) for i in range(layer_count - 1)]
    )
    stack = lambda shapes: tuple(((count, *shape), kind) for shape, kind in shapes)
    factors = (((rows, width), BF), ((rows, width), BF), ((rows, hidden), BF))
    linear_outs = stack((full, full, *saved, *saved, *factors, *factors))
    gathered = [gather_dp(chunk, turned) for chunk in chunks]
    every = [gathered[c][i] for i in range(count) for c in range(CHUNKS)]

    def all_linear():
        return tuple(
            call_each(
                all_linear_kernel, linear_outs, order, (sizes,), every, weights
            )
        )

    linear = lax.cond(device < layer_count - 2, all_linear, lambda: tuple(unwritten(linear_outs)))
    received, linear = lax.optimization_barrier((received, linear))
    got = call(
        back_kernel, (piece,) * (2 * CHUNKS), (is_last,), weights, both,
        (guess, received, corrected, middles, *kept), rows, 4,
    )
    relaxed, fine = got[0:CHUNKS], got[CHUNKS:]
    adjoint_ends, adjoint_out = list(relaxed), list(fine)
    carried = [jnp.zeros((c * part, 2 * width), F32) for c in range(1, CHUNKS)]
    for block in range(layer_count - 3, -1, -1):
        incoming = [
            lax.ppermute(adjoint_out[c], "layer", [(block + 1, block)])
            for c in range(CHUNKS - 1, -1, -1)
        ][::-1]
        for c in range(CHUNKS - 1, -1, -1):
            outs = (piece, piece)
            old = (adjoint_ends[c], adjoint_out[c])
            if c > 0:
                outs += (((c * part, 2 * width), F32),)
                old += (carried[c - 1],)
            later = () if c == CHUNKS - 1 else (carried[c],)
            got = lax.cond(
                device == block,
                functools.partial(
                    call, functools.partial(adjoint_kernel, c), outs, (), weights,
                    first_layer, (incoming[c], relaxed[c], fine[c], corrected, *even_saved, *later),
                    part, 2,
                ),
                lambda old=old: old,
            )
            adjoint_ends[c], adjoint_out[c] = got[0:2]
            if c > 0:
                carried[c - 1] = got[2]
    linear, adjoint_out = lax.optimization_barrier((linear, adjoint_out))
    linear = lax.cond(device < layer_count - 2, lambda: linear, all_linear)
    gathered = [gather_dp(adjoint_ends[c]) for c in range(CHUNKS - 1, -1, -1)][::-1]
    every_adjoint = [gathered[c][i] for i in range(count) for c in range(CHUNKS)]
    lefts = (linear[8:11], linear[11:14])
    rights = (((rows, 3 * width), BF), ((rows, hidden), BF), ((rows, width), BF))
    got = call_each(
        all_back_kernel, stack((*rights, *rights)), order, (), every_adjoint, weights,
        linear[0:8],
    )
    totals = [[], [], [], []]
    for left, right in zip(lefts, (got[0:3], got[3:6])):
        normed, context, gated = (x.reshape(count * rows, -1) for x in left)
        d_packed, d_up, d_out = (x.reshape(count * rows, -1) for x in right)
        for total, pair in zip(
            totals, ((normed, d_packed), (context, d_out), (normed, d_up), (gated, d_out))
        ):
            total.append(STEP * dot(*pair, TN))
    totals = tuple(jnp.stack(total) for total in totals)
    weight_count = float(sum((math.prod(weight.shape[1:]) for weight in weights)))
    square = sum((jnp.sum(total * total, axis=(1, 2)) for total in totals))
    scale = jnp.sqrt(square / weight_count + 1e-06)[:, None, None]
    results = tuple((total / scale for total in totals))
    adjoint_out = jnp.concatenate(adjoint_out, axis=0)
    return (ends[None, None], adjoint_out[None, None], *results)


def solution(mesh):
    in_specs = (
        P("layer", "dp", None, None),
        P("dp", None, None),
        P("dp"),
        P("layer", None, None),
        P("layer", None, None),
        P("layer", None, None),
        P("layer", None, None),
    )
    out_specs = (
        P("layer", "dp", None, None),
        P("layer", "dp", None, None),
        P("layer", None, None),
        P("layer", None, None),
        P("layer", None, None),
        P("layer", None, None),
    )
    return jax.shard_map(
        on_device, mesh=mesh, in_specs=in_specs, out_specs=out_specs, check_vma=False
    )
```

```python
import functools
import math
import types

import jax
import jax.numpy as jnp
from jax import lax
from jax.experimental import pallas as pl
from jax.experimental.pallas import tpu as pltpu
from jax.sharding import PartitionSpec as P

HEADS = 8
STEP = 0.125
CHUNKS = 2
PAIR = 128
TILE = 512

BF = jnp.bfloat16
F32 = jnp.float32
NN = ((1,), (0,))
NT = ((1,), (1,))
TN = ((0,), (0,))
GELU_A = math.sqrt(2.0 / math.pi)
GELU_B = 0.044715


def dot(a, b, dims=NN):
    return lax.dot_general(a, b, (dims, ((), ())), preferred_element_type=F32)


def norm_scale(u):
    return lax.rsqrt(jnp.mean(u * u, axis=-1, keepdims=True) + 1e-06)


def half_masks(value):
    lane = lax.broadcasted_iota(jnp.int32, (1, PAIR), 1)
    first = jnp.where(lane < PAIR // 2, value, 0.0).astype(BF)
    second = jnp.where(lane < PAIR // 2, 0.0, value).astype(BF)
    return (first, second)


def join(pair):
    lane = lax.broadcasted_iota(jnp.int32, pair[0].shape, 1)
    return jnp.where(lane < PAIR // 2, pair[0], pair[1])


def gelu_parts(x):
    inner = jnp.tanh(GELU_A * (x + GELU_B * (x * x * x)))
    return 0.5 * (1.0 + inner), inner


def at(i, size, base=0):
    return slice(base + i * size, base + (i + 1) * size)


def loop(count, body):
    for i in range(count):
        body(i)


class Layer:
    def __init__(self, index, sources, targets, sems, when=None):
        self.targets, self.when = targets, when
        self.copies = [
            pltpu.make_async_copy(source.at[index], target, sems.at[i])
            for i, (source, target) in enumerate(zip(sources, targets))
        ]
        self.waiting = [True] * len(targets)

    def do(self, action):
        if self.when is None:
            action()
        else:
            pl.when(self.when)(action)

    def start(self, order):
        for i in order:
            self.do(self.copies[i].start)

    def get(self, i):
        if self.waiting[i]:
            self.do(self.copies[i].wait)
            self.waiting[i] = False
        return self.targets[i]


QKV, OUT, UP, DOWN = range(4)
FORWARD = (QKV, UP, OUT, DOWN)
BACKWARD = (OUT, DOWN, QKV, UP)


def project(u, layer, work):
    width = u.shape[1]
    work.normed[...] = (u * norm_scale(u)).astype(BF)
    qkv_w = layer.get(QKV)

    def step(i):
        work.packed[:, at(i, TILE)] = dot(work.normed[...], qkv_w[:, at(i, TILE)]).astype(BF)

    loop(3 * width // TILE, step)


def forward_rows(u, layer, length, row0, work, old=None):
    rows, width = u.shape
    head = width // HEADS
    project(u, layer, work)
    shape = (rows, row0 + rows)
    key_pos = lax.broadcasted_iota(jnp.int32, shape, 1)
    query_pos = lax.broadcasted_iota(jnp.int32, shape, 0) + row0
    seen = (key_pos <= query_pos) & (key_pos < length)
    masks = half_masks(head**-0.5)

    def attend(pair):
        queries = work.packed[:, at(pair, PAIR)]
        keys = work.packed[:, at(pair, PAIR, width)]
        vals = work.packed[:, at(pair, PAIR, 2 * width)]
        if old is not None:
            keys = jnp.concatenate([old[:, at(pair, PAIR)], keys], axis=0)
            vals = jnp.concatenate([old[:, at(pair, PAIR, width)], vals], axis=0)
        outs = []
        for mask in masks:
            scores = dot(queries * mask, keys, NT)
            scores = jnp.where(seen, scores, -jnp.inf)
            weight = jnp.exp(scores - jnp.max(scores, axis=-1, keepdims=True))
            probs = (weight * (1.0 / jnp.sum(weight, axis=-1, keepdims=True))).astype(BF)
            outs.append(dot(probs, vals))
        work.context[:, at(pair, PAIR)] = join(outs).astype(BF)

    loop(width // PAIR, attend)
    up_w = layer.get(UP)

    def expand(i):
        up = dot(work.normed[...], up_w[:, at(i, TILE)])
        work.hidden[:, at(i, TILE)] = (up * gelu_parts(up)[0]).astype(BF)

    loop(work.hidden.shape[1] // TILE, expand)
    return contract(layer, work, work.context, work.hidden)


def contract(layer, work, context, hidden):
    out_w, down_w = layer.get(OUT), layer.get(DOWN)
    tile = TILE // 2

    def step(i):
        cols = at(i, tile)
        work.value[:, cols] = dot(context[...], out_w[:, cols]) + dot(hidden[...], down_w[:, cols])

    loop(work.value.shape[1] // tile, step)
    return work.value[...]


def linearize_rows(u, layer, length, saved, work, factors=None):
    packed_ref, probs_ref, slope_ref = saved
    rows, width = u.shape
    head = width // HEADS
    project(u, layer, work)
    packed_ref[...] = work.packed[...]
    key_pos = lax.broadcasted_iota(jnp.int32, (rows, rows), 0)
    query_pos = lax.broadcasted_iota(jnp.int32, (rows, rows), 1)
    seen = (key_pos <= query_pos) & (key_pos < length)
    masks = half_masks(head**-0.5)

    def attend(pair):
        queries = work.packed[:, at(pair, PAIR)]
        keys = work.packed[:, at(pair, PAIR, width)]
        vals = work.packed[:, at(pair, PAIR, 2 * width)]
        outs = []
        for half, mask in enumerate(masks):
            scores = dot(keys, queries * mask, NT)
            scores = jnp.where(seen, scores, -jnp.inf)
            weight = jnp.exp(scores - jnp.max(scores, axis=0, keepdims=True))
            probs = (weight * (1.0 / jnp.sum(weight, axis=0, keepdims=True))).astype(BF)
            probs_ref[2 * pair + half] = probs
            if factors is not None:
                outs.append(dot(probs, vals, TN))
        if factors is not None:
            factors[1][:, at(pair, PAIR)] = join(outs).astype(BF)

    loop(width // PAIR, attend)
    up_w = layer.get(UP)

    def expand(i):
        cols = at(i, TILE)
        up = dot(work.normed[...], up_w[:, cols])
        gate, inner = gelu_parts(up)
        rise = GELU_A + 3.0 * GELU_A * GELU_B * up * up
        slope_ref[:, cols] = (gate + 0.5 * up * (1.0 - inner * inner) * rise).astype(BF)
        if factors is not None:
            factors[2][:, cols] = (up * gate).astype(BF)

    loop(slope_ref.shape[1] // TILE, expand)
    if factors is not None:
        factors[0][...] = work.normed[...]


def backward_rows(ct, u, layer, saved, work, row0, later=None, earlier=None, right=None):
    packed_ref, probs_ref, slope_ref = saved
    rows, width = ct.shape
    head = width // HEADS
    end = row0 + rows
    d_packed, d_up, low = right if right is not None else (work.d_packed, work.d_up, work.low)
    low[...] = ct.astype(BF)
    out_w = layer.get(OUT)
    half_tile = TILE // 2

    def back_context(i):
        cols = at(i, half_tile)
        work.d_context[:, cols] = dot(low[...], out_w[cols, :], NT).astype(BF)

    loop(width // half_tile, back_context)
    ones = half_masks(1.0)

    def attend(pair):
        cols = at(pair, PAIR)
        queries = packed_ref[row0:end, cols]
        keys = packed_ref[0:end, at(pair, PAIR, width)]
        vals = packed_ref[0:end, at(pair, PAIR, 2 * width)]
        d_pair = work.d_context[:, cols]
        dq, dk, dv = [], [], []
        for half, mask in enumerate(ones):
            probs = probs_ref[2 * pair + half, 0:end, row0:end]
            wide = probs.astype(F32)
            d_probs = dot(vals, d_pair * mask, NT)
            mean = jnp.sum(wide * d_probs, axis=0, keepdims=True)
            d_scores = (wide * (d_probs - mean) * head**-0.5).astype(BF)
            dq.append(dot(d_scores, keys, TN))
            dk.append(dot(d_scores, queries))
            dv.append(dot(probs, d_pair))
        d_packed[:, cols] = join(dq).astype(BF)
        for place, value in ((width, join(dk)), (2 * width, join(dv))):
            if later is not None:
                value = value + later[0:end, at(pair, PAIR, place - width)]
            d_packed[:, at(pair, PAIR, place)] = value[row0:end].astype(BF)
            if earlier is not None:
                earlier[:, at(pair, PAIR, place - width)] = value[0:row0]

    loop(width // PAIR, attend)
    down_w = layer.get(DOWN)

    def back_hidden(i):
        cols = at(i, TILE)
        d_hidden = dot(low[...], down_w[cols, :], NT)
        d_up[:, cols] = (d_hidden * slope_ref[row0:end, cols].astype(F32)).astype(BF)

    loop(slope_ref.shape[1] // TILE, back_hidden)
    qkv_w, up_w = layer.get(QKV), layer.get(UP)

    def back_normed(i):
        cols = at(i, half_tile)
        work.value[:, cols] = dot(d_packed[...], qkv_w[cols, :], NT) + dot(d_up[...], up_w[cols, :], NT)

    loop(width // half_tile, back_normed)
    d_normed = work.value[...]
    scale = norm_scale(u)
    unit = u * scale
    return scale * (d_normed - unit * jnp.mean(unit * d_normed, axis=-1, keepdims=True))


def whole(refs):
    return jnp.concatenate([ref[...] for ref in refs], axis=0)


def split(value, refs):
    rows = refs[0].shape[0]
    for c, ref in enumerate(refs):
        ref[...] = value[c * rows : (c + 1) * rows]


def relax_kernel(smem, ins, outs, work, layers):
    even, odd = layers
    even.start(FORWARD)
    odd.start(FORWARD)
    length = smem[0][0]
    state = ins[0][...]
    state = state + STEP * forward_rows(state, even, length, 0, work)
    outs[0][...] = state + STEP * forward_rows(state, odd, length, 0, work)


def fine_kernel(smem, ins, outs, work, layers):
    even, odd = layers
    even.start(FORWARD)
    odd.start(FORWARD)
    length = smem[0][0]
    state = jnp.where(smem[1][0] == 1, ins[0][...], ins[1][...])
    value = forward_rows(state, even, length, 0, work)
    middle = state + STEP * value
    split(state, outs[0:CHUNKS])
    split(middle, outs[CHUNKS : 2 * CHUNKS])
    coarse = state + 2.0 * STEP * value
    end = middle + STEP * forward_rows(middle, odd, length, 0, work)
    split(end, outs[2 * CHUNKS : 3 * CHUNKS])
    split(end - coarse, outs[3 * CHUNKS : 4 * CHUNKS])


def coarse_kernel(chunk, smem, ins, outs, work, layers):
    (even,) = layers
    even.start(FORWARD)
    state, defect = ins[0:2]
    old = ins[2] if chunk > 0 else None
    current = state[...]
    rows, width = current.shape
    value = forward_rows(current, even, smem[0][0], chunk * rows, work, old)
    outs[0][...] = current
    outs[1][...] = current + STEP * value
    outs[2][...] = current + 2.0 * STEP * value + defect[...]
    if len(outs) > 3:
        if chunk > 0:
            outs[3][0 : chunk * rows, :] = old[...]
        outs[3][chunk * rows :, :] = work.packed[:, width:]


def turn_kernel(smem, ins, outs, work, layers):
    even, odd = layers
    odd.start(FORWARD)
    even.start(FORWARD)
    length = smem[0][0]
    corrected, middles, ends = (whole(ins[i * CHUNKS : (i + 1) * CHUNKS]) for i in range(3))
    target = ins[3 * CHUNKS]
    even_saved, odd_saved = outs[0:3], outs[3:6]
    guess_ref, out, corrected_ref, middles_ref, ends_ref = outs[6:]
    corrected_ref[...] = corrected
    middles_ref[...] = middles
    ends_ref[...] = ends
    position = lax.broadcasted_iota(jnp.int32, ends.shape, 0)
    guess_ref[...] = jnp.where(position < length, ends - target[...], 0.0)
    linearize_rows(middles_ref[...], odd, length, odd_saved, work)
    linearize_rows(corrected_ref[...], even, length, even_saved, work)
    state = guess_ref[...]
    state = state + STEP * backward_rows(state, middles_ref[...], odd, odd_saved, work, 0)
    out[...] = state + STEP * backward_rows(state, corrected_ref[...], even, even_saved, work, 0)


def back_kernel(smem, ins, outs, work, layers):
    even, odd = layers
    odd.start(BACKWARD)
    even.start(BACKWARD)
    guess, received, corrected, middles = ins[0:4]
    even_saved, odd_saved = ins[4:7], ins[7:10]
    state = jnp.where(smem[0][0] == 1, guess[...], received[...])
    split(state, outs[0:CHUNKS])
    state = state + STEP * backward_rows(state, middles[...], odd, odd_saved, work, 0)
    state = state + STEP * backward_rows(state, corrected[...], even, even_saved, work, 0)
    split(state, outs[CHUNKS : 2 * CHUNKS])


def adjoint_kernel(chunk, smem, ins, outs, work, layers):
    (even,) = layers
    even.start(BACKWARD)
    incoming, relaxed, fine, corrected = ins[0:4]
    saved = ins[4:7]
    later = ins[7] if chunk < CHUNKS - 1 else None
    rows = incoming.shape[0]
    current = incoming[...]
    gap = current - relaxed[...]
    state = corrected[chunk * rows : (chunk + 1) * rows, :]
    change = backward_rows(
        gap, state, even, saved, work, chunk * rows, later, outs[2] if chunk > 0 else None
    )
    outs[0][...] = current
    outs[1][...] = fine[...] + (gap + 2.0 * STEP * change)


def pick(order, blocks, held):
    place = order[pl.program_id(0)]
    for i, group in enumerate(blocks):

        @pl.when(place == i)
        def _(group=group):
            first = 0
            for ref in group:
                held[first : first + ref.shape[0], :] = ref[...]
                first += ref.shape[0]


def all_linear_kernel(order, smem, ins, moving, outs, work, layers, held):
    del moving
    pick(order, [ins[i : i + CHUNKS] for i in range(0, len(ins), CHUNKS)], held)
    even, odd = layers
    even.start(FORWARD)
    odd.start((QKV, UP))
    corrected, middles = outs[0:2]
    even_saved, odd_saved = outs[2:5], outs[5:8]
    even_factors, odd_factors = outs[8:11], outs[11:14]
    length = smem[0][order[pl.program_id(0)]]
    corrected[...] = held[...]
    linearize_rows(held[...], even, length, even_saved, work, even_factors)
    middles[...] = held[...] + STEP * contract(even, work, even_factors[1], even_factors[2])
    linearize_rows(middles[...], odd, length, odd_saved, work, odd_factors)


def all_back_kernel(order, smem, ins, moving, outs, work, layers, held):
    del smem
    pick(order, [ins[i : i + CHUNKS] for i in range(0, len(ins), CHUNKS)], held)
    even, odd = layers
    odd.start(BACKWARD)
    even.start(BACKWARD)
    corrected, middles, even_saved, odd_saved = moving[0], moving[1], moving[2:5], moving[5:8]
    state = held[...]
    change = backward_rows(state, middles[...], odd, odd_saved, work, 0, right=outs[3:6])
    held[...] = state + STEP * change
    backward_rows(held[...], corrected[...], even, even_saved, work, 0, right=outs[0:3])


def nothing_kernel(*refs):
    del refs


WORK = ("normed", "packed", "context", "hidden", "value", "low", "d_context", "d_packed", "d_up")


def scratch(rows, weights, layers):
    _, width, hidden = weights[UP].shape
    shapes = [
        pltpu.VMEM((rows, columns), F32 if name == "value" else BF)
        for name, columns in zip(
            WORK, (width, 3 * width, width, hidden, width, width, width, 3 * width, hidden)
        )
    ]
    shapes += [pltpu.VMEM(w.shape[1:], w.dtype) for _ in layers for w in weights]
    return shapes + [pltpu.SemaphoreType.DMA((len(layers), len(weights)))]


def room(shapes, scratches):
    total = sum(math.prod(shape) * jnp.dtype(kind).itemsize for shape, kind in shapes)
    for item in scratches[:-1]:
        total += math.prod(item.shape) * jnp.dtype(item.dtype).itemsize
    return pltpu.CompilerParams(vmem_limit_bytes=int(total * 1.25) + 6 * 1024 * 1024)


def unpack(refs, sources, layers, when=None):
    work = types.SimpleNamespace(**dict(zip(WORK, refs)))
    count = len(sources)
    refs, sems = refs[len(WORK) : -1], refs[-1]
    found = [
        Layer(index, sources, refs[i * count : (i + 1) * count], sems.at[i], when)
        for i, index in enumerate(layers)
    ]
    return work, found


def cost(rows, weights, layers):
    flops = 2 * rows * sum(math.prod(w.shape[1:]) for w in weights) * layers
    return pl.CostEstimate(flops=6 * flops, bytes_accessed=0, transcendentals=0)


def call(kernel, outs, smem, weights, layers, ins, rows, passes=1):
    counts = [len(smem), len(ins), len(weights), len(outs)]
    held = scratch(rows, weights, layers)

    def body(*refs):
        cuts = [sum(counts[:i]) for i in range(5)]
        parts = [refs[cuts[i] : cuts[i + 1]] for i in range(4)]
        kernel(parts[0], parts[1], parts[3], *unpack(refs[cuts[4] :], parts[2], layers))

    return pl.pallas_call(
        body,
        out_shape=tuple(jax.ShapeDtypeStruct(shape, kind) for shape, kind in outs),
        in_specs=[pl.BlockSpec(memory_space=pltpu.SMEM)] * len(smem)
        + [pl.BlockSpec(memory_space=pltpu.VMEM)] * len(ins)
        + [pl.BlockSpec(memory_space=pl.ANY)] * len(weights),
        out_specs=tuple(pl.BlockSpec(memory_space=pltpu.VMEM) for _ in outs),
        scratch_shapes=held,
        cost_estimate=cost(rows, weights, passes),
        compiler_params=room([*((x.shape, x.dtype) for x in ins), *outs], held),
    )(*smem, *ins, *weights)


def call_each(kernel, outs, order, smem, gathered, weights, moving=()):
    rows, width = outs[0][0][1], weights[OUT].shape[1]
    held = scratch(rows, weights, (0, 1))
    counts = [len(smem), len(gathered), len(weights), len(moving), len(outs)]

    def block(shape):
        rest = (0,) * (len(shape) - 1)
        return pl.BlockSpec((None, *shape[1:]), lambda i, order: (i, *rest))

    def body(order_ref, *refs):
        cuts = [sum(counts[:i]) for i in range(6)]
        parts = [refs[cuts[i] : cuts[i + 1]] for i in range(5)]
        work, layers = unpack(refs[cuts[5] : -1], parts[2], (0, 1), pl.program_id(0) == 0)
        kernel(order_ref, parts[0], parts[1], parts[3], parts[4], work, layers, refs[-1])

    return pl.pallas_call(
        body,
        grid_spec=pltpu.PrefetchScalarGridSpec(
            num_scalar_prefetch=1,
            grid=order.shape,
            in_specs=[pl.BlockSpec(memory_space=pltpu.SMEM)] * len(smem)
            + [pl.BlockSpec(memory_space=pltpu.VMEM)] * len(gathered)
            + [pl.BlockSpec(memory_space=pl.ANY)] * len(weights)
            + [block(x.shape) for x in moving],
            out_specs=tuple(block(shape) for shape, _ in outs),
            scratch_shapes=held + [pltpu.VMEM((rows, width), F32)],
        ),
        out_shape=tuple(jax.ShapeDtypeStruct(shape, kind) for shape, kind in outs),
        cost_estimate=cost(rows, weights, 4 * order.shape[0]),
        compiler_params=room(
            [(x.shape, x.dtype) for x in gathered]
            + 2 * [(x.shape[1:], x.dtype) for x in moving]
            + 2 * [(shape[1:], kind) for shape, kind in outs],
            held,
        ),
    )(order, *smem, *gathered, *weights, *moving)


def unwritten(outs):
    return pl.pallas_call(
        nothing_kernel,
        out_shape=tuple(jax.ShapeDtypeStruct(shape, kind) for shape, kind in outs),
        out_specs=tuple(pl.BlockSpec(memory_space=pl.ANY) for _ in outs),
    )()


def gather_dp(block, then=None):
    count = lax.axis_size("dp")
    if count == 1:
        return [block]
    swap = [(i, i ^ 1) for i in range(count)]
    mine = [block]
    for turn in range(1, count // 2):
        route = [(i, (i + 2 * turn) % count) for i in range(count)]
        mine.append(lax.ppermute(block, "dp", route))
    theirs = [lax.ppermute(block, "dp", swap)]
    if then is not None:
        mine, _ = lax.optimization_barrier((mine, then))
    theirs += [lax.ppermute(own, "dp", swap) for own in mine[1:]]
    return [x for pair in zip(mine, theirs) for x in pair]


def gathered_order():
    count = lax.axis_size("dp")
    place = lax.axis_index("dp")
    other = jnp.arange(count, dtype=jnp.int32)
    turn = (place // 2 - other // 2) % max(count // 2, 1)
    return (2 * turn + (place + other) % 2).astype(jnp.int32) if count > 1 else other


def on_device(states, target, lengths, qkv_weight, out_weight, up_weight, down_weight):
    layer_count = lax.axis_size("layer")
    device = lax.axis_index("layer")
    weights = (qkv_weight, out_weight, up_weight, down_weight)
    starts, goal = states[0, 0], target[0]
    rows, width = starts.shape
    hidden = up_weight.shape[2]
    part = rows // CHUNKS
    full = ((rows, width), F32)
    piece = ((part, width), F32)
    saved = (((rows, 3 * width), BF), ((HEADS, rows, rows), BF), ((rows, hidden), BF))
    sizes = jnp.concatenate(gather_dp(lengths))
    both, first_layer = (0, 1), (0,)
    order = gathered_order()
    count = order.shape[0]
    is_first = (device == 0).astype(jnp.int32).reshape(1)
    is_last = (device == layer_count - 1).astype(jnp.int32).reshape(1)

    (first_end,) = call(relax_kernel, (full,), (lengths,), weights, both, (starts,), rows, 2)
    received = lax.ppermute(
        first_end, "layer", [(i, i + 1) for i in range(layer_count - 1)]
    )
    received, sizes = lax.optimization_barrier((received, sizes))
    got = call(
        fine_kernel, (piece,) * (4 * CHUNKS), (lengths, is_first), weights, both,
        (starts, received), rows, 2,
    )
    corrected, middles, ends, defect = (
        list(got[i * CHUNKS : (i + 1) * CHUNKS]) for i in range(4)
    )
    stores = [jnp.zeros((c * part, 2 * width), BF) for c in range(1, CHUNKS)]
    for block in range(2, layer_count):
        incoming = [lax.ppermute(ends[c], "layer", [(block - 1, block)]) for c in range(CHUNKS)]
        for c in range(CHUNKS):
            outs = (piece, piece, piece)
            kept = (corrected[c], middles[c], ends[c])
            if c < CHUNKS - 1:
                outs += (((((c + 1) * part), 2 * width), BF),)
                kept += (stores[c],)
            old = () if c == 0 else (stores[c - 1],)
            got = lax.cond(
                device == block,
                functools.partial(
                    call, functools.partial(coarse_kernel, c), outs, (lengths,), weights,
                    first_layer, (incoming[c], defect[c], *old), part,
                ),
                lambda kept=kept: kept,
            )
            corrected[c], middles[c], ends[c] = got[0:3]
            if c < CHUNKS - 1:
                stores[c] = got[3]
    chunks = corrected
    *kept, guess, turned, corrected, middles, ends = call(
        turn_kernel, (*saved, *saved, full, full, full, full, full), (lengths,), weights, both,
        (*corrected, *middles, *ends, goal), rows, 6,
    )
    even_saved = kept[0:3]
    received = lax.ppermute(
        turned, "layer", [(i + 1, i) for i in range(layer_count - 1)]
    )
    stack = lambda shapes: tuple(((count, *shape), kind) for shape, kind in shapes)
    factors = (((rows, width), BF), ((rows, width), BF), ((rows, hidden), BF))
    linear_outs = stack((full, full, *saved, *saved, *factors, *factors))
    gathered = [gather_dp(chunk, turned) for chunk in chunks]
    every = [gathered[c][i] for i in range(count) for c in range(CHUNKS)]

    def all_linear():
        return tuple(
            call_each(
                all_linear_kernel, linear_outs, order, (sizes,), every, weights
            )
        )

    linear = lax.cond(device < layer_count - 2, all_linear, lambda: tuple(unwritten(linear_outs)))
    received, linear = lax.optimization_barrier((received, linear))
    got = call(
        back_kernel, (piece,) * (2 * CHUNKS), (is_last,), weights, both,
        (guess, received, corrected, middles, *kept), rows, 4,
    )
    relaxed, fine = got[0:CHUNKS], got[CHUNKS:]
    adjoint_ends, adjoint_out = list(relaxed), list(fine)
    carried = [jnp.zeros((c * part, 2 * width), F32) for c in range(1, CHUNKS)]
    for block in range(layer_count - 3, -1, -1):
        incoming = [
            lax.ppermute(adjoint_out[c], "layer", [(block + 1, block)])
            for c in range(CHUNKS - 1, -1, -1)
        ][::-1]
        for c in range(CHUNKS - 1, -1, -1):
            outs = (piece, piece)
            old = (adjoint_ends[c], adjoint_out[c])
            if c > 0:
                outs += (((c * part, 2 * width), F32),)
                old += (carried[c - 1],)
            later = () if c == CHUNKS - 1 else (carried[c],)
            got = lax.cond(
                device == block,
                functools.partial(
                    call, functools.partial(adjoint_kernel, c), outs, (), weights,
                    first_layer, (incoming[c], relaxed[c], fine[c], corrected, *even_saved, *later),
                    part, 2,
                ),
                lambda old=old: old,
            )
            adjoint_ends[c], adjoint_out[c] = got[0:2]
            if c > 0:
                carried[c - 1] = got[2]
    linear, adjoint_out = lax.optimization_barrier((linear, adjoint_out))
    linear = lax.cond(device < layer_count - 2, lambda: linear, all_linear)
    gathered = [gather_dp(adjoint_ends[c]) for c in range(CHUNKS - 1, -1, -1)][::-1]
    every_adjoint = [gathered[c][i] for i in range(count) for c in range(CHUNKS)]
    lefts = (linear[8:11], linear[11:14])
    rights = (((rows, 3 * width), BF), ((rows, hidden), BF), ((rows, width), BF))
    got = call_each(
        all_back_kernel, stack((*rights, *rights)), order, (), every_adjoint, weights,
        linear[0:8],
    )
    totals = [[], [], [], []]
    for left, right in zip(lefts, (got[0:3], got[3:6])):
        normed, context, gated = (x.reshape(count * rows, -1) for x in left)
        d_packed, d_up, d_out = (x.reshape(count * rows, -1) for x in right)
        for total, pair in zip(
            totals, ((normed, d_packed), (context, d_out), (normed, d_up), (gated, d_out))
        ):
            total.append(STEP * dot(*pair, TN))
    totals = tuple(jnp.stack(total) for total in totals)
    weight_count = float(sum((math.prod(weight.shape[1:]) for weight in weights)))
    square = sum((jnp.sum(total * total, axis=(1, 2)) for total in totals))
    scale = jnp.sqrt(square / weight_count + 1e-06)[:, None, None]
    results = tuple((total / scale for total in totals))
    adjoint_out = jnp.concatenate(adjoint_out, axis=0)
    return (ends[None, None], adjoint_out[None, None], *results)


def solution(mesh):
    in_specs = (
        P("layer", "dp", None, None),
        P("dp", None, None),
        P("dp"),
        P("layer", None, None),
        P("layer", None, None),
        P("layer", None, None),
        P("layer", None, None),
    )
    out_specs = (
        P("layer", "dp", None, None),
        P("layer", "dp", None, None),
        P("layer", None, None),
        P("layer", None, None),
        P("layer", None, None),
        P("layer", None, None),
    )
    return jax.shard_map(
        on_device, mesh=mesh, in_specs=in_specs, out_specs=out_specs, check_vma=False
    )
```

```python
import functools
import math

import jax
import jax.numpy as jnp
from jax import lax
from jax.experimental import pallas as pl
from jax.experimental.pallas import tpu as pltpu
from jax.sharding import PartitionSpec as P

HEADS = 8
STEP = 0.125
CHUNKS = 2
PAIR = 128
TILE = 512

BF = jnp.bfloat16
F32 = jnp.float32
NN = ((1,), (0,))
NT = ((1,), (1,))
TN = ((0,), (0,))
GELU_A = math.sqrt(2.0 / math.pi)
GELU_B = 0.044715


def dot(a, b, dims=NN):
    return lax.dot_general(a, b, (dims, ((), ())), preferred_element_type=F32)


def norm_scale(u):
    return lax.rsqrt(jnp.mean(u * u, axis=-1, keepdims=True) + 1e-06)


def half_masks(value):
    lane = lax.broadcasted_iota(jnp.int32, (1, PAIR), 1)
    first = jnp.where(lane < PAIR // 2, value, 0.0).astype(BF)
    second = jnp.where(lane < PAIR // 2, 0.0, value).astype(BF)
    return (first, second)


def join(pair):
    lane = lax.broadcasted_iota(jnp.int32, pair[0].shape, 1)
    return jnp.where(lane < PAIR // 2, pair[0], pair[1])


def gelu_parts(x):
    inner = jnp.tanh(GELU_A * (x + GELU_B * (x * x * x)))
    return 0.5 * (1.0 + inner), inner


def at(i, size, base=0):
    return slice(base + i * size, base + (i + 1) * size)


def loop(count, body):
    for i in range(count):
        body(i)


class Layer:
    def __init__(self, index, sources, targets, sems, when=None):
        self.targets, self.when = targets, when
        self.copies = [
            pltpu.make_async_copy(source.at[index], target, sems.at[i])
            for i, (source, target) in enumerate(zip(sources, targets))
        ]
        self.waiting = [True] * len(targets)

    def do(self, action):
        if self.when is None:
            action()
        else:
            pl.when(self.when)(action)

    def start(self, order):
        for i in order:
            self.do(self.copies[i].start)

    def get(self, i):
        if self.waiting[i]:
            self.do(self.copies[i].wait)
            self.waiting[i] = False
        return self.targets[i]


QKV, OUT, UP, DOWN = range(4)
FORWARD = (QKV, UP, OUT, DOWN)
BACKWARD = (OUT, DOWN, QKV, UP)


def attention_sides(packed, pair, width):
    cols = pair * PAIR
    return [packed[:, base + cols : base + cols + PAIR] for base in (0, width, 2 * width)]


def forward_rows(u, layer, length, row0=0, old=None, whole_rows=0):
    rows, width = u.shape
    head = width // HEADS
    normed = (u * norm_scale(u)).astype(BF)
    packed = dot(normed, layer.get(QKV)[...]).astype(BF)
    own = packed[:, width:]
    both = own if old is None else jnp.concatenate([old, own], axis=0)
    if whole_rows > both.shape[0]:
        both = jnp.concatenate([both, both[0 : whole_rows - both.shape[0]]], axis=0)
    shape = (rows, both.shape[0])
    key_pos = lax.broadcasted_iota(jnp.int32, shape, 1)
    query_pos = lax.broadcasted_iota(jnp.int32, shape, 0) + row0
    seen = (key_pos <= query_pos) & (key_pos < length)
    masks = half_masks(head**-0.5)
    parts = []
    for pair in range(width // PAIR):
        cols = slice(pair * PAIR, (pair + 1) * PAIR)
        keys, vals = both[:, cols], both[:, width + pair * PAIR : width + (pair + 1) * PAIR]
        outs = []
        for mask in masks:
            scores = dot(packed[:, cols] * mask, keys, NT)
            scores = jnp.where(seen, scores, -jnp.inf)
            weight = jnp.exp(scores - jnp.max(scores, axis=-1, keepdims=True))
            probs = (weight * (1.0 / jnp.sum(weight, axis=-1, keepdims=True))).astype(BF)
            outs.append(dot(probs, vals))
        parts.append(join(outs).astype(BF))
    context = jnp.concatenate(parts, axis=1)
    up = dot(normed, layer.get(UP)[...])
    hidden = (up * gelu_parts(up)[0]).astype(BF)
    return dot(context, layer.get(OUT)[...]) + dot(hidden, layer.get(DOWN)[...]), own


def linearize_rows(u, layer, length, saved, factors=None):
    packed_ref, probs_ref, slope_ref = saved
    rows, width = u.shape
    head = width // HEADS
    wide = u * norm_scale(u)
    normed = wide.astype(BF)
    packed = dot(normed, layer.get(QKV)[...]).astype(BF)
    packed_ref[...] = packed
    key_pos = lax.broadcasted_iota(jnp.int32, (rows, rows), 0)
    query_pos = lax.broadcasted_iota(jnp.int32, (rows, rows), 1)
    seen = (key_pos <= query_pos) & (key_pos < length)
    masks = half_masks(head**-0.5)
    parts = []
    for pair in range(width // PAIR):
        queries, keys, vals = attention_sides(packed, pair, width)
        outs = []
        for half, mask in enumerate(masks):
            scores = dot(keys, queries * mask, NT)
            scores = jnp.where(seen, scores, -jnp.inf)
            weight = jnp.exp(scores - jnp.max(scores, axis=0, keepdims=True))
            probs = (weight * (1.0 / jnp.sum(weight, axis=0, keepdims=True))).astype(BF)
            probs_ref[2 * pair + half] = probs
            if factors is not None:
                outs.append(dot(probs, vals, TN))
        if factors is not None:
            parts.append(join(outs))
    up = dot(normed, layer.get(UP)[...])
    gate, inner = gelu_parts(up)
    rise = GELU_A + 3.0 * GELU_A * GELU_B * up * up
    slope_ref[...] = (gate + 0.5 * up * (1.0 - inner * inner) * rise).astype(BF)
    if factors is None:
        return None
    context, hidden = jnp.concatenate(parts, axis=1), up * gate
    for ref, value in zip(factors, (wide, context, hidden)):
        ref[...] = value.T.astype(BF)
    return context.astype(BF), hidden.astype(BF)


def backward_rows(ct, u, layer, saved, row0=0, later=None, earlier=None, right=None):
    packed_ref, probs_ref, slope_ref = saved
    rows, width = ct.shape
    head = width // HEADS
    end = row0 + rows
    low = ct.astype(BF)
    d_context = dot(low, layer.get(OUT)[...], NT).astype(BF)
    d_hidden = dot(low, layer.get(DOWN)[...], NT)
    d_up = (d_hidden * slope_ref[row0:end, :].astype(F32)).astype(BF)
    ones = half_masks(1.0)
    d_queries, d_sides = [], [[], []]
    for pair in range(width // PAIR):
        lo = pair * PAIR
        queries = packed_ref[row0:end, lo : lo + PAIR]
        keys = packed_ref[:, width + lo : width + lo + PAIR]
        vals = packed_ref[:, 2 * width + lo : 2 * width + lo + PAIR]
        d_pair = d_context[:, lo : lo + PAIR]
        dq, dk, dv = [], [], []
        for half, mask in enumerate(ones):
            probs = probs_ref[2 * pair + half, :, row0:end]
            wide = probs.astype(F32)
            d_probs = dot(vals, d_pair * mask, NT)
            mean = jnp.sum(wide * d_probs, axis=0, keepdims=True)
            d_scores = (wide * (d_probs - mean) * head**-0.5).astype(BF)
            dq.append(dot(d_scores, keys, TN))
            dk.append(dot(d_scores, queries))
            dv.append(dot(probs, d_pair))
        d_queries.append(join(dq).astype(BF))
        for side, value in enumerate((join(dk)[0:end], join(dv)[0:end])):
            base = side * width + lo
            if later is not None:
                value = value + later[0:end, base : base + PAIR]
            d_sides[side].append(value[row0:end].astype(BF))
            if earlier is not None:
                earlier[:, base : base + PAIR] = value[0:row0]
    d_packed = jnp.concatenate([*d_queries, *d_sides[0], *d_sides[1]], axis=1)
    if right is not None:
        for ref, value in zip(right, (d_packed, d_up, low)):
            ref[...] = value
    d_normed = dot(d_packed, layer.get(QKV)[...], NT) + dot(d_up, layer.get(UP)[...], NT)
    scale = norm_scale(u)
    unit = u * scale
    return scale * (d_normed - unit * jnp.mean(unit * d_normed, axis=-1, keepdims=True))


def whole(refs):
    return jnp.concatenate([ref[...] for ref in refs], axis=0)


def split(value, refs):
    rows = refs[0].shape[0]
    for c, ref in enumerate(refs):
        ref[...] = value[c * rows : (c + 1) * rows]


def relax_kernel(smem, ins, outs, layers):
    even, odd = layers
    even.start(FORWARD)
    odd.start(FORWARD)
    length = smem[0][0]
    state = ins[0][...]
    state = state + STEP * forward_rows(state, even, length)[0]
    outs[0][...] = state + STEP * forward_rows(state, odd, length)[0]


def fine_kernel(smem, ins, outs, layers):
    even, odd = layers
    even.start(FORWARD)
    odd.start(FORWARD)
    length = smem[0][0]
    state = jnp.where(smem[1][0] == 1, ins[0][...], ins[1][...])
    value = forward_rows(state, even, length)[0]
    middle = state + STEP * value
    split(state, outs[0:CHUNKS])
    split(middle, outs[CHUNKS : 2 * CHUNKS])
    coarse = state + 2.0 * STEP * value
    end = middle + STEP * forward_rows(middle, odd, length)[0]
    split(end, outs[2 * CHUNKS : 3 * CHUNKS])
    split(end - coarse, outs[3 * CHUNKS : 4 * CHUNKS])


def coarse_kernel(chunk, smem, ins, outs, layers):
    (even,) = layers
    even.start(FORWARD)
    state, defect = ins[0:2]
    old = ins[2][...] if chunk > 0 else None
    current = state[...]
    rows = current.shape[0]
    value, own = forward_rows(
        current, even, smem[0][0], chunk * rows, old, CHUNKS * rows
    )
    outs[0][...] = current
    outs[1][...] = current + STEP * value
    outs[2][...] = current + 2.0 * STEP * value + defect[...]
    if len(outs) > 3:
        if chunk > 0:
            outs[3][0 : chunk * rows, :] = old
        outs[3][chunk * rows :, :] = own


def turn_kernel(smem, ins, outs, layers):
    even, odd = layers
    odd.start(FORWARD)
    even.start(FORWARD)
    length = smem[0][0]
    corrected, middles, ends = (whole(ins[i * CHUNKS : (i + 1) * CHUNKS]) for i in range(3))
    target = ins[3 * CHUNKS]
    even_saved, odd_saved = outs[0:3], outs[3:6]
    guess_ref, out, corrected_ref, middles_ref, ends_ref = outs[6:]
    corrected_ref[...] = corrected
    middles_ref[...] = middles
    ends_ref[...] = ends
    position = lax.broadcasted_iota(jnp.int32, ends.shape, 0)
    guess_ref[...] = jnp.where(position < length, ends - target[...], 0.0)
    linearize_rows(middles, odd, length, odd_saved)
    linearize_rows(corrected, even, length, even_saved)
    state = guess_ref[...]
    state = state + STEP * backward_rows(state, middles, odd, odd_saved)
    out[...] = state + STEP * backward_rows(state, corrected, even, even_saved)


def back_kernel(smem, ins, outs, layers):
    even, odd = layers
    odd.start(BACKWARD)
    even.start(BACKWARD)
    guess, received, corrected, middles = ins[0:4]
    even_saved, odd_saved = ins[4:7], ins[7:10]
    state = jnp.where(smem[0][0] == 1, guess[...], received[...])
    split(state, outs[0:CHUNKS])
    state = state + STEP * backward_rows(state, middles[...], odd, odd_saved)
    state = state + STEP * backward_rows(state, corrected[...], even, even_saved)
    split(state, outs[CHUNKS : 2 * CHUNKS])


def adjoint_kernel(chunk, smem, ins, outs, layers):
    (even,) = layers
    even.start(BACKWARD)
    incoming, relaxed, fine, corrected = ins[0:4]
    saved = ins[4:7]
    later = ins[7] if chunk < CHUNKS - 1 else None
    rows = incoming.shape[0]
    current = incoming[...]
    gap = current - relaxed[...]
    state = corrected[chunk * rows : (chunk + 1) * rows, :]
    change = backward_rows(
        gap, state, even, saved, chunk * rows, later, outs[2] if chunk > 0 else None
    )
    outs[0][...] = current
    outs[1][...] = fine[...] + (gap + 2.0 * STEP * change)


def pick(order, blocks, held):
    place = order[pl.program_id(0)]
    for i, group in enumerate(blocks):

        @pl.when(place == i)
        def _(group=group):
            first = 0
            for ref in group:
                held[first : first + ref.shape[0], :] = ref[...]
                first += ref.shape[0]


def all_linear_kernel(order, smem, ins, moving, outs, layers, held):
    del moving
    pick(order, [ins[i : i + CHUNKS] for i in range(0, len(ins), CHUNKS)], held)
    even, odd = layers
    even.start(FORWARD)
    odd.start((QKV, UP))
    corrected, middles = outs[0:2]
    even_saved, odd_saved = outs[2:5], outs[5:8]
    even_factors, odd_factors = ([ref.at[i] for ref in outs[8:11]] for i in range(2))
    length = smem[0][order[pl.program_id(0)]]
    state = held[...]
    corrected[...] = state
    context, hidden = linearize_rows(state, even, length, even_saved, even_factors)
    value = dot(context, even.get(OUT)[...]) + dot(hidden, even.get(DOWN)[...])
    middle = state + STEP * value
    middles[...] = middle
    linearize_rows(middle, odd, length, odd_saved, odd_factors)


def all_back_kernel(order, smem, ins, moving, outs, layers, held):
    del smem
    pick(order, [ins[i : i + CHUNKS] for i in range(0, len(ins), CHUNKS)], held)
    even, odd = layers
    odd.start(BACKWARD)
    even.start(BACKWARD)
    corrected, middles, even_saved, odd_saved = moving[0], moving[1], moving[2:5], moving[5:8]
    state = held[...]
    even_right, odd_right = ([ref.at[i] for ref in outs] for i in range(2))
    change = backward_rows(state, middles[...], odd, odd_saved, right=odd_right)
    state = state + STEP * change
    backward_rows(state, corrected[...], even, even_saved, right=even_right)


def gradient_kernel(count, *refs):
    (normed, context, hidden), (d_packed, d_up, low) = refs[0:3], refs[3:6]
    outs, sums, sems = refs[6:10], refs[10:14], refs[14]
    layer, k = pl.program_id(0), pl.program_id(1)
    pairs = ((normed, d_packed), (context, low), (normed, d_up), (hidden, low))
    tile = TILE // 2
    total = jnp.zeros((1, tile), F32)
    for (left, right), held in zip(pairs, sums):
        depth = left.shape[1]

        def step(i, total, left=left, right=right, held=held, depth=depth):
            cols = pl.ds(pl.multiple_of(i * tile, tile), tile)
            value = STEP * dot(left[...], right[:, :, cols].reshape(depth, tile))
            value = jnp.where(k == 0, value, held[layer, :, cols] + value)
            held[layer, :, cols] = value
            return total + jnp.sum(value * value, axis=0, keepdims=True)

        total = lax.fori_loop(0, right.shape[2] // tile, step, total)

    def copies(index):
        return [
            pltpu.make_async_copy(held.at[index], out.at[index], sems.at[i])
            for i, (held, out) in enumerate(zip(sums, outs))
        ]

    @pl.when(k == pl.num_programs(1) - 1)
    def _():
        square = jnp.sum(total, axis=1, keepdims=True)
        inverse = 1.0 / jnp.sqrt(square / count + 1e-06)
        for held in sums:
            held[layer] = held[layer] * inverse

        @pl.when(layer == 0)
        def _():
            for copy in copies(0):
                copy.start()

        @pl.when(layer == 1)
        def _():
            for copy in copies(0):
                copy.wait()
            for copy in copies(1):
                copy.start()
            for copy in copies(1):
                copy.wait()


def gradients(lefts, rights, weights):
    _, count, rows, _ = rights[0].shape
    group = min(count, 4)
    sizes = [w.shape[1:] for w in weights]
    blocks = [(2, x.shape[1] * group * rows) for x in lefts]
    blocks += [(2, group * rows * x.shape[3]) for x in rights]
    return pl.pallas_call(
        functools.partial(gradient_kernel, float(sum(math.prod(size) for size in sizes))),
        grid=(2, count // group),
        in_specs=[
            pl.BlockSpec((None, x.shape[1], group * rows), lambda i, k: (i, 0, k)) for x in lefts
        ]
        + [
            pl.BlockSpec((None, group, rows, x.shape[3]), lambda i, k: (i, k, 0, 0))
            for x in rights
        ],
        out_specs=tuple(pl.BlockSpec(memory_space=pl.ANY) for _ in sizes),
        out_shape=tuple(jax.ShapeDtypeStruct((2, *size), F32) for size in sizes),
        scratch_shapes=[pltpu.VMEM((2, *size), F32) for size in sizes]
        + [pltpu.SemaphoreType.DMA((len(sizes),))],
        cost_estimate=pl.CostEstimate(
            flops=4 * count * rows * sum(math.prod(size) for size in sizes),
            bytes_accessed=0,
            transcendentals=0,
        ),
        compiler_params=room(
            [(block, BF) for block in blocks] + [((2, *size), F32) for size in sizes], [None]
        ),
    )(*lefts, *rights)


def nothing_kernel(*refs):
    del refs


def scratch(weights, layers):
    shapes = [pltpu.VMEM(w.shape[1:], w.dtype) for _ in layers for w in weights]
    return shapes + [pltpu.SemaphoreType.DMA((len(layers), len(weights)))]


def room(shapes, scratches):
    total = sum(math.prod(shape) * jnp.dtype(kind).itemsize for shape, kind in shapes)
    for item in scratches[:-1]:
        total += math.prod(item.shape) * jnp.dtype(item.dtype).itemsize
    return pltpu.CompilerParams(vmem_limit_bytes=int(total * 1.1) + 10 * 1024 * 1024)


def unpack(refs, sources, layers, when=None):
    count = len(sources)
    refs, sems = refs[:-1], refs[-1]
    return [
        Layer(index, sources, refs[i * count : (i + 1) * count], sems.at[i], when)
        for i, index in enumerate(layers)
    ]


def cost(rows, weights, layers):
    flops = 2 * rows * sum(math.prod(w.shape[1:]) for w in weights) * layers
    return pl.CostEstimate(flops=6 * flops, bytes_accessed=0, transcendentals=0)


def call(kernel, outs, smem, weights, layers, ins, rows, passes=1):
    counts = [len(smem), len(ins), len(weights), len(outs)]
    held = scratch(weights, layers)

    def body(*refs):
        cuts = [sum(counts[:i]) for i in range(5)]
        parts = [refs[cuts[i] : cuts[i + 1]] for i in range(4)]
        kernel(parts[0], parts[1], parts[3], unpack(refs[cuts[4] :], parts[2], layers))

    return pl.pallas_call(
        body,
        out_shape=tuple(jax.ShapeDtypeStruct(shape, kind) for shape, kind in outs),
        in_specs=[pl.BlockSpec(memory_space=pltpu.SMEM)] * len(smem)
        + [pl.BlockSpec(memory_space=pltpu.VMEM)] * len(ins)
        + [pl.BlockSpec(memory_space=pl.ANY)] * len(weights),
        out_specs=tuple(pl.BlockSpec(memory_space=pltpu.VMEM) for _ in outs),
        scratch_shapes=held,
        cost_estimate=cost(rows, weights, passes),
        compiler_params=room([*((x.shape, x.dtype) for x in ins), *outs], held),
    )(*smem, *ins, *weights)


def call_each(kernel, outs, order, smem, gathered, weights, moving=()):
    rows = sum(x.shape[0] for x in gathered) // order.shape[0]
    width = gathered[0].shape[1]
    specs = [pl.BlockSpec(shape, index) for _, _, shape, index in outs]
    sizes = [[size for size in shape if size] for _, _, shape, _ in outs]
    outs = [(shape, kind) for shape, kind, _, _ in outs]
    held = scratch(weights, (0, 1))
    counts = [len(smem), len(gathered), len(weights), len(moving), len(outs)]

    def block(shape):
        rest = (0,) * (len(shape) - 1)
        return pl.BlockSpec((None, *shape[1:]), lambda i, order: (i, *rest))

    def body(order_ref, *refs):
        cuts = [sum(counts[:i]) for i in range(6)]
        parts = [refs[cuts[i] : cuts[i + 1]] for i in range(5)]
        layers = unpack(refs[cuts[5] : -1], parts[2], (0, 1), pl.program_id(0) == 0)
        kernel(order_ref, parts[0], parts[1], parts[3], parts[4], layers, refs[-1])

    return pl.pallas_call(
        body,
        grid_spec=pltpu.PrefetchScalarGridSpec(
            num_scalar_prefetch=1,
            grid=order.shape,
            in_specs=[pl.BlockSpec(memory_space=pltpu.SMEM)] * len(smem)
            + [pl.BlockSpec(memory_space=pltpu.VMEM)] * len(gathered)
            + [pl.BlockSpec(memory_space=pl.ANY)] * len(weights)
            + [block(x.shape) for x in moving],
            out_specs=tuple(specs),
            scratch_shapes=held + [pltpu.VMEM((rows, width), F32)],
        ),
        out_shape=tuple(jax.ShapeDtypeStruct(shape, kind) for shape, kind in outs),
        cost_estimate=cost(rows, weights, 4 * order.shape[0]),
        compiler_params=room(
            [(x.shape, x.dtype) for x in gathered]
            + 2 * [(x.shape[1:], x.dtype) for x in moving]
            + 2 * [(shape, kind) for shape, (_, kind) in zip(sizes, outs)],
            held,
        ),
    )(order, *smem, *gathered, *weights, *moving)


def unwritten(outs):
    return pl.pallas_call(
        nothing_kernel,
        out_shape=tuple(jax.ShapeDtypeStruct(shape, kind) for shape, kind in outs),
        out_specs=tuple(pl.BlockSpec(memory_space=pl.ANY) for _ in outs),
    )()


def gather_dp(block, then=None):
    count = lax.axis_size("dp")
    if count == 1:
        return [block]
    swap = [(i, i ^ 1) for i in range(count)]
    mine = [block]
    for turn in range(1, count // 2):
        route = [(i, (i + 2 * turn) % count) for i in range(count)]
        mine.append(lax.ppermute(block, "dp", route))
    theirs = [lax.ppermute(block, "dp", swap)]
    if then is not None:
        mine, _ = lax.optimization_barrier((mine, then))
    theirs += [lax.ppermute(own, "dp", swap) for own in mine[1:]]
    return [x for pair in zip(mine, theirs) for x in pair]


def gathered_order():
    count = lax.axis_size("dp")
    place = lax.axis_index("dp")
    other = jnp.arange(count, dtype=jnp.int32)
    turn = (place // 2 - other // 2) % max(count // 2, 1)
    return (2 * turn + (place + other) % 2).astype(jnp.int32) if count > 1 else other


def on_device(states, target, lengths, qkv_weight, out_weight, up_weight, down_weight):
    layer_count = lax.axis_size("layer")
    device = lax.axis_index("layer")
    weights = (qkv_weight, out_weight, up_weight, down_weight)
    starts, goal = states[0, 0], target[0]
    rows, width = starts.shape
    hidden = up_weight.shape[2]
    part = rows // CHUNKS
    full = ((rows, width), F32)
    piece = ((part, width), F32)
    saved = (((rows, 3 * width), BF), ((HEADS, rows, rows), BF), ((rows, hidden), BF))
    sizes = jnp.concatenate(gather_dp(lengths))
    both, first_layer = (0, 1), (0,)
    order = gathered_order()
    count = order.shape[0]
    is_first = (device == 0).astype(jnp.int32).reshape(1)
    is_last = (device == layer_count - 1).astype(jnp.int32).reshape(1)

    (first_end,) = call(relax_kernel, (full,), (lengths,), weights, both, (starts,), rows, 2)
    received = lax.ppermute(
        first_end, "layer", [(i, i + 1) for i in range(layer_count - 1)]
    )
    received, sizes = lax.optimization_barrier((received, sizes))
    got = call(
        fine_kernel, (piece,) * (4 * CHUNKS), (lengths, is_first), weights, both,
        (starts, received), rows, 2,
    )
    corrected, middles, ends, defect = (
        list(got[i * CHUNKS : (i + 1) * CHUNKS]) for i in range(4)
    )
    stores = [jnp.zeros((c * part, 2 * width), BF) for c in range(1, CHUNKS)]
    for block in range(2, layer_count):
        incoming = [lax.ppermute(ends[c], "layer", [(block - 1, block)]) for c in range(CHUNKS)]
        for c in range(CHUNKS):
            outs = (piece, piece, piece)
            kept = (corrected[c], middles[c], ends[c])
            if c < CHUNKS - 1:
                outs += (((((c + 1) * part), 2 * width), BF),)
                kept += (stores[c],)
            old = () if c == 0 else (stores[c - 1],)
            got = lax.cond(
                device == block,
                functools.partial(
                    call, functools.partial(coarse_kernel, c), outs, (lengths,), weights,
                    first_layer, (incoming[c], defect[c], *old), part,
                ),
                lambda kept=kept: kept,
            )
            corrected[c], middles[c], ends[c] = got[0:3]
            if c < CHUNKS - 1:
                stores[c] = got[3]
    chunks = corrected
    *kept, guess, turned, corrected, middles, ends = call(
        turn_kernel, (*saved, *saved, full, full, full, full, full), (lengths,), weights, both,
        (*corrected, *middles, *ends, goal), rows, 6,
    )
    even_saved = kept[0:3]
    received = lax.ppermute(
        turned, "layer", [(i + 1, i) for i in range(layer_count - 1)]
    )
    linear_outs = [
        ((count, *shape), kind, (None, *shape), lambda i, order, n=len(shape): (i,) + (0,) * n)
        for shape, kind in (full, full, *saved, *saved)
    ]
    linear_outs += [
        ((2, columns, count * rows), BF, (2, columns, rows), lambda i, order: (0, 0, i))
        for columns in (width, width, hidden)
    ]
    gathered = [gather_dp(chunk, turned) for chunk in chunks]
    every = [gathered[c][i] for i in range(count) for c in range(CHUNKS)]

    def all_linear():
        return tuple(
            call_each(
                all_linear_kernel, linear_outs, order, (sizes,), every, weights
            )
        )

    linear = lax.cond(device < layer_count - 2, all_linear, lambda: tuple(unwritten([out[0:2] for out in linear_outs])))
    received, linear = lax.optimization_barrier((received, linear))
    got = call(
        back_kernel, (piece,) * (2 * CHUNKS), (is_last,), weights, both,
        (guess, received, corrected, middles, *kept), rows, 4,
    )
    relaxed, fine = got[0:CHUNKS], got[CHUNKS:]
    adjoint_ends, adjoint_out = list(relaxed), list(fine)
    carried = [jnp.zeros((c * part, 2 * width), F32) for c in range(1, CHUNKS)]
    for block in range(layer_count - 3, -1, -1):
        incoming = [
            lax.ppermute(adjoint_out[c], "layer", [(block + 1, block)])
            for c in range(CHUNKS - 1, -1, -1)
        ][::-1]
        if block == 0:
            adjoint_ends = [
                jnp.where(device == 0, new, old) for new, old in zip(incoming, adjoint_ends)
            ]
            gathered = [gather_dp(adjoint_ends[c]) for c in range(CHUNKS - 1, -1, -1)][::-1]
        for c in range(CHUNKS - 1, -1, -1):
            outs = (piece, piece)
            old = (adjoint_ends[c], adjoint_out[c])
            if c > 0:
                outs += (((c * part, 2 * width), F32),)
                old += (carried[c - 1],)
            later = () if c == CHUNKS - 1 else (carried[c],)
            got = lax.cond(
                device == block,
                functools.partial(
                    call, functools.partial(adjoint_kernel, c), outs, (), weights,
                    first_layer, (incoming[c], relaxed[c], fine[c], corrected, *even_saved, *later),
                    part, 2,
                ),
                lambda old=old: old,
            )
            adjoint_ends[c], adjoint_out[c] = got[0:2]
            if c > 0:
                carried[c - 1] = got[2]
    linear, adjoint_out = lax.optimization_barrier((linear, adjoint_out))
    linear = lax.cond(device < layer_count - 2, lambda: linear, all_linear)
    every_adjoint = [gathered[c][i] for i in range(count) for c in range(CHUNKS)]
    rights = [
        ((2, count, rows, columns), BF, (2, None, rows, columns), lambda i, order: (0, i, 0, 0))
        for columns in (3 * width, hidden, width)
    ]
    got = call_each(
        all_back_kernel, rights, order, (), every_adjoint, weights, linear[0:8]
    )
    results = gradients(linear[8:11], got, weights)
    adjoint_out = jnp.concatenate(adjoint_out, axis=0)
    return (ends[None, None], adjoint_out[None, None], *results)


def solution(mesh):
    in_specs = (
        P("layer", "dp", None, None),
        P("dp", None, None),
        P("dp"),
        P("layer", None, None),
        P("layer", None, None),
        P("layer", None, None),
        P("layer", None, None),
    )
    out_specs = (
        P("layer", "dp", None, None),
        P("layer", "dp", None, None),
        P("layer", None, None),
        P("layer", None, None),
        P("layer", None, None),
        P("layer", None, None),
    )
    return jax.shard_map(
        on_device, mesh=mesh, in_specs=in_specs, out_specs=out_specs, check_vma=False
    )
```

```python
import functools
import math

import jax
import jax.numpy as jnp
from jax import lax
from jax.experimental import pallas as pl
from jax.experimental.pallas import tpu as pltpu
from jax.sharding import PartitionSpec as P

HEADS = 8
STEP = 0.125
CHUNKS = 2
PAIR = 128
TILE = 512
TOGETHER = 2
WHOLE_LIMIT = 60 * 1024 * 1024

BF = jnp.bfloat16
F32 = jnp.float32
NN = ((1,), (0,))
NT = ((1,), (1,))
TN = ((0,), (0,))
GELU_A = math.sqrt(2.0 / math.pi)
GELU_B = 0.044715


def dot(a, b, dims=NN):
    return lax.dot_general(a, b, (dims, ((), ())), preferred_element_type=F32)


def norm_scale(u):
    return lax.rsqrt(jnp.mean(u * u, axis=-1, keepdims=True) + 1e-06)


def half_masks(value):
    lane = lax.broadcasted_iota(jnp.int32, (1, PAIR), 1)
    first = jnp.where(lane < PAIR // 2, value, 0.0).astype(BF)
    second = jnp.where(lane < PAIR // 2, 0.0, value).astype(BF)
    return (first, second)


def join(pair):
    lane = lax.broadcasted_iota(jnp.int32, pair[0].shape, 1)
    return jnp.where(lane < PAIR // 2, pair[0], pair[1])


def gelu_parts(x):
    inner = jnp.tanh(GELU_A * (x + GELU_B * (x * x * x)))
    return 0.5 * (1.0 + inner), inner


def at(i, size, base=0):
    return slice(base + i * size, base + (i + 1) * size)


def loop(count, body):
    for i in range(count):
        body(i)


class Layer:
    def __init__(self, index, sources, targets, sems, when=None):
        self.index, self.sources, self.targets, self.sems = index, sources, targets, sems
        self.when, self.waiting = when, set()

    def copy(self, i):
        source = self.sources[i].at[self.index]
        return pltpu.make_async_copy(source, self.targets[i], self.sems.at[i])

    def start(self, order):
        if self.when is None:
            for i in order:
                self.copy(i).start()
            self.waiting = set(order)

    def get(self, i):
        if i in self.waiting:
            self.copy(i).wait()
            self.waiting.remove(i)
        return self.targets[i]


def fetch(layers, when):
    @pl.when(when)
    def _():
        for layer in layers:
            for i in range(len(layer.targets)):
                layer.copy(i).start()
        for layer in layers:
            for i in range(len(layer.targets)):
                layer.copy(i).wait()


QKV, OUT, UP, DOWN = range(4)
FORWARD = (QKV, UP, OUT, DOWN)
BACKWARD = (OUT, DOWN, QKV, UP)


def attention_sides(packed, pair, width):
    cols = pair * PAIR
    return [packed[:, base + cols : base + cols + PAIR] for base in (0, width, 2 * width)]


def forward_rows(u, layer, length, row0=0, old=None, whole_rows=0):
    rows, width = u.shape
    head = width // HEADS
    normed = (u * norm_scale(u)).astype(BF)
    packed = dot(normed, layer.get(QKV)[...]).astype(BF)
    own = packed[:, width:]
    both = own if old is None else jnp.concatenate([old, own], axis=0)
    if whole_rows > both.shape[0]:
        both = jnp.concatenate([both, both[0 : whole_rows - both.shape[0]]], axis=0)
    shape = (rows, both.shape[0])
    key_pos = lax.broadcasted_iota(jnp.int32, shape, 1)
    query_pos = lax.broadcasted_iota(jnp.int32, shape, 0) + row0
    seen = (key_pos <= query_pos) & (key_pos < length)
    masks = half_masks(head**-0.5)
    parts = []
    for pair in range(width // PAIR):
        cols = slice(pair * PAIR, (pair + 1) * PAIR)
        keys, vals = both[:, cols], both[:, width + pair * PAIR : width + (pair + 1) * PAIR]
        outs = []
        for mask in masks:
            scores = dot(packed[:, cols] * mask, keys, NT)
            scores = jnp.where(seen, scores, -jnp.inf)
            weight = jnp.exp(scores - jnp.max(scores, axis=-1, keepdims=True))
            probs = (weight * (1.0 / jnp.sum(weight, axis=-1, keepdims=True))).astype(BF)
            outs.append(dot(probs, vals))
        parts.append(join(outs).astype(BF))
    context = jnp.concatenate(parts, axis=1)
    up = dot(normed, layer.get(UP)[...])
    hidden = (up * gelu_parts(up)[0]).astype(BF)
    return dot(context, layer.get(OUT)[...]) + dot(hidden, layer.get(DOWN)[...]), own


def linearize_rows(u, layer, length, saved, factors=None):
    packed_ref, probs_ref, slope_ref = saved
    rows, width = u.shape
    head = width // HEADS
    wide = u * norm_scale(u)
    normed = wide.astype(BF)
    packed = dot(normed, layer.get(QKV)[...]).astype(BF)
    packed_ref[...] = packed
    key_pos = lax.broadcasted_iota(jnp.int32, (rows, rows), 0)
    query_pos = lax.broadcasted_iota(jnp.int32, (rows, rows), 1)
    seen = (key_pos <= query_pos) & (key_pos < length)
    masks = half_masks(head**-0.5)
    parts = []
    for pair in range(width // PAIR):
        queries, keys, vals = attention_sides(packed, pair, width)
        outs = []
        for half, mask in enumerate(masks):
            scores = dot(keys, queries * mask, NT)
            scores = jnp.where(seen, scores, -jnp.inf)
            weight = jnp.exp(scores - jnp.max(scores, axis=0, keepdims=True))
            probs = (weight * (1.0 / jnp.sum(weight, axis=0, keepdims=True))).astype(BF)
            probs_ref[2 * pair + half] = probs
            if factors is not None:
                outs.append(dot(probs, vals, TN))
        if factors is not None:
            parts.append(join(outs))
    up = dot(normed, layer.get(UP)[...])
    gate, inner = gelu_parts(up)
    rise = GELU_A + 3.0 * GELU_A * GELU_B * up * up
    slope_ref[...] = (gate + 0.5 * up * (1.0 - inner * inner) * rise).astype(BF)
    if factors is None:
        return None
    context, hidden = jnp.concatenate(parts, axis=1), up * gate
    for ref, value in zip(factors, (wide, context, hidden)):
        ref[...] = value.T.astype(BF)
    return context.astype(BF), hidden.astype(BF)


def backward_rows(ct, u, layer, saved, row0=0, later=None, earlier=None, right=None):
    width = ct.shape[1]
    low = ct.astype(BF)
    d_context = dot(low, layer.get(OUT)[...], NT).astype(BF)
    d_hidden = dot(low, layer.get(DOWN)[...], NT)
    rows = ct.shape[0] // len(saved)
    d_ups, d_packs = [], []
    for i, one in enumerate(saved):
        part = slice(i * rows, (i + 1) * rows)
        slope = one[2][row0 : row0 + rows, :].astype(F32)
        d_ups.append((d_hidden[part] * slope).astype(BF))
        d_packs.append(backward_attention(d_context[part], one, row0, later, earlier))
    d_up, d_packed = jnp.concatenate(d_ups, axis=0), jnp.concatenate(d_packs, axis=0)
    if right is not None:
        for ref, value in zip(right, (d_packed, d_up, low)):
            for i in range(len(saved)):
                ref[i] = value[i * rows : (i + 1) * rows]
    d_normed = dot(d_packed, layer.get(QKV)[...], NT) + dot(d_up, layer.get(UP)[...], NT)
    scale = norm_scale(u)
    unit = u * scale
    return scale * (d_normed - unit * jnp.mean(unit * d_normed, axis=-1, keepdims=True))


def backward_attention(d_context, saved, row0, later, earlier):
    packed_ref, probs_ref, _ = saved
    rows, width = d_context.shape
    head = width // HEADS
    end = row0 + rows
    ones = half_masks(1.0)
    d_queries, d_sides = [], [[], []]
    for pair in range(width // PAIR):
        lo = pair * PAIR
        queries = packed_ref[row0:end, lo : lo + PAIR]
        keys = packed_ref[:, width + lo : width + lo + PAIR]
        vals = packed_ref[:, 2 * width + lo : 2 * width + lo + PAIR]
        d_pair = d_context[:, lo : lo + PAIR]
        dq, dk, dv = [], [], []
        for half, mask in enumerate(ones):
            probs = probs_ref[2 * pair + half, :, row0:end]
            wide = probs.astype(F32)
            d_probs = dot(vals, d_pair * mask, NT)
            mean = jnp.sum(wide * d_probs, axis=0, keepdims=True)
            d_scores = (wide * (d_probs - mean) * head**-0.5).astype(BF)
            dq.append(dot(d_scores, keys, TN))
            dk.append(dot(d_scores, queries))
            dv.append(dot(probs, d_pair))
        d_queries.append(join(dq).astype(BF))
        for side, value in enumerate((join(dk)[0:end], join(dv)[0:end])):
            base = side * width + lo
            if later is not None:
                value = value + later[0:end, base : base + PAIR]
            d_sides[side].append(value[row0:end].astype(BF))
            if earlier is not None:
                earlier[:, base : base + PAIR] = value[0:row0]
    return jnp.concatenate([*d_queries, *d_sides[0], *d_sides[1]], axis=1)


def whole(refs):
    return jnp.concatenate([ref[...] for ref in refs], axis=0)


def split(value, refs):
    rows = refs[0].shape[0]
    for c, ref in enumerate(refs):
        ref[...] = value[c * rows : (c + 1) * rows]


def relax_kernel(smem, ins, outs, layers):
    even, odd = layers
    even.start(FORWARD)
    odd.start(FORWARD)
    length = smem[0][0]
    state = ins[0][...]
    state = state + STEP * forward_rows(state, even, length)[0]
    outs[0][...] = state + STEP * forward_rows(state, odd, length)[0]


def fine_kernel(smem, ins, outs, layers):
    even, odd = layers
    even.start(FORWARD)
    odd.start(FORWARD)
    length = smem[0][0]
    state = jnp.where(smem[1][0] == 1, ins[0][...], ins[1][...])
    value = forward_rows(state, even, length)[0]
    middle = state + STEP * value
    split(state, outs[0:CHUNKS])
    split(middle, outs[CHUNKS : 2 * CHUNKS])
    coarse = state + 2.0 * STEP * value
    end = middle + STEP * forward_rows(middle, odd, length)[0]
    split(end, outs[2 * CHUNKS : 3 * CHUNKS])
    split(end - coarse, outs[3 * CHUNKS : 4 * CHUNKS])


def coarse_kernel(chunk, smem, ins, outs, layers):
    (even,) = layers
    even.start(FORWARD)
    state, defect = ins[0:2]
    old = ins[2][...] if chunk > 0 else None
    current = state[...]
    rows = current.shape[0]
    value, own = forward_rows(
        current, even, smem[0][0], chunk * rows, old, CHUNKS * rows
    )
    outs[0][...] = current
    outs[1][...] = current + STEP * value
    outs[2][...] = current + 2.0 * STEP * value + defect[...]
    if len(outs) > 3:
        if chunk > 0:
            outs[3][0 : chunk * rows, :] = old
        outs[3][chunk * rows :, :] = own


def turn_kernel(smem, ins, outs, layers):
    even, odd = layers
    odd.start(FORWARD)
    even.start(FORWARD)
    length = smem[0][0]
    corrected, middles, ends = (whole(ins[i * CHUNKS : (i + 1) * CHUNKS]) for i in range(3))
    target = ins[3 * CHUNKS]
    even_saved, odd_saved = outs[0:3], outs[3:6]
    guess_ref, out, corrected_ref, middles_ref, ends_ref = outs[6:]
    corrected_ref[...] = corrected
    middles_ref[...] = middles
    ends_ref[...] = ends
    position = lax.broadcasted_iota(jnp.int32, ends.shape, 0)
    guess_ref[...] = jnp.where(position < length, ends - target[...], 0.0)
    linearize_rows(middles, odd, length, odd_saved)
    linearize_rows(corrected, even, length, even_saved)
    state = guess_ref[...]
    state = state + STEP * backward_rows(state, middles, odd, [odd_saved])
    out[...] = state + STEP * backward_rows(state, corrected, even, [even_saved])


def back_kernel(smem, ins, outs, layers):
    even, odd = layers
    odd.start(BACKWARD)
    even.start(BACKWARD)
    guess, received, corrected, middles = ins[0:4]
    even_saved, odd_saved = ins[4:7], ins[7:10]
    state = jnp.where(smem[0][0] == 1, guess[...], received[...])
    split(state, outs[0:CHUNKS])
    state = state + STEP * backward_rows(state, middles[...], odd, [odd_saved])
    state = state + STEP * backward_rows(state, corrected[...], even, [even_saved])
    split(state, outs[CHUNKS : 2 * CHUNKS])


def adjoint_kernel(chunk, smem, ins, outs, layers):
    (even,) = layers
    even.start(BACKWARD)
    incoming, relaxed, fine, corrected = ins[0:4]
    saved = ins[4:7]
    later = ins[7] if chunk < CHUNKS - 1 else None
    rows = incoming.shape[0]
    current = incoming[...]
    gap = current - relaxed[...]
    state = corrected[chunk * rows : (chunk + 1) * rows, :]
    change = backward_rows(
        gap, state, even, [saved], chunk * rows, later, outs[2] if chunk > 0 else None
    )
    outs[0][...] = current
    outs[1][...] = fine[...] + (gap + 2.0 * STEP * change)


def first_block_kernel(smem, ins, outs, layers):
    del smem
    (even,) = layers
    even.start(BACKWARD)
    current, relaxed, fine = (whole(ins[i * CHUNKS : (i + 1) * CHUNKS]) for i in range(3))
    gap = current - relaxed
    change = backward_rows(gap, ins[3 * CHUNKS][...], even, [ins[3 * CHUNKS + 1 :]])
    split(fine + (gap + 2.0 * STEP * change), outs)


def pick(place, blocks, held, first_row=0):
    for i, group in enumerate(blocks):

        @pl.when(place == i)
        def _(group=group):
            first = first_row
            for ref in group:
                held[first : first + ref.shape[0], :] = ref[...]
                first += ref.shape[0]


def all_linear_kernel(order, smem, ins, moving, outs, layers, held):
    del moving
    pick(
        order[pl.program_id(0)], [ins[i : i + CHUNKS] for i in range(0, len(ins), CHUNKS)], held
    )
    even, odd = layers
    corrected, middles = outs[0:2]
    even_saved, odd_saved = outs[2:5], outs[5:8]
    even_factors, odd_factors = ([ref.at[i] for ref in outs[8:11]] for i in range(2))
    length = smem[0][order[pl.program_id(0)]]
    state = held[...]
    corrected[...] = state
    context, hidden = linearize_rows(state, even, length, even_saved, even_factors)
    value = dot(context, even.get(OUT)[...]) + dot(hidden, even.get(DOWN)[...])
    middle = state + STEP * value
    middles[...] = middle
    linearize_rows(middle, odd, length, odd_saved, odd_factors)


def all_back_kernel(order, smem, ins, moving, outs, layers, held):
    del smem
    together, rows = moving[0].shape[0:2]
    blocks = [ins[i : i + CHUNKS] for i in range(0, len(ins), CHUNKS)]
    for i in range(together):
        pick(order[pl.program_id(0) * together + i], blocks, held, i * rows)
    even, odd = layers
    corrected, middles = (
        jnp.concatenate([ref[i] for i in range(together)], axis=0) for ref in moving[0:2]
    )
    even_saved, odd_saved = (
        [[ref.at[i] for ref in refs] for i in range(together)] for refs in (moving[2:5], moving[5:8])
    )
    even_right, odd_right = ([ref.at[i] for ref in outs] for i in range(2))
    state = held[...]
    change = backward_rows(state, middles, odd, odd_saved, right=odd_right)
    state = state + STEP * change
    backward_rows(state, corrected, even, even_saved, right=even_right)


def gradient_kernel(count, steps, *refs):
    (normed, context, hidden), (d_packed, d_up, low) = refs[0:3], refs[3:6]
    outs, sums, sems = refs[6:10], refs[10:14], refs[14]
    layer, k = pl.program_id(0), pl.program_id(1)
    pairs = ((normed, d_packed), (context, low), (normed, d_up), (hidden, low))
    tile = TILE // 2
    total = jnp.zeros((1, tile), F32)
    for (left, right), held in zip(pairs, sums):
        depth = left.shape[1]

        def step(i, total, left=left, right=right, held=held, depth=depth):
            cols = pl.ds(pl.multiple_of(i * tile, tile), tile)
            value = STEP * dot(left[...], right[:, :, cols].reshape(depth, tile))
            if steps > 1:
                value = jnp.where(k == 0, value, held[layer, :, cols] + value)
            held[layer, :, cols] = value
            return total + jnp.sum(value * value, axis=0, keepdims=True)

        total = lax.fori_loop(0, right.shape[2] // tile, step, total)

    def copies(index):
        return [
            pltpu.make_async_copy(held.at[index], out.at[index], sems.at[i])
            for i, (held, out) in enumerate(zip(sums, outs))
        ]

    @pl.when(k == pl.num_programs(1) - 1)
    def _():
        square = jnp.sum(total, axis=1, keepdims=True)
        inverse = 1.0 / jnp.sqrt(square / count + 1e-06)
        for held in sums:
            held[layer] = held[layer] * inverse

        @pl.when(layer == 0)
        def _():
            for copy in copies(0):
                copy.start()

        @pl.when(layer == 1)
        def _():
            for copy in copies(0):
                copy.wait()
            for copy in copies(1):
                copy.start()
            for copy in copies(1):
                copy.wait()


def gradients(lefts, rights, weights):
    _, count, rows, _ = rights[0].shape
    group = min(count, 4)
    sizes = [w.shape[1:] for w in weights]
    blocks = [(2, x.shape[1] * group * rows) for x in lefts]
    blocks += [(2, group * rows * x.shape[3]) for x in rights]
    return pl.pallas_call(
        functools.partial(
            gradient_kernel, float(sum(math.prod(size) for size in sizes)), count // group
        ),
        grid=(2, count // group),
        in_specs=[
            pl.BlockSpec((None, x.shape[1], group * rows), lambda i, k: (i, 0, k)) for x in lefts
        ]
        + [
            pl.BlockSpec((None, group, rows, x.shape[3]), lambda i, k: (i, k, 0, 0))
            for x in rights
        ],
        out_specs=tuple(pl.BlockSpec(memory_space=pl.ANY) for _ in sizes),
        out_shape=tuple(jax.ShapeDtypeStruct((2, *size), F32) for size in sizes),
        scratch_shapes=[pltpu.VMEM((2, *size), F32) for size in sizes]
        + [pltpu.SemaphoreType.DMA((len(sizes),))],
        cost_estimate=pl.CostEstimate(
            flops=4 * count * rows * sum(math.prod(size) for size in sizes),
            bytes_accessed=0,
            transcendentals=0,
        ),
        compiler_params=room(
            [(block, BF) for block in blocks] + [((2, *size), F32) for size in sizes], [None]
        ),
    )(*lefts, *rights)


def nothing_kernel(*refs):
    del refs


def scratch(weights, layers):
    shapes = [pltpu.VMEM(w.shape[1:], w.dtype) for _ in layers for w in weights]
    return shapes + [pltpu.SemaphoreType.DMA((len(layers), len(weights)))]


def room(shapes, scratches):
    total = sum(math.prod(shape) * jnp.dtype(kind).itemsize for shape, kind in shapes)
    for item in scratches[:-1]:
        total += math.prod(item.shape) * jnp.dtype(item.dtype).itemsize
    return pltpu.CompilerParams(vmem_limit_bytes=int(total * 1.1) + 10 * 1024 * 1024)


def unpack(refs, sources, layers, when=None):
    count = len(sources)
    refs, sems = refs[:-1], refs[-1]
    return [
        Layer(index, sources, refs[i * count : (i + 1) * count], sems.at[i], when)
        for i, index in enumerate(layers)
    ]


def cost(rows, weights, layers):
    flops = 2 * rows * sum(math.prod(w.shape[1:]) for w in weights) * layers
    return pl.CostEstimate(flops=6 * flops, bytes_accessed=0, transcendentals=0)


def call(kernel, outs, smem, weights, layers, ins, rows, passes=1, limit=None):
    counts = [len(smem), len(ins), len(weights), len(outs)]
    held = scratch(weights, layers)

    def body(*refs):
        cuts = [sum(counts[:i]) for i in range(5)]
        parts = [refs[cuts[i] : cuts[i + 1]] for i in range(4)]
        kernel(parts[0], parts[1], parts[3], unpack(refs[cuts[4] :], parts[2], layers))

    return pl.pallas_call(
        body,
        out_shape=tuple(jax.ShapeDtypeStruct(shape, kind) for shape, kind in outs),
        in_specs=[pl.BlockSpec(memory_space=pltpu.SMEM)] * len(smem)
        + [pl.BlockSpec(memory_space=pltpu.VMEM)] * len(ins)
        + [pl.BlockSpec(memory_space=pl.ANY)] * len(weights),
        out_specs=tuple(pl.BlockSpec(memory_space=pltpu.VMEM) for _ in outs),
        scratch_shapes=held,
        cost_estimate=cost(rows, weights, passes),
        compiler_params=pltpu.CompilerParams(vmem_limit_bytes=limit)
        if limit
        else room([*((x.shape, x.dtype) for x in ins), *outs], held),
    )(*smem, *ins, *weights)


def call_each(kernel, outs, order, smem, gathered, weights, moving=(), together=None):
    rows = sum(x.shape[0] for x in gathered) // order.shape[0]
    width = gathered[0].shape[1]
    specs = [pl.BlockSpec(shape, index) for _, _, shape, index in outs]
    sizes = [[size for size in shape if size] for _, _, shape, _ in outs]
    outs = [(shape, kind) for shape, kind, _, _ in outs]
    held = scratch(weights, (0, 1))
    counts = [len(smem), len(gathered), len(weights), len(moving), len(outs)]

    def block(shape):
        rest = (0,) * (len(shape) - 1)
        return pl.BlockSpec((together, *shape[1:]), lambda i, order: (i, *rest))

    steps = order.shape[0] // (together or 1)

    def body(order_ref, *refs):
        cuts = [sum(counts[:i]) for i in range(6)]
        parts = [refs[cuts[i] : cuts[i + 1]] for i in range(5)]
        first = pl.program_id(0) == 0
        layers = unpack(refs[cuts[5] : -1], parts[2], (0, 1), first)
        fetch(layers, first)
        kernel(order_ref, parts[0], parts[1], parts[3], parts[4], layers, refs[-1])

    return pl.pallas_call(
        body,
        grid_spec=pltpu.PrefetchScalarGridSpec(
            num_scalar_prefetch=1,
            grid=(steps,),
            in_specs=[pl.BlockSpec(memory_space=pltpu.SMEM)] * len(smem)
            + [pl.BlockSpec(memory_space=pltpu.VMEM)] * len(gathered)
            + [pl.BlockSpec(memory_space=pl.ANY)] * len(weights)
            + [block(x.shape) for x in moving],
            out_specs=tuple(specs),
            scratch_shapes=held + [pltpu.VMEM(((together or 1) * rows, width), F32)],
        ),
        out_shape=tuple(jax.ShapeDtypeStruct(shape, kind) for shape, kind in outs),
        cost_estimate=cost(rows, weights, 4 * order.shape[0]),
        compiler_params=pltpu.CompilerParams(
            vmem_limit_bytes=WHOLE_LIMIT
        )
        if together
        else room(
            [(x.shape, x.dtype) for x in gathered]
            + 2 * [(shape, kind) for shape, (_, kind) in zip(sizes, outs)],
            held,
        ),
    )(order, *smem, *gathered, *weights, *moving)


def unwritten(outs):
    return pl.pallas_call(
        nothing_kernel,
        out_shape=tuple(jax.ShapeDtypeStruct(shape, kind) for shape, kind in outs),
        out_specs=tuple(pl.BlockSpec(memory_space=pl.ANY) for _ in outs),
    )()


def gather_dp(block, then=None):
    count = lax.axis_size("dp")
    if count == 1:
        return [block]
    swap = [(i, i ^ 1) for i in range(count)]
    mine = [block]
    for turn in range(1, count // 2):
        route = [(i, (i + 2 * turn) % count) for i in range(count)]
        mine.append(lax.ppermute(block, "dp", route))
    theirs = [lax.ppermute(block, "dp", swap)]
    if then is not None:
        mine, _ = lax.optimization_barrier((mine, then))
    theirs += [lax.ppermute(own, "dp", swap) for own in mine[1:]]
    return [x for pair in zip(mine, theirs) for x in pair]


def gathered_order():
    count = lax.axis_size("dp")
    place = lax.axis_index("dp")
    other = jnp.arange(count, dtype=jnp.int32)
    turn = (place // 2 - other // 2) % max(count // 2, 1)
    return (2 * turn + (place + other) % 2).astype(jnp.int32) if count > 1 else other


def on_device(states, target, lengths, qkv_weight, out_weight, up_weight, down_weight):
    layer_count = lax.axis_size("layer")
    device = lax.axis_index("layer")
    weights = (qkv_weight, out_weight, up_weight, down_weight)
    starts, goal = states[0, 0], target[0]
    rows, width = starts.shape
    hidden = up_weight.shape[2]
    part = rows // CHUNKS
    full = ((rows, width), F32)
    piece = ((part, width), F32)
    saved = (((rows, 3 * width), BF), ((HEADS, rows, rows), BF), ((rows, hidden), BF))
    sizes = jnp.concatenate(gather_dp(lengths))
    both, first_layer = (0, 1), (0,)
    order = gathered_order()
    count = order.shape[0]
    is_first = (device == 0).astype(jnp.int32).reshape(1)
    is_last = (device == layer_count - 1).astype(jnp.int32).reshape(1)

    (first_end,) = call(relax_kernel, (full,), (lengths,), weights, both, (starts,), rows, 2)
    received = lax.ppermute(
        first_end, "layer", [(i, i + 1) for i in range(layer_count - 1)]
    )
    received, sizes = lax.optimization_barrier((received, sizes))
    got = call(
        fine_kernel, (piece,) * (4 * CHUNKS), (lengths, is_first), weights, both,
        (starts, received), rows, 2,
    )
    corrected, middles, ends, defect = (
        list(got[i * CHUNKS : (i + 1) * CHUNKS]) for i in range(4)
    )
    stores = [jnp.zeros((c * part, 2 * width), BF) for c in range(1, CHUNKS)]
    for block in range(2, layer_count):
        incoming = [lax.ppermute(ends[c], "layer", [(block - 1, block)]) for c in range(CHUNKS)]
        for c in range(CHUNKS):
            outs = (piece, piece, piece)
            kept = (corrected[c], middles[c], ends[c])
            if c < CHUNKS - 1:
                outs += (((((c + 1) * part), 2 * width), BF),)
                kept += (stores[c],)
            old = () if c == 0 else (stores[c - 1],)
            got = lax.cond(
                device == block,
                functools.partial(
                    call, functools.partial(coarse_kernel, c), outs, (lengths,), weights,
                    first_layer, (incoming[c], defect[c], *old), part,
                ),
                lambda kept=kept: kept,
            )
            corrected[c], middles[c], ends[c] = got[0:3]
            if c < CHUNKS - 1:
                stores[c] = got[3]
    chunks = corrected
    *kept, guess, turned, corrected, middles, ends = call(
        turn_kernel, (*saved, *saved, full, full, full, full, full), (lengths,), weights, both,
        (*corrected, *middles, *ends, goal), rows, 6,
    )
    even_saved = kept[0:3]
    received = lax.ppermute(
        turned, "layer", [(i + 1, i) for i in range(layer_count - 1)]
    )
    linear_outs = [
        ((count, *shape), kind, (None, *shape), lambda i, order, n=len(shape): (i,) + (0,) * n)
        for shape, kind in (full, full, *saved, *saved)
    ]
    linear_outs += [
        ((2, columns, count * rows), BF, (2, columns, rows), lambda i, order: (0, 0, i))
        for columns in (width, width, hidden)
    ]
    gathered = [gather_dp(chunk, turned) for chunk in chunks]
    every = [gathered[c][i] for i in range(count) for c in range(CHUNKS)]

    def all_linear():
        return tuple(
            call_each(
                all_linear_kernel, linear_outs, order, (sizes,), every, weights
            )
        )

    linear = lax.cond(device < layer_count - 2, all_linear, lambda: tuple(unwritten([out[0:2] for out in linear_outs])))
    received, linear = lax.optimization_barrier((received, linear))
    got = call(
        back_kernel, (piece,) * (2 * CHUNKS), (is_last,), weights, both,
        (guess, received, corrected, middles, *kept), rows, 4, WHOLE_LIMIT,
    )
    relaxed, fine = got[0:CHUNKS], got[CHUNKS:]
    adjoint_ends, adjoint_out = list(relaxed), list(fine)
    carried = [jnp.zeros((c * part, 2 * width), F32) for c in range(1, CHUNKS)]
    for block in range(layer_count - 3, -1, -1):
        incoming = [
            lax.ppermute(adjoint_out[c], "layer", [(block + 1, block)])
            for c in range(CHUNKS - 1, -1, -1)
        ][::-1]
        if block == 0:
            adjoint_ends = [
                jnp.where(device == 0, new, old) for new, old in zip(incoming, adjoint_ends)
            ]
            gathered = [gather_dp(adjoint_ends[c]) for c in range(CHUNKS - 1, -1, -1)][::-1]
            adjoint_out = lax.cond(
                device == 0,
                functools.partial(
                    call, first_block_kernel, (piece,) * CHUNKS, (), weights, first_layer,
                    (*incoming, *relaxed, *fine, corrected, *even_saved), rows, 2,
                ),
                lambda adjoint_out=adjoint_out: tuple(adjoint_out),
            )
            break
        for c in range(CHUNKS - 1, -1, -1):
            outs = (piece, piece)
            old = (adjoint_ends[c], adjoint_out[c])
            if c > 0:
                outs += (((c * part, 2 * width), F32),)
                old += (carried[c - 1],)
            later = () if c == CHUNKS - 1 else (carried[c],)
            got = lax.cond(
                device == block,
                functools.partial(
                    call, functools.partial(adjoint_kernel, c), outs, (), weights,
                    first_layer, (incoming[c], relaxed[c], fine[c], corrected, *even_saved, *later),
                    part, 2,
                ),
                lambda old=old: old,
            )
            adjoint_ends[c], adjoint_out[c] = got[0:2]
            if c > 0:
                carried[c - 1] = got[2]
    linear, adjoint_out = lax.optimization_barrier((linear, adjoint_out))
    linear = lax.cond(device < layer_count - 2, lambda: linear, all_linear)
    every_adjoint = [gathered[c][i] for i in range(count) for c in range(CHUNKS)]
    rights = [
        ((2, count, rows, columns), BF, (2, TOGETHER, rows, columns), lambda i, order: (0, i, 0, 0))
        for columns in (3 * width, hidden, width)
    ]
    got = call_each(
        all_back_kernel, rights, order, (), every_adjoint, weights, linear[0:8], TOGETHER
    )
    results = gradients(linear[8:11], got, weights)
    adjoint_out = jnp.concatenate(adjoint_out, axis=0)
    return (ends[None, None], adjoint_out[None, None], *results)


def solution(mesh):
    in_specs = (
        P("layer", "dp", None, None),
        P("dp", None, None),
        P("dp"),
        P("layer", None, None),
        P("layer", None, None),
        P("layer", None, None),
        P("layer", None, None),
    )
    out_specs = (
        P("layer", "dp", None, None),
        P("layer", "dp", None, None),
        P("layer", None, None),
        P("layer", None, None),
        P("layer", None, None),
        P("layer", None, None),
    )
    return jax.shard_map(
        on_device, mesh=mesh, in_specs=in_specs, out_specs=out_specs, check_vma=False
    )
```

```python
import functools
import math

import jax
import jax.numpy as jnp
from jax import lax
from jax.experimental import pallas as pl
from jax.experimental.pallas import tpu as pltpu
from jax.sharding import PartitionSpec as P

HEADS = 8
STEP = 0.125
CHUNKS = 4
PAIR = 128
TILE = 512
PIECES = 2
WHOLE_LIMIT = 60 * 1024 * 1024

BF = jnp.bfloat16
F32 = jnp.float32
NN = ((1,), (0,))
NT = ((1,), (1,))
TN = ((0,), (0,))
GELU_A = math.sqrt(2.0 / math.pi)
GELU_B = 0.044715


def dot(a, b, dims=NN):
    return lax.dot_general(a, b, (dims, ((), ())), preferred_element_type=F32)


def norm_scale(u):
    return lax.rsqrt(jnp.mean(u * u, axis=-1, keepdims=True) + 1e-06)


def half_masks(value):
    lane = lax.broadcasted_iota(jnp.int32, (1, PAIR), 1)
    first = jnp.where(lane < PAIR // 2, value, 0.0).astype(BF)
    second = jnp.where(lane < PAIR // 2, 0.0, value).astype(BF)
    return (first, second)


def join(pair):
    lane = lax.broadcasted_iota(jnp.int32, pair[0].shape, 1)
    return jnp.where(lane < PAIR // 2, pair[0], pair[1])


def gelu_parts(x):
    inner = jnp.tanh(GELU_A * (x + GELU_B * (x * x * x)))
    return 0.5 * (1.0 + inner), inner


def at(i, size, base=0):
    return slice(base + i * size, base + (i + 1) * size)


def loop(count, body):
    for i in range(count):
        body(i)


class Layer:
    def __init__(self, index, sources, targets, sems, when=None):
        self.index, self.sources, self.targets, self.sems = index, sources, targets, sems
        self.when, self.waiting = when, set()

    def copy(self, i):
        source = self.sources[i].at[self.index]
        return pltpu.make_async_copy(source, self.targets[i], self.sems.at[i])

    def start(self, order):
        if self.when is None:
            for i in order:
                self.copy(i).start()
            self.waiting = set(order)

    def get(self, i):
        if i in self.waiting:
            self.copy(i).wait()
            self.waiting.remove(i)
        return self.targets[i]


def fetch(layers, when):
    @pl.when(when)
    def _():
        for layer in layers:
            for i in range(len(layer.targets)):
                layer.copy(i).start()
        for layer in layers:
            for i in range(len(layer.targets)):
                layer.copy(i).wait()


QKV, OUT, UP, DOWN = range(4)
FORWARD = (QKV, UP, OUT, DOWN)
BACKWARD = (OUT, DOWN, QKV, UP)


def attention_sides(packed, pair, width):
    cols = pair * PAIR
    return [packed[:, base + cols : base + cols + PAIR] for base in (0, width, 2 * width)]


def forward_rows(u, layer, length, row0=0, old=None, whole_rows=0):
    rows, width = u.shape
    head = width // HEADS
    normed = (u * norm_scale(u)).astype(BF)
    packed = dot(normed, layer.get(QKV)[...]).astype(BF)
    own = packed[:, width:]
    both = own if old is None else jnp.concatenate([old, own], axis=0)
    spare = whole_rows - both.shape[0]
    if spare > 0:
        both = jnp.concatenate([both, *([own] * (spare // rows))], axis=0)
    shape = (rows, both.shape[0])
    key_pos = lax.broadcasted_iota(jnp.int32, shape, 1)
    query_pos = lax.broadcasted_iota(jnp.int32, shape, 0) + row0
    seen = (key_pos <= query_pos) & (key_pos < length)
    masks = half_masks(head**-0.5)
    parts = []
    for pair in range(width // PAIR):
        cols = slice(pair * PAIR, (pair + 1) * PAIR)
        keys, vals = both[:, cols], both[:, width + pair * PAIR : width + (pair + 1) * PAIR]
        outs = []
        for mask in masks:
            scores = dot(packed[:, cols] * mask, keys, NT)
            scores = jnp.where(seen, scores, -jnp.inf)
            weight = jnp.exp(scores - jnp.max(scores, axis=-1, keepdims=True))
            probs = (weight * (1.0 / jnp.sum(weight, axis=-1, keepdims=True))).astype(BF)
            outs.append(dot(probs, vals))
        parts.append(join(outs).astype(BF))
    context = jnp.concatenate(parts, axis=1)
    up = dot(normed, layer.get(UP)[...])
    hidden = (up * gelu_parts(up)[0]).astype(BF)
    return dot(context, layer.get(OUT)[...]) + dot(hidden, layer.get(DOWN)[...]), own


def linearize_rows(u, layer, length, saved, factors=None):
    packed_ref, probs_ref, slope_ref = saved
    rows, width = u.shape
    head = width // HEADS
    wide = u * norm_scale(u)
    normed = wide.astype(BF)
    packed = dot(normed, layer.get(QKV)[...]).astype(BF)
    packed_ref[...] = packed
    key_pos = lax.broadcasted_iota(jnp.int32, (rows, rows), 0)
    query_pos = lax.broadcasted_iota(jnp.int32, (rows, rows), 1)
    seen = (key_pos <= query_pos) & (key_pos < length)
    masks = half_masks(head**-0.5)
    parts = []
    for pair in range(width // PAIR):
        queries, keys, vals = attention_sides(packed, pair, width)
        outs = []
        for half, mask in enumerate(masks):
            scores = dot(keys, queries * mask, NT)
            scores = jnp.where(seen, scores, -jnp.inf)
            weight = jnp.exp(scores - jnp.max(scores, axis=0, keepdims=True))
            probs = (weight * (1.0 / jnp.sum(weight, axis=0, keepdims=True))).astype(BF)
            probs_ref[2 * pair + half] = probs
            if factors is not None:
                outs.append(dot(probs, vals, TN))
        if factors is not None:
            parts.append(join(outs))
    up = dot(normed, layer.get(UP)[...])
    gate, inner = gelu_parts(up)
    rise = GELU_A + 3.0 * GELU_A * GELU_B * up * up
    slope_ref[...] = (gate + 0.5 * up * (1.0 - inner * inner) * rise).astype(BF)
    if factors is None:
        return None
    context, hidden = jnp.concatenate(parts, axis=1), up * gate
    for ref, value in zip(factors, (wide, context, hidden)):
        ref[...] = value.T.astype(BF)
    return context.astype(BF), hidden.astype(BF)


def backward_rows(ct, u, layer, saved, row0=0, later=None, earlier=None, right=None):
    width = ct.shape[1]
    low = ct.astype(BF)
    d_context = dot(low, layer.get(OUT)[...], NT).astype(BF)
    d_hidden = dot(low, layer.get(DOWN)[...], NT)
    rows = ct.shape[0] // len(saved)
    d_ups, d_packs = [], []
    for i, one in enumerate(saved):
        part = slice(i * rows, (i + 1) * rows)
        slope = one[2][row0 : row0 + rows, :].astype(F32)
        d_ups.append((d_hidden[part] * slope).astype(BF))
        d_packs.append(backward_attention(d_context[part], one, row0, later, earlier))
    d_up, d_packed = jnp.concatenate(d_ups, axis=0), jnp.concatenate(d_packs, axis=0)
    if right is not None:
        for ref, value in zip(right, (d_packed, d_up, low)):
            ref[...] = value
    d_normed = dot(d_packed, layer.get(QKV)[...], NT) + dot(d_up, layer.get(UP)[...], NT)
    scale = norm_scale(u)
    unit = u * scale
    return scale * (d_normed - unit * jnp.mean(unit * d_normed, axis=-1, keepdims=True))


def backward_attention(d_context, saved, row0, later, earlier):
    packed_ref, probs_ref, _ = saved
    rows, width = d_context.shape
    head = width // HEADS
    end = row0 + rows
    ones = half_masks(1.0)
    d_queries, d_sides = [], [[], []]
    for pair in range(width // PAIR):
        lo = pair * PAIR
        queries = packed_ref[row0:end, lo : lo + PAIR]
        keys = packed_ref[:, width + lo : width + lo + PAIR]
        vals = packed_ref[:, 2 * width + lo : 2 * width + lo + PAIR]
        d_pair = d_context[:, lo : lo + PAIR]
        dq, dk, dv = [], [], []
        for half, mask in enumerate(ones):
            probs = probs_ref[2 * pair + half, :, row0:end]
            wide = probs.astype(F32)
            d_probs = dot(vals, d_pair * mask, NT)
            mean = jnp.sum(wide * d_probs, axis=0, keepdims=True)
            d_scores = (wide * (d_probs - mean) * head**-0.5).astype(BF)
            dq.append(dot(d_scores, keys, TN))
            dk.append(dot(d_scores, queries))
            dv.append(dot(probs, d_pair))
        d_queries.append(join(dq).astype(BF))
        for side, value in enumerate((join(dk)[0:end], join(dv)[0:end])):
            base = side * width + lo
            if later is not None:
                value = value + later[0:end, base : base + PAIR]
            d_sides[side].append(value[row0:end].astype(BF))
            if earlier is not None:
                earlier[:, base : base + PAIR] = value[0:row0]
    return jnp.concatenate([*d_queries, *d_sides[0], *d_sides[1]], axis=1)


def whole(refs):
    return jnp.concatenate([ref[...] for ref in refs], axis=0)


def split(value, refs):
    rows = refs[0].shape[0]
    for c, ref in enumerate(refs):
        ref[...] = value[c * rows : (c + 1) * rows]


def relax_kernel(smem, ins, outs, layers):
    even, odd = layers
    even.start(FORWARD)
    odd.start(FORWARD)
    length = smem[0][0]
    state = ins[0][...]
    state = state + STEP * forward_rows(state, even, length)[0]
    outs[0][...] = state + STEP * forward_rows(state, odd, length)[0]


def fine_kernel(smem, ins, outs, layers):
    even, odd = layers
    even.start(FORWARD)
    odd.start(FORWARD)
    length = smem[0][0]
    state = jnp.where(smem[1][0] == 1, ins[0][...], ins[1][...])
    value = forward_rows(state, even, length)[0]
    middle = state + STEP * value
    split(state, outs[0:CHUNKS])
    split(middle, outs[CHUNKS : 2 * CHUNKS])
    coarse = state + 2.0 * STEP * value
    end = middle + STEP * forward_rows(middle, odd, length)[0]
    split(end, outs[2 * CHUNKS : 3 * CHUNKS])
    split(end - coarse, outs[3 * CHUNKS : 4 * CHUNKS])


def coarse_kernel(chunk, smem, ins, outs, layers):
    (even,) = layers
    even.start(FORWARD)
    state, defect = ins[0:2]
    old = ins[2][...] if chunk > 0 else None
    current = state[...]
    rows = current.shape[0]
    value, own = forward_rows(
        current, even, smem[0][0], chunk * rows, old, CHUNKS * rows
    )
    outs[0][...] = current
    outs[1][...] = current + STEP * value
    outs[2][...] = current + 2.0 * STEP * value + defect[...]
    if len(outs) > 3:
        if chunk > 0:
            outs[3][0 : chunk * rows, :] = old
        outs[3][chunk * rows :, :] = own


def turn_kernel(smem, ins, outs, layers):
    even, odd = layers
    odd.start(FORWARD)
    even.start(FORWARD)
    length = smem[0][0]
    corrected, middles, ends = (whole(ins[i * CHUNKS : (i + 1) * CHUNKS]) for i in range(3))
    target = ins[3 * CHUNKS]
    even_saved, odd_saved = outs[0:3], outs[3:6]
    guess_ref, out, corrected_ref, middles_ref, ends_ref = outs[6:]
    corrected_ref[...] = corrected
    middles_ref[...] = middles
    ends_ref[...] = ends
    position = lax.broadcasted_iota(jnp.int32, ends.shape, 0)
    guess_ref[...] = jnp.where(position < length, ends - target[...], 0.0)
    linearize_rows(middles, odd, length, odd_saved)
    linearize_rows(corrected, even, length, even_saved)
    state = guess_ref[...]
    state = state + STEP * backward_rows(state, middles, odd, [odd_saved])
    out[...] = state + STEP * backward_rows(state, corrected, even, [even_saved])


def back_kernel(smem, ins, outs, layers):
    even, odd = layers
    odd.start(BACKWARD)
    even.start(BACKWARD)
    guess, received, corrected, middles = ins[0:4]
    even_saved, odd_saved = ins[4:7], ins[7:10]
    state = jnp.where(smem[0][0] == 1, guess[...], received[...])
    split(state, outs[0:CHUNKS])
    state = state + STEP * backward_rows(state, middles[...], odd, [odd_saved])
    state = state + STEP * backward_rows(state, corrected[...], even, [even_saved])
    split(state, outs[CHUNKS : 2 * CHUNKS])


def adjoint_kernel(chunk, smem, ins, outs, layers):
    (even,) = layers
    even.start(BACKWARD)
    incoming, relaxed, fine, corrected = ins[0:4]
    saved = ins[4:7]
    later = ins[7] if chunk < CHUNKS - 1 else None
    rows = incoming.shape[0]
    current = incoming[...]
    gap = current - relaxed[...]
    state = corrected[chunk * rows : (chunk + 1) * rows, :]
    change = backward_rows(
        gap, state, even, [saved], chunk * rows, later, outs[2] if chunk > 0 else None
    )
    outs[0][...] = current
    outs[1][...] = fine[...] + (gap + 2.0 * STEP * change)


def first_block_kernel(smem, ins, outs, layers):
    del smem
    (even,) = layers
    even.start(BACKWARD)
    current, relaxed, fine = (whole(ins[i * CHUNKS : (i + 1) * CHUNKS]) for i in range(3))
    gap = current - relaxed
    change = backward_rows(gap, ins[3 * CHUNKS][...], even, [ins[3 * CHUNKS + 1 :]])
    split(fine + (gap + 2.0 * STEP * change), outs)


def pick(place, blocks, held):
    for i, group in enumerate(blocks):

        @pl.when(place == i)
        def _(group=group):
            first = 0
            for ref in group:
                held[first : first + ref.shape[0], :] = ref[...]
                first += ref.shape[0]


def all_linear_kernel(order, smem, ins, moving, outs, layers, held):
    del moving
    pick(
        order[pl.program_id(0)], [ins[i : i + PIECES] for i in range(0, len(ins), PIECES)], held
    )
    even, odd = layers
    corrected, middles = outs[0:2]
    even_saved, odd_saved = ([ref.at[i] for ref in outs[2:5]] for i in range(2))
    even_factors, odd_factors = ([ref.at[i] for ref in outs[5:8]] for i in range(2))
    length = smem[0][order[pl.program_id(0)]]
    state = held[...]
    corrected[...] = state
    context, hidden = linearize_rows(state, even, length, even_saved, even_factors)
    value = dot(context, even.get(OUT)[...]) + dot(hidden, even.get(DOWN)[...])
    middle = state + STEP * value
    middles[...] = middle
    linearize_rows(middle, odd, length, odd_saved, odd_factors)


def all_back_kernel(order, smem, ins, moving, outs, layers, held):
    del smem
    blocks = [ins[i : i + PIECES] for i in range(0, len(ins), PIECES)]
    pick(order[pl.program_id(0)], blocks, held)
    even, odd = layers
    corrected, middles = (ref[...] for ref in moving[0:2])
    even_saved, odd_saved = ([[ref.at[i] for ref in moving[2:5]]] for i in range(2))
    even_right, odd_right = ([ref.at[i] for ref in outs] for i in range(2))
    state = held[...]
    change = backward_rows(state, middles, odd, odd_saved, right=odd_right)
    state = state + STEP * change
    backward_rows(state, corrected, even, even_saved, right=even_right)


def gradient_kernel(count, steps, *refs):
    (normed, context, hidden), (d_packed, d_up, low) = refs[0:3], refs[3:6]
    outs, sums, sems = refs[6:10], refs[10:14], refs[14]
    layer, k = pl.program_id(0), pl.program_id(1)
    pairs = ((normed, d_packed), (context, low), (normed, d_up), (hidden, low))
    tile = TILE // 2
    total = jnp.zeros((1, tile), F32)
    for (left, right), held in zip(pairs, sums):
        depth = left.shape[1]

        def step(i, total, left=left, right=right, held=held, depth=depth):
            cols = pl.ds(pl.multiple_of(i * tile, tile), tile)
            value = STEP * dot(left[...], right[:, :, cols].reshape(depth, tile))
            if steps > 1:
                value = jnp.where(k == 0, value, held[layer, :, cols] + value)
            held[layer, :, cols] = value
            return total + jnp.sum(value * value, axis=0, keepdims=True)

        total = lax.fori_loop(0, right.shape[2] // tile, step, total)

    def copies(index):
        return [
            pltpu.make_async_copy(held.at[index], out.at[index], sems.at[i])
            for i, (held, out) in enumerate(zip(sums, outs))
        ]

    @pl.when(k == pl.num_programs(1) - 1)
    def _():
        square = jnp.sum(total, axis=1, keepdims=True)
        inverse = 1.0 / jnp.sqrt(square / count + 1e-06)
        for held in sums:
            held[layer] = held[layer] * inverse

        @pl.when(layer == 0)
        def _():
            for copy in copies(0):
                copy.start()

        @pl.when(layer == 1)
        def _():
            for copy in copies(0):
                copy.wait()
            for copy in copies(1):
                copy.start()
            for copy in copies(1):
                copy.wait()


def gradients(lefts, rights, weights):
    _, count, rows, _ = rights[0].shape
    group = min(count, 4)
    sizes = [w.shape[1:] for w in weights]
    blocks = [(2, x.shape[1] * group * rows) for x in lefts]
    blocks += [(2, group * rows * x.shape[3]) for x in rights]
    return pl.pallas_call(
        functools.partial(
            gradient_kernel, float(sum(math.prod(size) for size in sizes)), count // group
        ),
        grid=(2, count // group),
        in_specs=[
            pl.BlockSpec((None, x.shape[1], group * rows), lambda i, k: (i, 0, k)) for x in lefts
        ]
        + [
            pl.BlockSpec((None, group, rows, x.shape[3]), lambda i, k: (i, k, 0, 0))
            for x in rights
        ],
        out_specs=tuple(pl.BlockSpec(memory_space=pl.ANY) for _ in sizes),
        out_shape=tuple(jax.ShapeDtypeStruct((2, *size), F32) for size in sizes),
        scratch_shapes=[pltpu.VMEM((2, *size), F32) for size in sizes]
        + [pltpu.SemaphoreType.DMA((len(sizes),))],
        cost_estimate=pl.CostEstimate(
            flops=4 * count * rows * sum(math.prod(size) for size in sizes),
            bytes_accessed=0,
            transcendentals=0,
        ),
        compiler_params=room(
            [(block, BF) for block in blocks] + [((2, *size), F32) for size in sizes], [None]
        ),
    )(*lefts, *rights)


def nothing_kernel(*refs):
    del refs


def scratch(weights, layers):
    shapes = [pltpu.VMEM(w.shape[1:], w.dtype) for _ in layers for w in weights]
    return shapes + [pltpu.SemaphoreType.DMA((len(layers), len(weights)))]


def room(shapes, scratches):
    total = sum(math.prod(shape) * jnp.dtype(kind).itemsize for shape, kind in shapes)
    for item in scratches[:-1]:
        total += math.prod(item.shape) * jnp.dtype(item.dtype).itemsize
    return pltpu.CompilerParams(vmem_limit_bytes=int(total * 1.1) + 10 * 1024 * 1024)


def unpack(refs, sources, layers, when=None):
    count = len(sources)
    refs, sems = refs[:-1], refs[-1]
    return [
        Layer(index, sources, refs[i * count : (i + 1) * count], sems.at[i], when)
        for i, index in enumerate(layers)
    ]


def cost(rows, weights, layers):
    flops = 2 * rows * sum(math.prod(w.shape[1:]) for w in weights) * layers
    return pl.CostEstimate(flops=6 * flops, bytes_accessed=0, transcendentals=0)


def call(kernel, outs, smem, weights, layers, ins, rows, passes=1, limit=None):
    counts = [len(smem), len(ins), len(weights), len(outs)]
    held = scratch(weights, layers)

    def body(*refs):
        cuts = [sum(counts[:i]) for i in range(5)]
        parts = [refs[cuts[i] : cuts[i + 1]] for i in range(4)]
        kernel(parts[0], parts[1], parts[3], unpack(refs[cuts[4] :], parts[2], layers))

    return pl.pallas_call(
        body,
        out_shape=tuple(jax.ShapeDtypeStruct(shape, kind) for shape, kind in outs),
        in_specs=[pl.BlockSpec(memory_space=pltpu.SMEM)] * len(smem)
        + [pl.BlockSpec(memory_space=pltpu.VMEM)] * len(ins)
        + [pl.BlockSpec(memory_space=pl.ANY)] * len(weights),
        out_specs=tuple(pl.BlockSpec(memory_space=pltpu.VMEM) for _ in outs),
        scratch_shapes=held,
        cost_estimate=cost(rows, weights, passes),
        compiler_params=pltpu.CompilerParams(vmem_limit_bytes=limit)
        if limit
        else room([*((x.shape, x.dtype) for x in ins), *outs], held),
    )(*smem, *ins, *weights)


def call_each(kernel, outs, order, smem, gathered, weights, moving=(), limit=None, reused=()):
    rows = sum(x.shape[0] for x in gathered) // order.shape[0]
    width = gathered[0].shape[1]
    specs = [pl.BlockSpec(shape, index) for _, _, shape, index in outs]
    sizes = [[size for size in shape if size] for _, _, shape, _ in outs]
    outs = [(shape, kind) for shape, kind, _, _ in outs]
    held = scratch(weights, (0, 1))
    counts = [len(smem), len(gathered), len(weights), len(moving), len(outs)]

    before = 1 + len(smem) + len(gathered) + len(weights)
    moving_specs = [pl.BlockSpec(shape, index) for _, shape, index in moving]
    moving = [array for array, _, _ in moving]

    def body(order_ref, *refs):
        cuts = [sum(counts[:i]) for i in range(6)]
        parts = [refs[cuts[i] : cuts[i + 1]] for i in range(5)]
        first = pl.program_id(0) == 0
        layers = unpack(refs[cuts[5] : -1], parts[2], (0, 1), first)
        fetch(layers, first)
        kernel(order_ref, parts[0], parts[1], parts[3], parts[4], layers, refs[-1])

    return pl.pallas_call(
        body,
        grid_spec=pltpu.PrefetchScalarGridSpec(
            num_scalar_prefetch=1,
            grid=order.shape,
            in_specs=[pl.BlockSpec(memory_space=pltpu.SMEM)] * len(smem)
            + [pl.BlockSpec(memory_space=pltpu.VMEM)] * len(gathered)
            + [pl.BlockSpec(memory_space=pl.ANY)] * len(weights)
            + moving_specs,
            out_specs=tuple(specs),
            scratch_shapes=held + [pltpu.VMEM((rows, width), F32)],
        ),
        out_shape=tuple(jax.ShapeDtypeStruct(shape, kind) for shape, kind in outs),
        cost_estimate=cost(rows, weights, 4 * order.shape[0]),
        input_output_aliases={before + i: o for i, o in reused},
        compiler_params=pltpu.CompilerParams(vmem_limit_bytes=limit)
        if limit
        else room(
            [(x.shape, x.dtype) for x in gathered]
            + 2 * [(shape, kind) for shape, (_, kind) in zip(sizes, outs)],
            held,
        ),
    )(order, *smem, *gathered, *weights, *moving)


def unwritten(outs):
    return pl.pallas_call(
        nothing_kernel,
        out_shape=tuple(jax.ShapeDtypeStruct(shape, kind) for shape, kind in outs),
        out_specs=tuple(pl.BlockSpec(memory_space=pl.ANY) for _ in outs),
    )()


def gather_dp(block, then=None):
    count = lax.axis_size("dp")
    if count == 1:
        return [block]
    swap = [(i, i ^ 1) for i in range(count)]
    mine = [block]
    for turn in range(1, count // 2):
        route = [(i, (i + 2 * turn) % count) for i in range(count)]
        mine.append(lax.ppermute(block, "dp", route))
    theirs = [lax.ppermute(block, "dp", swap)]
    if then is not None:
        mine, _ = lax.optimization_barrier((mine, then))
    theirs += [lax.ppermute(own, "dp", swap) for own in mine[1:]]
    return [x for pair in zip(mine, theirs) for x in pair]


def joined(chunks):
    size = len(chunks) // PIECES
    return [jnp.concatenate(chunks[i : i + size], axis=0) for i in range(0, len(chunks), size)]


def gathered_order():
    count = lax.axis_size("dp")
    place = lax.axis_index("dp")
    other = jnp.arange(count, dtype=jnp.int32)
    turn = (place // 2 - other // 2) % max(count // 2, 1)
    return (2 * turn + (place + other) % 2).astype(jnp.int32) if count > 1 else other


def on_device(states, target, lengths, qkv_weight, out_weight, up_weight, down_weight):
    layer_count = lax.axis_size("layer")
    device = lax.axis_index("layer")
    weights = (qkv_weight, out_weight, up_weight, down_weight)
    starts, goal = states[0, 0], target[0]
    rows, width = starts.shape
    hidden = up_weight.shape[2]
    part = rows // CHUNKS
    full = ((rows, width), F32)
    piece = ((part, width), F32)
    saved = (((rows, 3 * width), BF), ((HEADS, rows, rows), BF), ((rows, hidden), BF))
    sizes = jnp.concatenate(gather_dp(lengths))
    both, first_layer = (0, 1), (0,)
    order = gathered_order()
    count = order.shape[0]
    is_first = (device == 0).astype(jnp.int32).reshape(1)
    is_last = (device == layer_count - 1).astype(jnp.int32).reshape(1)

    (first_end,) = call(relax_kernel, (full,), (lengths,), weights, both, (starts,), rows, 2)
    received = lax.ppermute(
        first_end, "layer", [(i, i + 1) for i in range(layer_count - 1)]
    )
    received, sizes = lax.optimization_barrier((received, sizes))
    got = call(
        fine_kernel, (piece,) * (4 * CHUNKS), (lengths, is_first), weights, both,
        (starts, received), rows, 2,
    )
    corrected, middles, ends, defect = (
        list(got[i * CHUNKS : (i + 1) * CHUNKS]) for i in range(4)
    )
    stores = [jnp.zeros((c * part, 2 * width), BF) for c in range(1, CHUNKS)]
    for block in range(2, layer_count):
        incoming = [lax.ppermute(ends[c], "layer", [(block - 1, block)]) for c in range(CHUNKS)]
        for c in range(CHUNKS):
            outs = (piece, piece, piece)
            kept = (corrected[c], middles[c], ends[c])
            if c < CHUNKS - 1:
                outs += (((((c + 1) * part), 2 * width), BF),)
                kept += (stores[c],)
            old = () if c == 0 else (stores[c - 1],)
            got = lax.cond(
                device == block,
                functools.partial(
                    call, functools.partial(coarse_kernel, c), outs, (lengths,), weights,
                    first_layer, (incoming[c], defect[c], *old), part,
                ),
                lambda kept=kept: kept,
            )
            corrected[c], middles[c], ends[c] = got[0:3]
            if c < CHUNKS - 1:
                stores[c] = got[3]
    chunks = corrected
    *kept, guess, turned, corrected, middles, ends = call(
        turn_kernel, (*saved, *saved, full, full, full, full, full), (lengths,), weights, both,
        (*corrected, *middles, *ends, goal), rows, 6,
    )
    even_saved = kept[0:3]
    received = lax.ppermute(
        turned, "layer", [(i + 1, i) for i in range(layer_count - 1)]
    )
    linear_outs = [
        ((count, rows, width), F32, (None, rows, width), lambda i, order: (i, 0, 0))
    ] * 2 + [
        ((2, count, *shape), kind, (2, None, *shape), lambda i, order, n=len(shape): (0, i) + (0,) * n)
        for shape, kind in saved
    ]
    linear_outs += [
        ((2, columns, count * rows), BF, (2, columns, rows), lambda i, order: (0, 0, i))
        for columns in (width, width, hidden)
    ]
    gathered = [gather_dp(piece, turned) for piece in joined(chunks)]
    every = [piece[i] for i in range(count) for piece in gathered]

    def all_linear():
        return tuple(
            call_each(
                all_linear_kernel, linear_outs, order, (sizes,), every, weights
            )
        )

    linear = lax.cond(device < layer_count - 2, all_linear, lambda: tuple(unwritten([out[0:2] for out in linear_outs])))
    received, linear = lax.optimization_barrier((received, linear))
    got = call(
        back_kernel, (piece,) * (2 * CHUNKS), (is_last,), weights, both,
        (guess, received, corrected, middles, *kept), rows, 4, WHOLE_LIMIT,
    )
    relaxed, fine = got[0:CHUNKS], got[CHUNKS:]
    adjoint_ends, adjoint_out = list(relaxed), list(fine)
    carried = [jnp.zeros((c * part, 2 * width), F32) for c in range(1, CHUNKS)]
    for block in range(layer_count - 3, -1, -1):
        incoming = [
            lax.ppermute(adjoint_out[c], "layer", [(block + 1, block)])
            for c in range(CHUNKS - 1, -1, -1)
        ][::-1]
        if block == 0:
            adjoint_ends = [
                jnp.where(device == 0, new, old) for new, old in zip(incoming, adjoint_ends)
            ]
            gathered = [gather_dp(piece) for piece in joined(adjoint_ends)[::-1]][::-1]
            adjoint_out = lax.cond(
                device == 0,
                functools.partial(
                    call, first_block_kernel, (piece,) * CHUNKS, (), weights, first_layer,
                    (*incoming, *relaxed, *fine, corrected, *even_saved), rows, 2,
                ),
                lambda adjoint_out=adjoint_out: tuple(adjoint_out),
            )
            break
        for c in range(CHUNKS - 1, -1, -1):
            outs = (piece, piece)
            old = (adjoint_ends[c], adjoint_out[c])
            if c > 0:
                outs += (((c * part, 2 * width), F32),)
                old += (carried[c - 1],)
            later = () if c == CHUNKS - 1 else (carried[c],)
            got = lax.cond(
                device == block,
                functools.partial(
                    call, functools.partial(adjoint_kernel, c), outs, (), weights,
                    first_layer, (incoming[c], relaxed[c], fine[c], corrected, *even_saved, *later),
                    part, 2,
                ),
                lambda old=old: old,
            )
            adjoint_ends[c], adjoint_out[c] = got[0:2]
            if c > 0:
                carried[c - 1] = got[2]
    linear, adjoint_out = lax.optimization_barrier((linear, adjoint_out))
    linear = lax.cond(device < layer_count - 2, lambda: linear, all_linear)
    every_adjoint = [piece[i] for i in range(count) for piece in gathered]
    moving = [(array, *out[2:4]) for array, out in zip(linear[0:5], linear_outs)]
    rights = [linear_outs[2], linear_outs[4]]
    rights += [
        ((2, count, rows, width), BF, (2, None, rows, width), lambda i, order: (0, i, 0, 0))
    ]
    got = call_each(
        all_back_kernel, rights, order, (), every_adjoint, weights, moving, WHOLE_LIMIT,
        ((2, 0), (4, 1)),
    )
    results = gradients(linear[5:8], got, weights)
    adjoint_out = jnp.concatenate(adjoint_out, axis=0)
    return (ends[None, None], adjoint_out[None, None], *results)


def solution(mesh):
    in_specs = (
        P("layer", "dp", None, None),
        P("dp", None, None),
        P("dp"),
        P("layer", None, None),
        P("layer", None, None),
        P("layer", None, None),
        P("layer", None, None),
    )
    out_specs = (
        P("layer", "dp", None, None),
        P("layer", "dp", None, None),
        P("layer", None, None),
        P("layer", None, None),
        P("layer", None, None),
        P("layer", None, None),
    )
    return jax.shard_map(
        on_device, mesh=mesh, in_specs=in_specs, out_specs=out_specs, check_vma=False
    )
```

```python
import functools
import math

import jax
import jax.numpy as jnp
from jax import lax
from jax.experimental import pallas as pl
from jax.experimental.pallas import tpu as pltpu
from jax.sharding import PartitionSpec as P

HEADS = 8
STEP = 0.125
CHUNKS = 2
PAIR = 128
TILE = 512
PIECES = 2
WHOLE_LIMIT = 60 * 1024 * 1024

BF = jnp.bfloat16
F32 = jnp.float32
NN = ((1,), (0,))
NT = ((1,), (1,))
TN = ((0,), (0,))
GELU_A = math.sqrt(2.0 / math.pi)
GELU_B = 0.044715


def dot(a, b, dims=NN):
    return lax.dot_general(a, b, (dims, ((), ())), preferred_element_type=F32)


def norm_scale(u):
    return lax.rsqrt(jnp.mean(u * u, axis=-1, keepdims=True) + 1e-06)


def half_masks(value):
    lane = lax.broadcasted_iota(jnp.int32, (1, PAIR), 1)
    first = jnp.where(lane < PAIR // 2, value, 0.0).astype(BF)
    second = jnp.where(lane < PAIR // 2, 0.0, value).astype(BF)
    return (first, second)


def join(pair):
    lane = lax.broadcasted_iota(jnp.int32, pair[0].shape, 1)
    return jnp.where(lane < PAIR // 2, pair[0], pair[1])


def gelu_parts(x):
    inner = jnp.tanh(GELU_A * (x + GELU_B * (x * x * x)))
    return 0.5 * (1.0 + inner), inner


def at(i, size, base=0):
    return slice(base + i * size, base + (i + 1) * size)


def loop(count, body):
    for i in range(count):
        body(i)


class Layer:
    def __init__(self, index, sources, targets, sems, when=None):
        self.index, self.sources, self.targets, self.sems = index, sources, targets, sems
        self.when, self.waiting = when, set()

    def copy(self, i):
        source = self.sources[i].at[self.index]
        return pltpu.make_async_copy(source, self.targets[i], self.sems.at[i])

    def start(self, order):
        if self.when is None:
            for i in order:
                self.copy(i).start()
            self.waiting = set(order)

    def get(self, i):
        if i in self.waiting:
            self.copy(i).wait()
            self.waiting.remove(i)
        return self.targets[i]


def fetch(layers, when):
    @pl.when(when)
    def _():
        for layer in layers:
            for i in range(len(layer.targets)):
                layer.copy(i).start()
        for layer in layers:
            for i in range(len(layer.targets)):
                layer.copy(i).wait()


QKV, OUT, UP, DOWN = range(4)
FORWARD = (QKV, UP, OUT, DOWN)
BACKWARD = (OUT, DOWN, QKV, UP)


def attention_sides(packed, pair, width):
    cols = pair * PAIR
    return [packed[:, base + cols : base + cols + PAIR] for base in (0, width, 2 * width)]


def forward_rows(u, layer, length, row0=0, old=None, whole_rows=0):
    rows, width = u.shape
    head = width // HEADS
    normed = (u * norm_scale(u)).astype(BF)
    packed = dot(normed, layer.get(QKV)[...]).astype(BF)
    own = packed[:, width:]
    both = own if old is None else jnp.concatenate([old, own], axis=0)
    spare = whole_rows - both.shape[0]
    if spare > 0:
        both = jnp.concatenate([both, *([own] * (spare // rows))], axis=0)
    shape = (rows, both.shape[0])
    key_pos = lax.broadcasted_iota(jnp.int32, shape, 1)
    query_pos = lax.broadcasted_iota(jnp.int32, shape, 0) + row0
    seen = (key_pos <= query_pos) & (key_pos < length)
    masks = half_masks(head**-0.5)
    parts = []
    for pair in range(width // PAIR):
        cols = slice(pair * PAIR, (pair + 1) * PAIR)
        keys, vals = both[:, cols], both[:, width + pair * PAIR : width + (pair + 1) * PAIR]
        outs = []
        for mask in masks:
            scores = dot(packed[:, cols] * mask, keys, NT)
            scores = jnp.where(seen, scores, -jnp.inf)
            weight = jnp.exp(scores - jnp.max(scores, axis=-1, keepdims=True))
            probs = (weight * (1.0 / jnp.sum(weight, axis=-1, keepdims=True))).astype(BF)
            outs.append(dot(probs, vals))
        parts.append(join(outs).astype(BF))
    context = jnp.concatenate(parts, axis=1)
    up = dot(normed, layer.get(UP)[...])
    hidden = (up * gelu_parts(up)[0]).astype(BF)
    return dot(context, layer.get(OUT)[...]) + dot(hidden, layer.get(DOWN)[...]), own


def linearize_rows(u, layer, length, saved, factors=None):
    packed_ref, probs_ref, slope_ref = saved
    rows, width = u.shape
    head = width // HEADS
    wide = u * norm_scale(u)
    normed = wide.astype(BF)
    packed = dot(normed, layer.get(QKV)[...]).astype(BF)
    packed_ref[...] = packed
    key_pos = lax.broadcasted_iota(jnp.int32, (rows, rows), 0)
    query_pos = lax.broadcasted_iota(jnp.int32, (rows, rows), 1)
    seen = (key_pos <= query_pos) & (key_pos < length)
    masks = half_masks(head**-0.5)
    parts = []
    for pair in range(width // PAIR):
        queries, keys, vals = attention_sides(packed, pair, width)
        outs = []
        for half, mask in enumerate(masks):
            scores = dot(keys, queries * mask, NT)
            scores = jnp.where(seen, scores, -jnp.inf)
            weight = jnp.exp(scores - jnp.max(scores, axis=0, keepdims=True))
            probs = (weight * (1.0 / jnp.sum(weight, axis=0, keepdims=True))).astype(BF)
            probs_ref[2 * pair + half] = probs
            if factors is not None:
                outs.append(dot(probs, vals, TN))
        if factors is not None:
            parts.append(join(outs))
    up = dot(normed, layer.get(UP)[...])
    gate, inner = gelu_parts(up)
    rise = GELU_A + 3.0 * GELU_A * GELU_B * up * up
    slope_ref[...] = (gate + 0.5 * up * (1.0 - inner * inner) * rise).astype(BF)
    if factors is None:
        return None
    context, hidden = jnp.concatenate(parts, axis=1), up * gate
    for ref, value in zip(factors, (wide, context, hidden)):
        ref[...] = value.T.astype(BF)
    return context.astype(BF), hidden.astype(BF)


def backward_rows(ct, u, layer, saved, row0=0, later=None, earlier=None, right=None):
    width = ct.shape[1]
    low = ct.astype(BF)
    d_context = dot(low, layer.get(OUT)[...], NT).astype(BF)
    d_hidden = dot(low, layer.get(DOWN)[...], NT)
    rows = ct.shape[0] // len(saved)
    d_ups, d_packs = [], []
    for i, one in enumerate(saved):
        part = slice(i * rows, (i + 1) * rows)
        slope = one[2][row0 : row0 + rows, :].astype(F32)
        d_ups.append((d_hidden[part] * slope).astype(BF))
        d_packs.append(backward_attention(d_context[part], one, row0, later, earlier))
    d_up, d_packed = jnp.concatenate(d_ups, axis=0), jnp.concatenate(d_packs, axis=0)
    if right is not None:
        for ref, value in zip(right, (d_packed, d_up, low)):
            ref[...] = value
    d_normed = dot(d_packed, layer.get(QKV)[...], NT) + dot(d_up, layer.get(UP)[...], NT)
    scale = norm_scale(u)
    unit = u * scale
    return scale * (d_normed - unit * jnp.mean(unit * d_normed, axis=-1, keepdims=True))


def backward_attention(d_context, saved, row0, later, earlier):
    packed_ref, probs_ref, _ = saved
    rows, width = d_context.shape
    head = width // HEADS
    end = row0 + rows
    ones = half_masks(1.0)
    d_queries, d_sides = [], [[], []]
    for pair in range(width // PAIR):
        lo = pair * PAIR
        queries = packed_ref[row0:end, lo : lo + PAIR]
        keys = packed_ref[:, width + lo : width + lo + PAIR]
        vals = packed_ref[:, 2 * width + lo : 2 * width + lo + PAIR]
        d_pair = d_context[:, lo : lo + PAIR]
        dq, dk, dv = [], [], []
        for half, mask in enumerate(ones):
            probs = probs_ref[2 * pair + half, :, row0:end]
            wide = probs.astype(F32)
            d_probs = dot(vals, d_pair * mask, NT)
            mean = jnp.sum(wide * d_probs, axis=0, keepdims=True)
            d_scores = (wide * (d_probs - mean) * head**-0.5).astype(BF)
            dq.append(dot(d_scores, keys, TN))
            dk.append(dot(d_scores, queries))
            dv.append(dot(probs, d_pair))
        d_queries.append(join(dq).astype(BF))
        for side, value in enumerate((join(dk)[0:end], join(dv)[0:end])):
            base = side * width + lo
            if later is not None:
                value = value + later[0:end, base : base + PAIR]
            d_sides[side].append(value[row0:end].astype(BF))
            if earlier is not None:
                earlier[:, base : base + PAIR] = value[0:row0]
    return jnp.concatenate([*d_queries, *d_sides[0], *d_sides[1]], axis=1)


def whole(refs):
    return jnp.concatenate([ref[...] for ref in refs], axis=0)


def split(value, refs):
    rows = refs[0].shape[0]
    for c, ref in enumerate(refs):
        ref[...] = value[c * rows : (c + 1) * rows]


def relax_kernel(smem, ins, outs, layers):
    even, odd = layers
    even.start(FORWARD)
    odd.start(FORWARD)
    length = smem[0][0]
    state = ins[0][...]
    state = state + STEP * forward_rows(state, even, length)[0]
    outs[0][...] = state + STEP * forward_rows(state, odd, length)[0]


def fine_kernel(smem, ins, outs, layers):
    even, odd = layers
    even.start(FORWARD)
    odd.start(FORWARD)
    length = smem[0][0]
    state = jnp.where(smem[1][0] == 1, ins[0][...], ins[1][...])
    value = forward_rows(state, even, length)[0]
    middle = state + STEP * value
    split(state, outs[0:CHUNKS])
    split(middle, outs[CHUNKS : 2 * CHUNKS])
    coarse = state + 2.0 * STEP * value
    end = middle + STEP * forward_rows(middle, odd, length)[0]
    split(end, outs[2 * CHUNKS : 3 * CHUNKS])
    split(end - coarse, outs[3 * CHUNKS : 4 * CHUNKS])


def coarse_kernel(chunk, smem, ins, outs, layers):
    (even,) = layers
    even.start(FORWARD)
    state, defect = ins[0:2]
    old = ins[2][...] if chunk > 0 else None
    current = state[...]
    rows = current.shape[0]
    value, own = forward_rows(
        current, even, smem[0][0], chunk * rows, old, CHUNKS * rows
    )
    outs[0][...] = current
    outs[1][...] = current + STEP * value
    outs[2][...] = current + 2.0 * STEP * value + defect[...]
    if len(outs) > 3:
        if chunk > 0:
            outs[3][0 : chunk * rows, :] = old
        outs[3][chunk * rows :, :] = own


def turn_kernel(smem, ins, outs, layers):
    even, odd = layers
    odd.start(FORWARD)
    even.start(FORWARD)
    length = smem[0][0]
    corrected, middles, ends = (whole(ins[i * CHUNKS : (i + 1) * CHUNKS]) for i in range(3))
    target = ins[3 * CHUNKS]
    even_saved, odd_saved = outs[0:3], outs[3:6]
    guess_ref, out, corrected_ref, middles_ref, ends_ref = outs[6:]
    corrected_ref[...] = corrected
    middles_ref[...] = middles
    ends_ref[...] = ends
    position = lax.broadcasted_iota(jnp.int32, ends.shape, 0)
    guess_ref[...] = jnp.where(position < length, ends - target[...], 0.0)
    linearize_rows(middles, odd, length, odd_saved)
    linearize_rows(corrected, even, length, even_saved)
    state = guess_ref[...]
    state = state + STEP * backward_rows(state, middles, odd, [odd_saved])
    out[...] = state + STEP * backward_rows(state, corrected, even, [even_saved])


def back_kernel(smem, ins, outs, layers):
    even, odd = layers
    odd.start(BACKWARD)
    even.start(BACKWARD)
    guess, received, corrected, middles = ins[0:4]
    even_saved, odd_saved = ins[4:7], ins[7:10]
    state = jnp.where(smem[0][0] == 1, guess[...], received[...])
    split(state, outs[0:CHUNKS])
    state = state + STEP * backward_rows(state, middles[...], odd, [odd_saved])
    state = state + STEP * backward_rows(state, corrected[...], even, [even_saved])
    split(state, outs[CHUNKS : 2 * CHUNKS])


def adjoint_kernel(chunk, smem, ins, outs, layers):
    (even,) = layers
    even.start(BACKWARD)
    incoming, relaxed, fine, corrected = ins[0:4]
    saved = ins[4:7]
    later = ins[7] if chunk < CHUNKS - 1 else None
    rows = incoming.shape[0]
    current = incoming[...]
    gap = current - relaxed[...]
    state = corrected[chunk * rows : (chunk + 1) * rows, :]
    change = backward_rows(
        gap, state, even, [saved], chunk * rows, later, outs[2] if chunk > 0 else None
    )
    outs[0][...] = current
    outs[1][...] = fine[...] + (gap + 2.0 * STEP * change)


def first_block_kernel(smem, ins, outs, layers):
    del smem
    (even,) = layers
    even.start(BACKWARD)
    current, relaxed, fine = (whole(ins[i * CHUNKS : (i + 1) * CHUNKS]) for i in range(3))
    gap = current - relaxed
    change = backward_rows(gap, ins[3 * CHUNKS][...], even, [ins[3 * CHUNKS + 1 :]])
    split(fine + (gap + 2.0 * STEP * change), outs)


def pick(place, blocks, held):
    for i, group in enumerate(blocks):

        @pl.when(place == i)
        def _(group=group):
            first = 0
            for ref in group:
                held[first : first + ref.shape[0], :] = ref[...]
                first += ref.shape[0]


def all_linear_kernel(order, smem, ins, moving, outs, layers, held):
    del moving
    pick(
        order[pl.program_id(0)], [ins[i : i + PIECES] for i in range(0, len(ins), PIECES)], held
    )
    even, odd = layers
    corrected, middles = outs[0:2]
    even_saved, odd_saved = ([ref.at[i] for ref in outs[2:5]] for i in range(2))
    even_factors, odd_factors = ([ref.at[i] for ref in outs[5:8]] for i in range(2))
    length = smem[0][order[pl.program_id(0)]]
    state = held[...]
    corrected[...] = state
    context, hidden = linearize_rows(state, even, length, even_saved, even_factors)
    value = dot(context, even.get(OUT)[...]) + dot(hidden, even.get(DOWN)[...])
    middle = state + STEP * value
    middles[...] = middle
    linearize_rows(middle, odd, length, odd_saved, odd_factors)


def all_back_kernel(order, smem, ins, moving, outs, layers, held):
    del smem
    blocks = [ins[i : i + PIECES] for i in range(0, len(ins), PIECES)]
    pick(order[pl.program_id(0)], blocks, held)
    even, odd = layers
    corrected, middles = (ref[...] for ref in moving[0:2])
    even_saved, odd_saved = ([[ref.at[i] for ref in moving[2:5]]] for i in range(2))
    even_right, odd_right = ([ref.at[i] for ref in outs] for i in range(2))
    state = held[...]
    change = backward_rows(state, middles, odd, odd_saved, right=odd_right)
    state = state + STEP * change
    backward_rows(state, corrected, even, even_saved, right=even_right)


def gradient_kernel(count, steps, *refs):
    (normed, context, hidden), (d_packed, d_up, low) = refs[0:3], refs[3:6]
    outs, sums, sems = refs[6:10], refs[10:14], refs[14]
    layer, k = pl.program_id(0), pl.program_id(1)
    pairs = ((normed, d_packed), (context, low), (normed, d_up), (hidden, low))
    tile = TILE // 2
    total = jnp.zeros((1, tile), F32)
    for (left, right), held in zip(pairs, sums):
        depth = left.shape[1]

        def step(i, total, left=left, right=right, held=held, depth=depth):
            cols = pl.ds(pl.multiple_of(i * tile, tile), tile)
            value = STEP * dot(left[...], right[:, :, cols].reshape(depth, tile))
            if steps > 1:
                value = jnp.where(k == 0, value, held[layer, :, cols] + value)
            held[layer, :, cols] = value
            return total + jnp.sum(value * value, axis=0, keepdims=True)

        total = lax.fori_loop(0, right.shape[2] // tile, step, total)

    def copies(index):
        return [
            pltpu.make_async_copy(held.at[index], out.at[index], sems.at[i])
            for i, (held, out) in enumerate(zip(sums, outs))
        ]

    @pl.when(k == pl.num_programs(1) - 1)
    def _():
        square = jnp.sum(total, axis=1, keepdims=True)
        inverse = 1.0 / jnp.sqrt(square / count + 1e-06)
        for held in sums:
            held[layer] = held[layer] * inverse

        @pl.when(layer == 0)
        def _():
            for copy in copies(0):
                copy.start()

        @pl.when(layer == 1)
        def _():
            for copy in copies(0):
                copy.wait()
            for copy in copies(1):
                copy.start()
            for copy in copies(1):
                copy.wait()


def gradients(lefts, rights, weights):
    _, count, rows, _ = rights[0].shape
    group = min(count, 4)
    sizes = [w.shape[1:] for w in weights]
    blocks = [(2, x.shape[1] * group * rows) for x in lefts]
    blocks += [(2, group * rows * x.shape[3]) for x in rights]
    return pl.pallas_call(
        functools.partial(
            gradient_kernel, float(sum(math.prod(size) for size in sizes)), count // group
        ),
        grid=(2, count // group),
        in_specs=[
            pl.BlockSpec((None, x.shape[1], group * rows), lambda i, k: (i, 0, k)) for x in lefts
        ]
        + [
            pl.BlockSpec((None, group, rows, x.shape[3]), lambda i, k: (i, k, 0, 0))
            for x in rights
        ],
        out_specs=tuple(pl.BlockSpec(memory_space=pl.ANY) for _ in sizes),
        out_shape=tuple(jax.ShapeDtypeStruct((2, *size), F32) for size in sizes),
        scratch_shapes=[pltpu.VMEM((2, *size), F32) for size in sizes]
        + [pltpu.SemaphoreType.DMA((len(sizes),))],
        cost_estimate=pl.CostEstimate(
            flops=4 * count * rows * sum(math.prod(size) for size in sizes),
            bytes_accessed=0,
            transcendentals=0,
        ),
        compiler_params=room(
            [(block, BF) for block in blocks] + [((2, *size), F32) for size in sizes], [None]
        ),
    )(*lefts, *rights)


def nothing_kernel(*refs):
    del refs


def scratch(weights, layers):
    shapes = [pltpu.VMEM(w.shape[1:], w.dtype) for _ in layers for w in weights]
    return shapes + [pltpu.SemaphoreType.DMA((len(layers), len(weights)))]


def room(shapes, scratches):
    total = sum(math.prod(shape) * jnp.dtype(kind).itemsize for shape, kind in shapes)
    for item in scratches[:-1]:
        total += math.prod(item.shape) * jnp.dtype(item.dtype).itemsize
    return pltpu.CompilerParams(vmem_limit_bytes=int(total * 1.1) + 10 * 1024 * 1024)


def unpack(refs, sources, layers, when=None):
    count = len(sources)
    refs, sems = refs[:-1], refs[-1]
    return [
        Layer(index, sources, refs[i * count : (i + 1) * count], sems.at[i], when)
        for i, index in enumerate(layers)
    ]


def cost(rows, weights, layers):
    flops = 2 * rows * sum(math.prod(w.shape[1:]) for w in weights) * layers
    return pl.CostEstimate(flops=6 * flops, bytes_accessed=0, transcendentals=0)


def call(kernel, outs, smem, weights, layers, ins, rows, passes=1, limit=None):
    counts = [len(smem), len(ins), len(weights), len(outs)]
    held = scratch(weights, layers)

    def body(*refs):
        cuts = [sum(counts[:i]) for i in range(5)]
        parts = [refs[cuts[i] : cuts[i + 1]] for i in range(4)]
        kernel(parts[0], parts[1], parts[3], unpack(refs[cuts[4] :], parts[2], layers))

    return pl.pallas_call(
        body,
        out_shape=tuple(jax.ShapeDtypeStruct(shape, kind) for shape, kind in outs),
        in_specs=[pl.BlockSpec(memory_space=pltpu.SMEM)] * len(smem)
        + [pl.BlockSpec(memory_space=pltpu.VMEM)] * len(ins)
        + [pl.BlockSpec(memory_space=pl.ANY)] * len(weights),
        out_specs=tuple(pl.BlockSpec(memory_space=pltpu.VMEM) for _ in outs),
        scratch_shapes=held,
        cost_estimate=cost(rows, weights, passes),
        compiler_params=pltpu.CompilerParams(vmem_limit_bytes=limit)
        if limit
        else room([*((x.shape, x.dtype) for x in ins), *outs], held),
    )(*smem, *ins, *weights)


def call_each(kernel, outs, order, smem, gathered, weights, moving=(), limit=None, reused=()):
    rows = sum(x.shape[0] for x in gathered) // order.shape[0]
    width = gathered[0].shape[1]
    specs = [pl.BlockSpec(shape, index) for _, _, shape, index in outs]
    sizes = [[size for size in shape if size] for _, _, shape, _ in outs]
    outs = [(shape, kind) for shape, kind, _, _ in outs]
    held = scratch(weights, (0, 1))
    counts = [len(smem), len(gathered), len(weights), len(moving), len(outs)]

    before = 1 + len(smem) + len(gathered) + len(weights)
    moving_specs = [pl.BlockSpec(shape, index) for _, shape, index in moving]
    moving = [array for array, _, _ in moving]

    def body(order_ref, *refs):
        cuts = [sum(counts[:i]) for i in range(6)]
        parts = [refs[cuts[i] : cuts[i + 1]] for i in range(5)]
        first = pl.program_id(0) == 0
        layers = unpack(refs[cuts[5] : -1], parts[2], (0, 1), first)
        fetch(layers, first)
        kernel(order_ref, parts[0], parts[1], parts[3], parts[4], layers, refs[-1])

    return pl.pallas_call(
        body,
        grid_spec=pltpu.PrefetchScalarGridSpec(
            num_scalar_prefetch=1,
            grid=order.shape,
            in_specs=[pl.BlockSpec(memory_space=pltpu.SMEM)] * len(smem)
            + [pl.BlockSpec(memory_space=pltpu.VMEM)] * len(gathered)
            + [pl.BlockSpec(memory_space=pl.ANY)] * len(weights)
            + moving_specs,
            out_specs=tuple(specs),
            scratch_shapes=held + [pltpu.VMEM((rows, width), F32)],
        ),
        out_shape=tuple(jax.ShapeDtypeStruct(shape, kind) for shape, kind in outs),
        cost_estimate=cost(rows, weights, 4 * order.shape[0]),
        input_output_aliases={before + i: o for i, o in reused},
        compiler_params=pltpu.CompilerParams(vmem_limit_bytes=limit)
        if limit
        else room(
            [(x.shape, x.dtype) for x in gathered]
            + 2 * [(shape, kind) for shape, (_, kind) in zip(sizes, outs)],
            held,
        ),
    )(order, *smem, *gathered, *weights, *moving)


def unwritten(outs):
    return pl.pallas_call(
        nothing_kernel,
        out_shape=tuple(jax.ShapeDtypeStruct(shape, kind) for shape, kind in outs),
        out_specs=tuple(pl.BlockSpec(memory_space=pl.ANY) for _ in outs),
    )()


def gather_dp(block, then=None):
    count = lax.axis_size("dp")
    if count == 1:
        return [block]
    swap = [(i, i ^ 1) for i in range(count)]
    mine = [block]
    for turn in range(1, count // 2):
        route = [(i, (i + 2 * turn) % count) for i in range(count)]
        mine.append(lax.ppermute(block, "dp", route))
    theirs = [lax.ppermute(block, "dp", swap)]
    if then is not None:
        mine, _ = lax.optimization_barrier((mine, then))
    theirs += [lax.ppermute(own, "dp", swap) for own in mine[1:]]
    return [x for pair in zip(mine, theirs) for x in pair]


def joined(chunks):
    size = len(chunks) // PIECES
    return [jnp.concatenate(chunks[i : i + size], axis=0) for i in range(0, len(chunks), size)]


def gathered_order():
    count = lax.axis_size("dp")
    place = lax.axis_index("dp")
    other = jnp.arange(count, dtype=jnp.int32)
    turn = (place // 2 - other // 2) % max(count // 2, 1)
    return (2 * turn + (place + other) % 2).astype(jnp.int32) if count > 1 else other


def on_device(states, target, lengths, qkv_weight, out_weight, up_weight, down_weight):
    layer_count = lax.axis_size("layer")
    device = lax.axis_index("layer")
    weights = (qkv_weight, out_weight, up_weight, down_weight)
    starts, goal = states[0, 0], target[0]
    rows, width = starts.shape
    hidden = up_weight.shape[2]
    part = rows // CHUNKS
    full = ((rows, width), F32)
    piece = ((part, width), F32)
    saved = (((rows, 3 * width), BF), ((HEADS, rows, rows), BF), ((rows, hidden), BF))
    sizes = jnp.concatenate(gather_dp(lengths))
    both, first_layer = (0, 1), (0,)
    order = gathered_order()
    count = order.shape[0]
    is_first = (device == 0).astype(jnp.int32).reshape(1)
    is_last = (device == layer_count - 1).astype(jnp.int32).reshape(1)

    (first_end,) = call(relax_kernel, (full,), (lengths,), weights, both, (starts,), rows, 2)
    received = lax.ppermute(
        first_end, "layer", [(i, i + 1) for i in range(layer_count - 1)]
    )
    received, sizes = lax.optimization_barrier((received, sizes))
    got = call(
        fine_kernel, (piece,) * (4 * CHUNKS), (lengths, is_first), weights, both,
        (starts, received), rows, 2,
    )
    corrected, middles, ends, defect = (
        list(got[i * CHUNKS : (i + 1) * CHUNKS]) for i in range(4)
    )
    stores = [jnp.zeros((c * part, 2 * width), BF) for c in range(1, CHUNKS)]
    for block in range(2, layer_count):
        incoming = [lax.ppermute(ends[c], "layer", [(block - 1, block)]) for c in range(CHUNKS)]
        for c in range(CHUNKS):
            outs = (piece, piece, piece)
            kept = (corrected[c], middles[c], ends[c])
            if c < CHUNKS - 1:
                outs += (((((c + 1) * part), 2 * width), BF),)
                kept += (stores[c],)
            old = () if c == 0 else (stores[c - 1],)
            got = lax.cond(
                device == block,
                functools.partial(
                    call, functools.partial(coarse_kernel, c), outs, (lengths,), weights,
                    first_layer, (incoming[c], defect[c], *old), part,
                ),
                lambda kept=kept: kept,
            )
            corrected[c], middles[c], ends[c] = got[0:3]
            if c < CHUNKS - 1:
                stores[c] = got[3]
    chunks = corrected
    *kept, guess, turned, corrected, middles, ends = call(
        turn_kernel, (*saved, *saved, full, full, full, full, full), (lengths,), weights, both,
        (*corrected, *middles, *ends, goal), rows, 6,
    )
    even_saved = kept[0:3]
    received = lax.ppermute(
        turned, "layer", [(i + 1, i) for i in range(layer_count - 1)]
    )
    linear_outs = [
        ((count, rows, width), F32, (None, rows, width), lambda i, order: (i, 0, 0))
    ] * 2 + [
        ((2, count, *shape), kind, (2, None, *shape), lambda i, order, n=len(shape): (0, i) + (0,) * n)
        for shape, kind in saved
    ]
    linear_outs += [
        ((2, columns, count * rows), BF, (2, columns, rows), lambda i, order: (0, 0, i))
        for columns in (width, width, hidden)
    ]
    gathered = [gather_dp(piece, turned) for piece in joined(chunks)]
    every = [piece[i] for i in range(count) for piece in gathered]

    def all_linear():
        return tuple(
            call_each(
                all_linear_kernel, linear_outs, order, (sizes,), every, weights
            )
        )

    linear = lax.cond(device < layer_count - 2, all_linear, lambda: tuple(unwritten([out[0:2] for out in linear_outs])))
    received, linear = lax.optimization_barrier((received, linear))
    got = call(
        back_kernel, (piece,) * (2 * CHUNKS), (is_last,), weights, both,
        (guess, received, corrected, middles, *kept), rows, 4, WHOLE_LIMIT,
    )
    relaxed, fine = got[0:CHUNKS], got[CHUNKS:]
    adjoint_ends, adjoint_out = list(relaxed), list(fine)
    carried = [jnp.zeros((c * part, 2 * width), F32) for c in range(1, CHUNKS)]
    for block in range(layer_count - 3, -1, -1):
        incoming = [
            lax.ppermute(adjoint_out[c], "layer", [(block + 1, block)])
            for c in range(CHUNKS - 1, -1, -1)
        ][::-1]
        if block == 0:
            adjoint_ends = [
                jnp.where(device == 0, new, old) for new, old in zip(incoming, adjoint_ends)
            ]
            gathered = [gather_dp(piece) for piece in joined(adjoint_ends)[::-1]][::-1]
            adjoint_out = lax.cond(
                device == 0,
                functools.partial(
                    call, first_block_kernel, (piece,) * CHUNKS, (), weights, first_layer,
                    (*incoming, *relaxed, *fine, corrected, *even_saved), rows, 2,
                ),
                lambda adjoint_out=adjoint_out: tuple(adjoint_out),
            )
            break
        for c in range(CHUNKS - 1, -1, -1):
            outs = (piece, piece)
            old = (adjoint_ends[c], adjoint_out[c])
            if c > 0:
                outs += (((c * part, 2 * width), F32),)
                old += (carried[c - 1],)
            later = () if c == CHUNKS - 1 else (carried[c],)
            got = lax.cond(
                device == block,
                functools.partial(
                    call, functools.partial(adjoint_kernel, c), outs, (), weights,
                    first_layer, (incoming[c], relaxed[c], fine[c], corrected, *even_saved, *later),
                    part, 2,
                ),
                lambda old=old: old,
            )
            adjoint_ends[c], adjoint_out[c] = got[0:2]
            if c > 0:
                carried[c - 1] = got[2]
    linear, adjoint_out = lax.optimization_barrier((linear, adjoint_out))
    linear = lax.cond(device < layer_count - 2, lambda: linear, all_linear)
    every_adjoint = [piece[i] for i in range(count) for piece in gathered]
    moving = [(array, *out[2:4]) for array, out in zip(linear[0:5], linear_outs)]
    rights = [linear_outs[2], linear_outs[4]]
    rights += [
        ((2, count, rows, width), BF, (2, None, rows, width), lambda i, order: (0, i, 0, 0))
    ]
    got = call_each(
        all_back_kernel, rights, order, (), every_adjoint, weights, moving, WHOLE_LIMIT,
        ((2, 0), (4, 1)),
    )
    results = gradients(linear[5:8], got, weights)
    adjoint_out = jnp.concatenate(adjoint_out, axis=0)
    return (ends[None, None], adjoint_out[None, None], *results)


def solution(mesh):
    in_specs = (
        P("layer", "dp", None, None),
        P("dp", None, None),
        P("dp"),
        P("layer", None, None),
        P("layer", None, None),
        P("layer", None, None),
        P("layer", None, None),
    )
    out_specs = (
        P("layer", "dp", None, None),
        P("layer", "dp", None, None),
        P("layer", None, None),
        P("layer", None, None),
        P("layer", None, None),
        P("layer", None, None),
    )
    return jax.shard_map(
        on_device, mesh=mesh, in_specs=in_specs, out_specs=out_specs, check_vma=False
    )
```

```python
import functools
import math

import jax
import jax.numpy as jnp
from jax import lax
from jax.experimental import pallas as pl
from jax.experimental.pallas import tpu as pltpu
from jax.sharding import PartitionSpec as P

HEADS = 8
STEP = 0.125
CHUNKS = 2
PAIR = 128
TILE = 512
PIECES = 2
WHOLE_LIMIT = 60 * 1024 * 1024

BF = jnp.bfloat16
F32 = jnp.float32
NN = ((1,), (0,))
NT = ((1,), (1,))
TN = ((0,), (0,))
GELU_A = math.sqrt(2.0 / math.pi)
GELU_B = 0.044715


def dot(a, b, dims=NN):
    return lax.dot_general(a, b, (dims, ((), ())), preferred_element_type=F32)


def norm_scale(u):
    return lax.rsqrt(jnp.mean(u * u, axis=-1, keepdims=True) + 1e-06)


def half_masks(value):
    lane = lax.broadcasted_iota(jnp.int32, (1, PAIR), 1)
    first = jnp.where(lane < PAIR // 2, value, 0.0).astype(BF)
    second = jnp.where(lane < PAIR // 2, 0.0, value).astype(BF)
    return (first, second)


def join(pair):
    lane = lax.broadcasted_iota(jnp.int32, pair[0].shape, 1)
    return jnp.where(lane < PAIR // 2, pair[0], pair[1])


def gelu_parts(x):
    inner = jnp.tanh(GELU_A * (x + GELU_B * (x * x * x)))
    return 0.5 * (1.0 + inner), inner


def at(i, size, base=0):
    return slice(base + i * size, base + (i + 1) * size)


def loop(count, body):
    for i in range(count):
        body(i)


class Layer:
    def __init__(self, index, sources, targets, sems, when=None):
        self.index, self.sources, self.targets, self.sems = index, sources, targets, sems
        self.when, self.waiting = when, set()

    def copy(self, i):
        source = self.sources[i].at[self.index]
        return pltpu.make_async_copy(source, self.targets[i], self.sems.at[i])

    def start(self, order):
        if self.when is None:
            for i in order:
                self.copy(i).start()
            self.waiting = set(order)

    def get(self, i):
        if i in self.waiting:
            self.copy(i).wait()
            self.waiting.remove(i)
        return self.targets[i]


def fetch(layers):
    @pl.when(layers[0].when)
    def _():
        for layer in layers:
            for i in range(len(layer.targets)):
                layer.copy(i).start()
        for i in range(len(layers[0].targets)):
            layers[0].copy(i).wait()


def settle(layer):
    @pl.when(layer.when)
    def _():
        for i in range(len(layer.targets)):
            layer.copy(i).wait()


QKV, OUT, UP, DOWN = range(4)
FORWARD = (QKV, UP, OUT, DOWN)
BACKWARD = (OUT, DOWN, QKV, UP)


def attention_sides(packed, pair, width):
    cols = pair * PAIR
    return [packed[:, base + cols : base + cols + PAIR] for base in (0, width, 2 * width)]


def forward_rows(u, layer, length, row0=0, old=None, whole_rows=0):
    rows, width = u.shape
    head = width // HEADS
    normed = (u * norm_scale(u)).astype(BF)
    packed = dot(normed, layer.get(QKV)[...]).astype(BF)
    own = packed[:, width:]
    both = own if old is None else jnp.concatenate([old, own], axis=0)
    spare = whole_rows - both.shape[0]
    if spare > 0:
        both = jnp.concatenate([both, *([own] * (spare // rows))], axis=0)
    shape = (rows, both.shape[0])
    key_pos = lax.broadcasted_iota(jnp.int32, shape, 1)
    query_pos = lax.broadcasted_iota(jnp.int32, shape, 0) + row0
    seen = (key_pos <= query_pos) & (key_pos < length)
    masks = half_masks(head**-0.5)
    parts = []
    for pair in range(width // PAIR):
        cols = slice(pair * PAIR, (pair + 1) * PAIR)
        keys, vals = both[:, cols], both[:, width + pair * PAIR : width + (pair + 1) * PAIR]
        outs = []
        for mask in masks:
            scores = dot(packed[:, cols] * mask, keys, NT)
            scores = jnp.where(seen, scores, -jnp.inf)
            weight = jnp.exp(scores - jnp.max(scores, axis=-1, keepdims=True))
            probs = (weight * (1.0 / jnp.sum(weight, axis=-1, keepdims=True))).astype(BF)
            outs.append(dot(probs, vals))
        parts.append(join(outs).astype(BF))
    context = jnp.concatenate(parts, axis=1)
    up = dot(normed, layer.get(UP)[...])
    hidden = (up * gelu_parts(up)[0]).astype(BF)
    return dot(context, layer.get(OUT)[...]) + dot(hidden, layer.get(DOWN)[...]), own


def linearize_rows(u, layer, length, saved, factors=None):
    packed_ref, probs_ref, slope_ref = saved
    rows, width = u.shape
    head = width // HEADS
    wide = u * norm_scale(u)
    normed = wide.astype(BF)
    packed = dot(normed, layer.get(QKV)[...]).astype(BF)
    packed_ref[...] = packed
    key_pos = lax.broadcasted_iota(jnp.int32, (rows, rows), 0)
    query_pos = lax.broadcasted_iota(jnp.int32, (rows, rows), 1)
    seen = (key_pos <= query_pos) & (key_pos < length)
    masks = half_masks(head**-0.5)
    parts = []
    for pair in range(width // PAIR):
        queries, keys, vals = attention_sides(packed, pair, width)
        outs = []
        for half, mask in enumerate(masks):
            scores = dot(keys, queries * mask, NT)
            scores = jnp.where(seen, scores, -jnp.inf)
            weight = jnp.exp(scores - jnp.max(scores, axis=0, keepdims=True))
            probs = (weight * (1.0 / jnp.sum(weight, axis=0, keepdims=True))).astype(BF)
            probs_ref[2 * pair + half] = probs
            if factors is not None:
                outs.append(dot(probs, vals, TN))
        if factors is not None:
            parts.append(join(outs))
    up = dot(normed, layer.get(UP)[...])
    gate, inner = gelu_parts(up)
    rise = GELU_A + 3.0 * GELU_A * GELU_B * up * up
    slope_ref[...] = (gate + 0.5 * up * (1.0 - inner * inner) * rise).astype(BF)
    if factors is None:
        return None
    context, hidden = jnp.concatenate(parts, axis=1), up * gate
    for ref, value in zip(factors, (wide, context, hidden)):
        ref[...] = value.T.astype(BF)
    return context.astype(BF), hidden.astype(BF)


def backward_rows(ct, u, layer, saved, row0=0, later=None, earlier=None, right=None):
    width = ct.shape[1]
    low = ct.astype(BF)
    d_context = dot(low, layer.get(OUT)[...], NT).astype(BF)
    d_hidden = dot(low, layer.get(DOWN)[...], NT)
    rows = ct.shape[0] // len(saved)
    d_ups, d_packs = [], []
    for i, one in enumerate(saved):
        part = slice(i * rows, (i + 1) * rows)
        slope = one[2][row0 : row0 + rows, :].astype(F32)
        d_ups.append((d_hidden[part] * slope).astype(BF))
        d_packs.append(backward_attention(d_context[part], one, row0, later, earlier))
    d_up, d_packed = jnp.concatenate(d_ups, axis=0), jnp.concatenate(d_packs, axis=0)
    if right is not None:
        for ref, value in zip(right, (d_packed, d_up, low)):
            ref[...] = value
    d_normed = dot(d_packed, layer.get(QKV)[...], NT) + dot(d_up, layer.get(UP)[...], NT)
    scale = norm_scale(u)
    unit = u * scale
    return scale * (d_normed - unit * jnp.mean(unit * d_normed, axis=-1, keepdims=True))


def backward_attention(d_context, saved, row0, later, earlier):
    packed_ref, probs_ref, _ = saved
    rows, width = d_context.shape
    head = width // HEADS
    end = row0 + rows
    ones = half_masks(1.0)
    d_queries, d_sides = [], [[], []]
    for pair in range(width // PAIR):
        lo = pair * PAIR
        queries = packed_ref[row0:end, lo : lo + PAIR]
        keys = packed_ref[:, width + lo : width + lo + PAIR]
        vals = packed_ref[:, 2 * width + lo : 2 * width + lo + PAIR]
        d_pair = d_context[:, lo : lo + PAIR]
        dq, dk, dv = [], [], []
        for half, mask in enumerate(ones):
            probs = probs_ref[2 * pair + half, :, row0:end]
            wide = probs.astype(F32)
            d_probs = dot(vals, d_pair * mask, NT)
            mean = jnp.sum(wide * d_probs, axis=0, keepdims=True)
            d_scores = (wide * (d_probs - mean) * head**-0.5).astype(BF)
            dq.append(dot(d_scores, keys, TN))
            dk.append(dot(d_scores, queries))
            dv.append(dot(probs, d_pair))
        d_queries.append(join(dq).astype(BF))
        for side, value in enumerate((join(dk)[0:end], join(dv)[0:end])):
            base = side * width + lo
            if later is not None:
                value = value + later[0:end, base : base + PAIR]
            d_sides[side].append(value[row0:end].astype(BF))
            if earlier is not None:
                earlier[:, base : base + PAIR] = value[0:row0]
    return jnp.concatenate([*d_queries, *d_sides[0], *d_sides[1]], axis=1)


def whole(refs):
    return jnp.concatenate([ref[...] for ref in refs], axis=0)


def split(value, refs):
    rows = refs[0].shape[0]
    for c, ref in enumerate(refs):
        ref[...] = value[c * rows : (c + 1) * rows]


def relax_kernel(smem, ins, outs, layers):
    even, odd = layers
    even.start(FORWARD)
    odd.start(FORWARD)
    length = smem[0][0]
    state = ins[0][...]
    state = state + STEP * forward_rows(state, even, length)[0]
    outs[0][...] = state + STEP * forward_rows(state, odd, length)[0]


def fine_kernel(smem, ins, outs, layers):
    even, odd = layers
    even.start(FORWARD)
    odd.start(FORWARD)
    length = smem[0][0]
    state = jnp.where(smem[1][0] == 1, ins[0][...], ins[1][...])
    value = forward_rows(state, even, length)[0]
    middle = state + STEP * value
    split(state, outs[0:CHUNKS])
    split(middle, outs[CHUNKS : 2 * CHUNKS])
    coarse = state + 2.0 * STEP * value
    end = middle + STEP * forward_rows(middle, odd, length)[0]
    split(end, outs[2 * CHUNKS : 3 * CHUNKS])
    split(end - coarse, outs[3 * CHUNKS : 4 * CHUNKS])


def coarse_kernel(chunk, smem, ins, outs, layers):
    (even,) = layers
    even.start(FORWARD)
    state, defect = ins[0:2]
    old = ins[2][...] if chunk > 0 else None
    current = state[...]
    rows = current.shape[0]
    value, own = forward_rows(
        current, even, smem[0][0], chunk * rows, old, CHUNKS * rows
    )
    outs[0][...] = current
    outs[1][...] = current + STEP * value
    outs[2][...] = current + 2.0 * STEP * value + defect[...]
    if len(outs) > 3:
        if chunk > 0:
            outs[3][0 : chunk * rows, :] = old
        outs[3][chunk * rows :, :] = own


def turn_kernel(smem, ins, outs, layers):
    even, odd = layers
    odd.start(FORWARD)
    even.start(FORWARD)
    length = smem[0][0]
    corrected, middles, ends = (whole(ins[i * CHUNKS : (i + 1) * CHUNKS]) for i in range(3))
    target = ins[3 * CHUNKS]
    even_saved, odd_saved = outs[0:3], outs[3:6]
    guess_ref, out, corrected_ref, middles_ref, ends_ref = outs[6:]
    corrected_ref[...] = corrected
    middles_ref[...] = middles
    ends_ref[...] = ends
    position = lax.broadcasted_iota(jnp.int32, ends.shape, 0)
    guess_ref[...] = jnp.where(position < length, ends - target[...], 0.0)
    linearize_rows(middles, odd, length, odd_saved)
    linearize_rows(corrected, even, length, even_saved)
    state = guess_ref[...]
    state = state + STEP * backward_rows(state, middles, odd, [odd_saved])
    out[...] = state + STEP * backward_rows(state, corrected, even, [even_saved])


def back_kernel(smem, ins, outs, layers):
    even, odd = layers
    odd.start(BACKWARD)
    even.start(BACKWARD)
    guess, received, corrected, middles = ins[0:4]
    even_saved, odd_saved = ins[4:7], ins[7:10]
    state = jnp.where(smem[0][0] == 1, guess[...], received[...])
    split(state, outs[0:CHUNKS])
    state = state + STEP * backward_rows(state, middles[...], odd, [odd_saved])
    state = state + STEP * backward_rows(state, corrected[...], even, [even_saved])
    split(state, outs[CHUNKS : 2 * CHUNKS])


def adjoint_kernel(chunk, smem, ins, outs, layers):
    (even,) = layers
    even.start(BACKWARD)
    incoming, relaxed, fine, corrected = ins[0:4]
    saved = ins[4:7]
    later = ins[7] if chunk < CHUNKS - 1 else None
    rows = incoming.shape[0]
    current = incoming[...]
    gap = current - relaxed[...]
    state = corrected[chunk * rows : (chunk + 1) * rows, :]
    change = backward_rows(
        gap, state, even, [saved], chunk * rows, later, outs[2] if chunk > 0 else None
    )
    outs[0][...] = current
    outs[1][...] = fine[...] + (gap + 2.0 * STEP * change)


def first_block_kernel(smem, ins, outs, layers):
    del smem
    (even,) = layers
    even.start(BACKWARD)
    current, relaxed, fine = (whole(ins[i * CHUNKS : (i + 1) * CHUNKS]) for i in range(3))
    gap = current - relaxed
    change = backward_rows(gap, ins[3 * CHUNKS][...], even, [ins[3 * CHUNKS + 1 :]])
    split(fine + (gap + 2.0 * STEP * change), outs)


def pick(place, blocks, held):
    for i, group in enumerate(blocks):

        @pl.when(place == i)
        def _(group=group):
            first = 0
            for ref in group:
                held[first : first + ref.shape[0], :] = ref[...]
                first += ref.shape[0]


def all_linear_kernel(order, smem, ins, moving, outs, layers, held):
    del moving
    pick(
        order[pl.program_id(0)], [ins[i : i + PIECES] for i in range(0, len(ins), PIECES)], held
    )
    even, odd = layers
    fetch((even, odd))
    corrected, middles = outs[0:2]
    even_saved, odd_saved = ([ref.at[i] for ref in outs[2:5]] for i in range(2))
    even_factors, odd_factors = ([ref.at[i] for ref in outs[5:8]] for i in range(2))
    length = smem[0][order[pl.program_id(0)]]
    state = held[...]
    corrected[...] = state
    context, hidden = linearize_rows(state, even, length, even_saved, even_factors)
    value = dot(context, even.get(OUT)[...]) + dot(hidden, even.get(DOWN)[...])
    middle = state + STEP * value
    middles[...] = middle
    settle(odd)
    linearize_rows(middle, odd, length, odd_saved, odd_factors)


def all_back_kernel(order, smem, ins, moving, outs, layers, held):
    del smem
    blocks = [ins[i : i + PIECES] for i in range(0, len(ins), PIECES)]
    pick(order[pl.program_id(0)], blocks, held)
    even, odd = layers
    fetch((odd, even))
    corrected, middles = (ref[...] for ref in moving[0:2])
    even_saved, odd_saved = ([[ref.at[i] for ref in moving[2:5]]] for i in range(2))
    even_right, odd_right = ([ref.at[i] for ref in outs] for i in range(2))
    state = held[...]
    change = backward_rows(state, middles, odd, odd_saved, right=odd_right)
    state = state + STEP * change
    settle(even)
    backward_rows(state, corrected, even, even_saved, right=even_right)


def gradient_kernel(count, steps, *refs):
    (normed, context, hidden), (d_packed, d_up, low) = refs[0:3], refs[3:6]
    outs, sums, sems = refs[6:10], refs[10:14], refs[14]
    layer, k = pl.program_id(0), pl.program_id(1)
    pairs = ((normed, d_packed), (context, low), (normed, d_up), (hidden, low))
    total = jnp.zeros((1, TILE), F32)
    for (left, right), held in zip(pairs, sums):
        for i in range(right.shape[2] // TILE):
            cols = at(i, TILE)
            value = STEP * dot(left[...], right[:, :, cols].reshape(left.shape[1], TILE))
            if steps > 1:
                value = jnp.where(k == 0, value, held[layer, :, cols] + value)
            held[layer, :, cols] = value
            total = total + jnp.sum(value * value, axis=0, keepdims=True)

    def copies(index):
        return [
            pltpu.make_async_copy(held.at[index], out.at[index], sems.at[i])
            for i, (held, out) in enumerate(zip(sums, outs))
        ]

    @pl.when(k == pl.num_programs(1) - 1)
    def _():
        square = jnp.sum(total, axis=1, keepdims=True)
        inverse = 1.0 / jnp.sqrt(square / count + 1e-06)
        for held in sums:
            held[layer] = held[layer] * inverse

        @pl.when(layer == 0)
        def _():
            for copy in copies(0):
                copy.start()

        @pl.when(layer == 1)
        def _():
            for copy in copies(0):
                copy.wait()
            for copy in copies(1):
                copy.start()
            for copy in copies(1):
                copy.wait()


def gradients(lefts, rights, weights):
    _, count, rows, _ = rights[0].shape
    group = min(count, 4)
    sizes = [w.shape[1:] for w in weights]
    blocks = [(2, x.shape[1] * group * rows) for x in lefts]
    blocks += [(2, group * rows * x.shape[3]) for x in rights]
    return pl.pallas_call(
        functools.partial(
            gradient_kernel, float(sum(math.prod(size) for size in sizes)), count // group
        ),
        grid=(2, count // group),
        in_specs=[
            pl.BlockSpec((None, x.shape[1], group * rows), lambda i, k: (i, 0, k)) for x in lefts
        ]
        + [
            pl.BlockSpec((None, group, rows, x.shape[3]), lambda i, k: (i, k, 0, 0))
            for x in rights
        ],
        out_specs=tuple(pl.BlockSpec(memory_space=pl.ANY) for _ in sizes),
        out_shape=tuple(jax.ShapeDtypeStruct((2, *size), F32) for size in sizes),
        scratch_shapes=[pltpu.VMEM((2, *size), F32) for size in sizes]
        + [pltpu.SemaphoreType.DMA((len(sizes),))],
        cost_estimate=pl.CostEstimate(
            flops=4 * count * rows * sum(math.prod(size) for size in sizes),
            bytes_accessed=0,
            transcendentals=0,
        ),
        compiler_params=room(
            [(block, BF) for block in blocks] + [((2, *size), F32) for size in sizes], [None], 8
        ),
    )(*lefts, *rights)


def nothing_kernel(*refs):
    del refs


def scratch(weights, layers):
    shapes = [pltpu.VMEM(w.shape[1:], w.dtype) for _ in layers for w in weights]
    return shapes + [pltpu.SemaphoreType.DMA((len(layers), len(weights)))]


def room(shapes, scratches, spare=10):
    total = sum(math.prod(shape) * jnp.dtype(kind).itemsize for shape, kind in shapes)
    for item in scratches[:-1]:
        total += math.prod(item.shape) * jnp.dtype(item.dtype).itemsize
    return pltpu.CompilerParams(vmem_limit_bytes=int(total * 1.1) + spare * 1024 * 1024)


def unpack(refs, sources, layers, when=None):
    count = len(sources)
    refs, sems = refs[:-1], refs[-1]
    return [
        Layer(index, sources, refs[i * count : (i + 1) * count], sems.at[i], when)
        for i, index in enumerate(layers)
    ]


def cost(rows, weights, layers):
    flops = 2 * rows * sum(math.prod(w.shape[1:]) for w in weights) * layers
    return pl.CostEstimate(flops=6 * flops, bytes_accessed=0, transcendentals=0)


def call(kernel, outs, smem, weights, layers, ins, rows, passes=1, limit=None):
    counts = [len(smem), len(ins), len(weights), len(outs)]
    held = scratch(weights, layers)

    def body(*refs):
        cuts = [sum(counts[:i]) for i in range(5)]
        parts = [refs[cuts[i] : cuts[i + 1]] for i in range(4)]
        kernel(parts[0], parts[1], parts[3], unpack(refs[cuts[4] :], parts[2], layers))

    return pl.pallas_call(
        body,
        out_shape=tuple(jax.ShapeDtypeStruct(shape, kind) for shape, kind in outs),
        in_specs=[pl.BlockSpec(memory_space=pltpu.SMEM)] * len(smem)
        + [pl.BlockSpec(memory_space=pltpu.VMEM)] * len(ins)
        + [pl.BlockSpec(memory_space=pl.ANY)] * len(weights),
        out_specs=tuple(pl.BlockSpec(memory_space=pltpu.VMEM) for _ in outs),
        scratch_shapes=held,
        cost_estimate=cost(rows, weights, passes),
        compiler_params=pltpu.CompilerParams(vmem_limit_bytes=limit)
        if limit
        else room([*((x.shape, x.dtype) for x in ins), *outs], held),
    )(*smem, *ins, *weights)


def call_each(kernel, outs, order, smem, gathered, weights, moving=(), limit=None, reused=()):
    rows = sum(x.shape[0] for x in gathered) // order.shape[0]
    width = gathered[0].shape[1]
    specs = [pl.BlockSpec(shape, index) for _, _, shape, index in outs]
    sizes = [[size for size in shape if size] for _, _, shape, _ in outs]
    outs = [(shape, kind) for shape, kind, _, _ in outs]
    held = scratch(weights, (0, 1))
    counts = [len(smem), len(gathered), len(weights), len(moving), len(outs)]

    before = 1 + len(smem) + len(gathered) + len(weights)
    moving_specs = [pl.BlockSpec(shape, index) for _, shape, index in moving]
    moving = [array for array, _, _ in moving]

    def body(order_ref, *refs):
        cuts = [sum(counts[:i]) for i in range(6)]
        parts = [refs[cuts[i] : cuts[i + 1]] for i in range(5)]
        first = pl.program_id(0) == 0
        layers = unpack(refs[cuts[5] : -1], parts[2], (0, 1), first)
        kernel(order_ref, parts[0], parts[1], parts[3], parts[4], layers, refs[-1])

    return pl.pallas_call(
        body,
        grid_spec=pltpu.PrefetchScalarGridSpec(
            num_scalar_prefetch=1,
            grid=order.shape,
            in_specs=[pl.BlockSpec(memory_space=pltpu.SMEM)] * len(smem)
            + [pl.BlockSpec(memory_space=pltpu.VMEM)] * len(gathered)
            + [pl.BlockSpec(memory_space=pl.ANY)] * len(weights)
            + moving_specs,
            out_specs=tuple(specs),
            scratch_shapes=held + [pltpu.VMEM((rows, width), F32)],
        ),
        out_shape=tuple(jax.ShapeDtypeStruct(shape, kind) for shape, kind in outs),
        cost_estimate=cost(rows, weights, 4 * order.shape[0]),
        input_output_aliases={before + i: o for i, o in reused},
        compiler_params=pltpu.CompilerParams(vmem_limit_bytes=limit)
        if limit
        else room(
            [(x.shape, x.dtype) for x in gathered]
            + 2 * [(shape, kind) for shape, (_, kind) in zip(sizes, outs)],
            held,
        ),
    )(order, *smem, *gathered, *weights, *moving)


def unwritten(outs):
    return pl.pallas_call(
        nothing_kernel,
        out_shape=tuple(jax.ShapeDtypeStruct(shape, kind) for shape, kind in outs),
        out_specs=tuple(pl.BlockSpec(memory_space=pl.ANY) for _ in outs),
    )()


def gather_dp(block, then=None):
    count = lax.axis_size("dp")
    if count == 1:
        return [block]
    swap = [(i, i ^ 1) for i in range(count)]
    mine = [block]
    for turn in range(1, count // 2):
        route = [(i, (i + 2 * turn) % count) for i in range(count)]
        mine.append(lax.ppermute(block, "dp", route))
    theirs = [lax.ppermute(block, "dp", swap)]
    if then is not None:
        mine, _ = lax.optimization_barrier((mine, then))
    theirs += [lax.ppermute(own, "dp", swap) for own in mine[1:]]
    return [x for pair in zip(mine, theirs) for x in pair]


def joined(chunks):
    size = len(chunks) // PIECES
    return [jnp.concatenate(chunks[i : i + size], axis=0) for i in range(0, len(chunks), size)]


def gathered_order():
    count = lax.axis_size("dp")
    place = lax.axis_index("dp")
    other = jnp.arange(count, dtype=jnp.int32)
    turn = (place // 2 - other // 2) % max(count // 2, 1)
    return (2 * turn + (place + other) % 2).astype(jnp.int32) if count > 1 else other


def on_device(states, target, lengths, qkv_weight, out_weight, up_weight, down_weight):
    layer_count = lax.axis_size("layer")
    device = lax.axis_index("layer")
    weights = (qkv_weight, out_weight, up_weight, down_weight)
    starts, goal = states[0, 0], target[0]
    rows, width = starts.shape
    hidden = up_weight.shape[2]
    part = rows // CHUNKS
    full = ((rows, width), F32)
    piece = ((part, width), F32)
    saved = (((rows, 3 * width), BF), ((HEADS, rows, rows), BF), ((rows, hidden), BF))
    sizes = jnp.concatenate(gather_dp(lengths))
    both, first_layer = (0, 1), (0,)
    order = gathered_order()
    count = order.shape[0]
    is_first = (device == 0).astype(jnp.int32).reshape(1)
    is_last = (device == layer_count - 1).astype(jnp.int32).reshape(1)

    (first_end,) = call(relax_kernel, (full,), (lengths,), weights, both, (starts,), rows, 2)
    received = lax.ppermute(
        first_end, "layer", [(i, i + 1) for i in range(layer_count - 1)]
    )
    received, sizes = lax.optimization_barrier((received, sizes))
    got = call(
        fine_kernel, (piece,) * (4 * CHUNKS), (lengths, is_first), weights, both,
        (starts, received), rows, 2,
    )
    corrected, middles, ends, defect = (
        list(got[i * CHUNKS : (i + 1) * CHUNKS]) for i in range(4)
    )
    stores = [jnp.zeros((c * part, 2 * width), BF) for c in range(1, CHUNKS)]
    for block in range(2, layer_count):
        incoming = [lax.ppermute(ends[c], "layer", [(block - 1, block)]) for c in range(CHUNKS)]
        for c in range(CHUNKS):
            outs = (piece, piece, piece)
            kept = (corrected[c], middles[c], ends[c])
            if c < CHUNKS - 1:
                outs += (((((c + 1) * part), 2 * width), BF),)
                kept += (stores[c],)
            old = () if c == 0 else (stores[c - 1],)
            got = lax.cond(
                device == block,
                functools.partial(
                    call, functools.partial(coarse_kernel, c), outs, (lengths,), weights,
                    first_layer, (incoming[c], defect[c], *old), part,
                ),
                lambda kept=kept: kept,
            )
            corrected[c], middles[c], ends[c] = got[0:3]
            if c < CHUNKS - 1:
                stores[c] = got[3]
    chunks = corrected
    *kept, guess, turned, corrected, middles, ends = call(
        turn_kernel, (*saved, *saved, full, full, full, full, full), (lengths,), weights, both,
        (*corrected, *middles, *ends, goal), rows, 6,
    )
    even_saved = kept[0:3]
    received = lax.ppermute(
        turned, "layer", [(i + 1, i) for i in range(layer_count - 1)]
    )
    linear_outs = [
        ((count, rows, width), F32, (None, rows, width), lambda i, order: (i, 0, 0))
    ] * 2 + [
        ((2, count, *shape), kind, (2, None, *shape), lambda i, order, n=len(shape): (0, i) + (0,) * n)
        for shape, kind in saved
    ]
    linear_outs += [
        ((2, columns, count * rows), BF, (2, columns, rows), lambda i, order: (0, 0, i))
        for columns in (width, width, hidden)
    ]
    gathered = [gather_dp(piece, turned) for piece in joined(chunks)]
    every = [piece[i] for i in range(count) for piece in gathered]

    def all_linear():
        return tuple(
            call_each(
                all_linear_kernel, linear_outs, order, (sizes,), every, weights
            )
        )

    linear = lax.cond(device < layer_count - 2, all_linear, lambda: tuple(unwritten([out[0:2] for out in linear_outs])))
    received, linear = lax.optimization_barrier((received, linear))
    got = call(
        back_kernel, (piece,) * (2 * CHUNKS), (is_last,), weights, both,
        (guess, received, corrected, middles, *kept), rows, 4, WHOLE_LIMIT,
    )
    relaxed, fine = got[0:CHUNKS], got[CHUNKS:]
    adjoint_ends, adjoint_out = list(relaxed), list(fine)
    carried = [jnp.zeros((c * part, 2 * width), F32) for c in range(1, CHUNKS)]
    for block in range(layer_count - 3, -1, -1):
        incoming = [
            lax.ppermute(adjoint_out[c], "layer", [(block + 1, block)])
            for c in range(CHUNKS - 1, -1, -1)
        ][::-1]
        if block == 0:
            adjoint_ends = [
                jnp.where(device == 0, new, old) for new, old in zip(incoming, adjoint_ends)
            ]
            gathered = [gather_dp(piece) for piece in joined(adjoint_ends)[::-1]][::-1]
            adjoint_out = lax.cond(
                device == 0,
                functools.partial(
                    call, first_block_kernel, (piece,) * CHUNKS, (), weights, first_layer,
                    (*incoming, *relaxed, *fine, corrected, *even_saved), rows, 2,
                ),
                lambda adjoint_out=adjoint_out: tuple(adjoint_out),
            )
            break
        for c in range(CHUNKS - 1, -1, -1):
            outs = (piece, piece)
            old = (adjoint_ends[c], adjoint_out[c])
            if c > 0:
                outs += (((c * part, 2 * width), F32),)
                old += (carried[c - 1],)
            later = () if c == CHUNKS - 1 else (carried[c],)
            got = lax.cond(
                device == block,
                functools.partial(
                    call, functools.partial(adjoint_kernel, c), outs, (), weights,
                    first_layer, (incoming[c], relaxed[c], fine[c], corrected, *even_saved, *later),
                    part, 2,
                ),
                lambda old=old: old,
            )
            adjoint_ends[c], adjoint_out[c] = got[0:2]
            if c > 0:
                carried[c - 1] = got[2]
    linear, adjoint_out = lax.optimization_barrier((linear, adjoint_out))
    linear = lax.cond(device < layer_count - 2, lambda: linear, all_linear)
    every_adjoint = [piece[i] for i in range(count) for piece in gathered]
    moving = [(array, *out[2:4]) for array, out in zip(linear[0:5], linear_outs)]
    rights = [linear_outs[2], linear_outs[4]]
    rights += [
        ((2, count, rows, width), BF, (2, None, rows, width), lambda i, order: (0, i, 0, 0))
    ]
    got = call_each(
        all_back_kernel, rights, order, (), every_adjoint, weights, moving, WHOLE_LIMIT,
        ((2, 0), (4, 1)),
    )
    results = gradients(linear[5:8], got, weights)
    adjoint_out = jnp.concatenate(adjoint_out, axis=0)
    return (ends[None, None], adjoint_out[None, None], *results)


def solution(mesh):
    in_specs = (
        P("layer", "dp", None, None),
        P("dp", None, None),
        P("dp"),
        P("layer", None, None),
        P("layer", None, None),
        P("layer", None, None),
        P("layer", None, None),
    )
    out_specs = (
        P("layer", "dp", None, None),
        P("layer", "dp", None, None),
        P("layer", None, None),
        P("layer", None, None),
        P("layer", None, None),
        P("layer", None, None),
    )
    return jax.shard_map(
        on_device, mesh=mesh, in_specs=in_specs, out_specs=out_specs, check_vma=False
    )
```

```python
import functools
import math

import jax
import jax.numpy as jnp
from jax import lax
from jax.experimental import pallas as pl
from jax.experimental.pallas import tpu as pltpu
from jax.sharding import PartitionSpec as P

HEADS = 8
STEP = 0.125
CHUNKS = 2
PAIR = 128
TILE = 512
PIECES = 2
WHOLE_LIMIT = 60 * 1024 * 1024

BF = jnp.bfloat16
F32 = jnp.float32
NN = ((1,), (0,))
NT = ((1,), (1,))
TN = ((0,), (0,))
GELU_A = math.sqrt(2.0 / math.pi)
GELU_B = 0.044715


def dot(a, b, dims=NN):
    return lax.dot_general(a, b, (dims, ((), ())), preferred_element_type=F32)


def norm_scale(u):
    return lax.rsqrt(jnp.mean(u * u, axis=-1, keepdims=True) + 1e-06)


def half_masks(value):
    lane = lax.broadcasted_iota(jnp.int32, (1, PAIR), 1)
    first = jnp.where(lane < PAIR // 2, value, 0.0).astype(BF)
    second = jnp.where(lane < PAIR // 2, 0.0, value).astype(BF)
    return (first, second)


def join(pair):
    lane = lax.broadcasted_iota(jnp.int32, pair[0].shape, 1)
    return jnp.where(lane < PAIR // 2, pair[0], pair[1])


def gelu_parts(x):
    inner = jnp.tanh(GELU_A * (x + GELU_B * (x * x * x)))
    return 0.5 * (1.0 + inner), inner


def at(i, size, base=0):
    return slice(base + i * size, base + (i + 1) * size)


def loop(count, body):
    for i in range(count):
        body(i)


class Layer:
    def __init__(self, index, sources, targets, sems, when=None):
        self.index, self.sources, self.targets, self.sems = index, sources, targets, sems
        self.when, self.waiting = when, set()

    def copy(self, i):
        source = self.sources[i].at[self.index]
        return pltpu.make_async_copy(source, self.targets[i], self.sems.at[i])

    def start(self, order):
        if self.when is None:
            for i in order:
                self.copy(i).start()
            self.waiting = set(order)

    def get(self, i):
        if i in self.waiting:
            self.copy(i).wait()
            self.waiting.remove(i)
        return self.targets[i]


def fetch(layers):
    @pl.when(layers[0].when)
    def _():
        for layer in layers:
            for i in range(len(layer.targets)):
                layer.copy(i).start()
        for i in range(len(layers[0].targets)):
            layers[0].copy(i).wait()


def settle(layer):
    @pl.when(layer.when)
    def _():
        for i in range(len(layer.targets)):
            layer.copy(i).wait()


QKV, OUT, UP, DOWN = range(4)
FORWARD = (QKV, UP, OUT, DOWN)
BACKWARD = (OUT, DOWN, QKV, UP)


def attention_sides(packed, pair, width):
    cols = pair * PAIR
    return [packed[:, base + cols : base + cols + PAIR] for base in (0, width, 2 * width)]


def forward_rows(u, layer, length, row0=0, old=None, whole_rows=0):
    rows, width = u.shape
    head = width // HEADS
    normed = (u * norm_scale(u)).astype(BF)
    packed = dot(normed, layer.get(QKV)[...]).astype(BF)
    own = packed[:, width:]
    both = own if old is None else jnp.concatenate([old, own], axis=0)
    spare = whole_rows - both.shape[0]
    if spare > 0:
        both = jnp.concatenate([both, *([own] * (spare // rows))], axis=0)
    shape = (rows, both.shape[0])
    key_pos = lax.broadcasted_iota(jnp.int32, shape, 1)
    query_pos = lax.broadcasted_iota(jnp.int32, shape, 0) + row0
    seen = (key_pos <= query_pos) & (key_pos < length)
    masks = half_masks(head**-0.5)
    parts = []
    for pair in range(width // PAIR):
        cols = slice(pair * PAIR, (pair + 1) * PAIR)
        keys, vals = both[:, cols], both[:, width + pair * PAIR : width + (pair + 1) * PAIR]
        outs = []
        for mask in masks:
            scores = dot(packed[:, cols] * mask, keys, NT)
            scores = jnp.where(seen, scores, -jnp.inf)
            weight = jnp.exp(scores - jnp.max(scores, axis=-1, keepdims=True))
            probs = (weight * (1.0 / jnp.sum(weight, axis=-1, keepdims=True))).astype(BF)
            outs.append(dot(probs, vals))
        parts.append(join(outs).astype(BF))
    context = jnp.concatenate(parts, axis=1)
    up = dot(normed, layer.get(UP)[...])
    hidden = (up * gelu_parts(up)[0]).astype(BF)
    return dot(context, layer.get(OUT)[...]) + dot(hidden, layer.get(DOWN)[...]), own


def linearize_rows(u, layer, length, saved, factors=None):
    packed_ref, probs_ref, slope_ref = saved
    rows, width = u.shape
    head = width // HEADS
    wide = u * norm_scale(u)
    normed = wide.astype(BF)
    packed = dot(normed, layer.get(QKV)[...]).astype(BF)
    packed_ref[...] = packed
    key_pos = lax.broadcasted_iota(jnp.int32, (rows, rows), 0)
    query_pos = lax.broadcasted_iota(jnp.int32, (rows, rows), 1)
    seen = (key_pos <= query_pos) & (key_pos < length)
    masks = half_masks(head**-0.5)
    parts = []
    for pair in range(width // PAIR):
        queries, keys, vals = attention_sides(packed, pair, width)
        outs = []
        for half, mask in enumerate(masks):
            scores = dot(keys, queries * mask, NT)
            scores = jnp.where(seen, scores, -jnp.inf)
            weight = jnp.exp(scores - jnp.max(scores, axis=0, keepdims=True))
            probs = (weight * (1.0 / jnp.sum(weight, axis=0, keepdims=True))).astype(BF)
            probs_ref[2 * pair + half] = probs
            if factors is not None:
                outs.append(dot(probs, vals, TN))
        if factors is not None:
            parts.append(join(outs))
    up = dot(normed, layer.get(UP)[...])
    gate, inner = gelu_parts(up)
    rise = GELU_A + 3.0 * GELU_A * GELU_B * up * up
    slope_ref[...] = (gate + 0.5 * up * (1.0 - inner * inner) * rise).astype(BF)
    if factors is None:
        return None
    context, hidden = jnp.concatenate(parts, axis=1), up * gate
    for ref, value in zip(factors, (wide, context, hidden)):
        ref[...] = value.T.astype(BF)
    return context.astype(BF), hidden.astype(BF)


def backward_rows(ct, u, layer, saved, row0=0, later=None, earlier=None, right=None):
    width = ct.shape[1]
    low = ct.astype(BF)
    d_context = dot(low, layer.get(OUT)[...], NT).astype(BF)
    d_hidden = dot(low, layer.get(DOWN)[...], NT)
    rows = ct.shape[0] // len(saved)
    d_ups, d_packs = [], []
    for i, one in enumerate(saved):
        part = slice(i * rows, (i + 1) * rows)
        slope = one[2][row0 : row0 + rows, :].astype(F32)
        d_ups.append((d_hidden[part] * slope).astype(BF))
        d_packs.append(backward_attention(d_context[part], one, row0, later, earlier))
    d_up, d_packed = jnp.concatenate(d_ups, axis=0), jnp.concatenate(d_packs, axis=0)
    if right is not None:
        for ref, value in zip(right, (d_packed, d_up, low)):
            ref[...] = value
    d_normed = dot(d_packed, layer.get(QKV)[...], NT) + dot(d_up, layer.get(UP)[...], NT)
    scale = norm_scale(u)
    unit = u * scale
    return scale * (d_normed - unit * jnp.mean(unit * d_normed, axis=-1, keepdims=True))


def backward_attention(d_context, saved, row0, later, earlier):
    packed_ref, probs_ref, _ = saved
    rows, width = d_context.shape
    head = width // HEADS
    end = row0 + rows
    ones = half_masks(1.0)
    d_queries, d_sides = [], [[], []]
    for pair in range(width // PAIR):
        lo = pair * PAIR
        queries = packed_ref[row0:end, lo : lo + PAIR]
        keys = packed_ref[:, width + lo : width + lo + PAIR]
        vals = packed_ref[:, 2 * width + lo : 2 * width + lo + PAIR]
        d_pair = d_context[:, lo : lo + PAIR]
        dq, dk, dv = [], [], []
        for half, mask in enumerate(ones):
            probs = probs_ref[2 * pair + half, :, row0:end]
            wide = probs.astype(F32)
            d_probs = dot(vals, d_pair * mask, NT)
            mean = jnp.sum(wide * d_probs, axis=0, keepdims=True)
            d_scores = (wide * (d_probs - mean) * head**-0.5).astype(BF)
            dq.append(dot(d_scores, keys, TN))
            dk.append(dot(d_scores, queries))
            dv.append(dot(probs, d_pair))
        d_queries.append(join(dq).astype(BF))
        for side, value in enumerate((join(dk)[0:end], join(dv)[0:end])):
            base = side * width + lo
            if later is not None:
                value = value + later[0:end, base : base + PAIR]
            d_sides[side].append(value[row0:end].astype(BF))
            if earlier is not None:
                earlier[:, base : base + PAIR] = value[0:row0]
    return jnp.concatenate([*d_queries, *d_sides[0], *d_sides[1]], axis=1)


def whole(refs):
    return jnp.concatenate([ref[...] for ref in refs], axis=0)


def split(value, refs):
    rows = refs[0].shape[0]
    for c, ref in enumerate(refs):
        ref[...] = value[c * rows : (c + 1) * rows]


def relax_kernel(smem, ins, outs, layers):
    even, odd = layers
    even.start(FORWARD)
    odd.start(FORWARD)
    length = smem[0][0]
    state = ins[0][...]
    state = state + STEP * forward_rows(state, even, length)[0]
    outs[0][...] = state + STEP * forward_rows(state, odd, length)[0]


def fine_kernel(smem, ins, outs, layers):
    even, odd = layers
    even.start(FORWARD)
    odd.start(FORWARD)
    length = smem[0][0]
    state = jnp.where(smem[1][0] == 1, ins[0][...], ins[1][...])
    value = forward_rows(state, even, length)[0]
    middle = state + STEP * value
    split(state, outs[0:CHUNKS])
    split(middle, outs[CHUNKS : 2 * CHUNKS])
    coarse = state + 2.0 * STEP * value
    end = middle + STEP * forward_rows(middle, odd, length)[0]
    split(end, outs[2 * CHUNKS : 3 * CHUNKS])
    split(end - coarse, outs[3 * CHUNKS : 4 * CHUNKS])


def coarse_kernel(chunk, smem, ins, outs, layers):
    (even,) = layers
    even.start(FORWARD)
    state, defect = ins[0:2]
    old = ins[2][...] if chunk > 0 else None
    current = state[...]
    rows = current.shape[0]
    value, own = forward_rows(
        current, even, smem[0][0], chunk * rows, old, CHUNKS * rows
    )
    outs[0][...] = current
    outs[1][...] = current + STEP * value
    outs[2][...] = current + 2.0 * STEP * value + defect[...]
    if len(outs) > 3:
        if chunk > 0:
            outs[3][0 : chunk * rows, :] = old
        outs[3][chunk * rows :, :] = own


def turn_kernel(smem, ins, outs, layers):
    even, odd = layers
    odd.start(FORWARD)
    even.start(FORWARD)
    length = smem[0][0]
    corrected, middles, ends = (whole(ins[i * CHUNKS : (i + 1) * CHUNKS]) for i in range(3))
    target = ins[3 * CHUNKS]
    even_saved, odd_saved = outs[0:3], outs[3:6]
    guess_ref, out, corrected_ref, middles_ref, ends_ref = outs[6:]
    corrected_ref[...] = corrected
    middles_ref[...] = middles
    ends_ref[...] = ends
    position = lax.broadcasted_iota(jnp.int32, ends.shape, 0)
    guess_ref[...] = jnp.where(position < length, ends - target[...], 0.0)
    linearize_rows(middles, odd, length, odd_saved)
    linearize_rows(corrected, even, length, even_saved)
    state = guess_ref[...]
    state = state + STEP * backward_rows(state, middles, odd, [odd_saved])
    out[...] = state + STEP * backward_rows(state, corrected, even, [even_saved])


def back_kernel(smem, ins, outs, layers):
    even, odd = layers
    odd.start(BACKWARD)
    even.start(BACKWARD)
    guess, received, corrected, middles = ins[0:4]
    even_saved, odd_saved = ins[4:7], ins[7:10]
    state = jnp.where(smem[0][0] == 1, guess[...], received[...])
    split(state, outs[0:CHUNKS])
    state = state + STEP * backward_rows(state, middles[...], odd, [odd_saved])
    state = state + STEP * backward_rows(state, corrected[...], even, [even_saved])
    split(state, outs[CHUNKS : 2 * CHUNKS])


def adjoint_kernel(chunk, smem, ins, outs, layers):
    (even,) = layers
    even.start(BACKWARD)
    incoming, relaxed, fine, corrected = ins[0:4]
    saved = ins[4:7]
    later = ins[7] if chunk < CHUNKS - 1 else None
    rows = incoming.shape[0]
    current = incoming[...]
    gap = current - relaxed[...]
    state = corrected[chunk * rows : (chunk + 1) * rows, :]
    change = backward_rows(
        gap, state, even, [saved], chunk * rows, later, outs[2] if chunk > 0 else None
    )
    outs[0][...] = current
    outs[1][...] = fine[...] + (gap + 2.0 * STEP * change)


def first_block_kernel(smem, ins, outs, layers):
    del smem
    (even,) = layers
    even.start(BACKWARD)
    current, relaxed, fine = (whole(ins[i * CHUNKS : (i + 1) * CHUNKS]) for i in range(3))
    gap = current - relaxed
    change = backward_rows(gap, ins[3 * CHUNKS][...], even, [ins[3 * CHUNKS + 1 :]])
    split(fine + (gap + 2.0 * STEP * change), outs)


def pick(place, blocks, held):
    for i, group in enumerate(blocks):

        @pl.when(place == i)
        def _(group=group):
            first = 0
            for ref in group:
                held[first : first + ref.shape[0], :] = ref[...]
                first += ref.shape[0]


def all_linear_kernel(order, smem, ins, moving, outs, layers, held):
    del moving
    pick(
        order[pl.program_id(0)], [ins[i : i + PIECES] for i in range(0, len(ins), PIECES)], held
    )
    even, odd = layers
    fetch((even, odd))
    corrected, middles = outs[0:2]
    even_saved, odd_saved = ([ref.at[i] for ref in outs[2:5]] for i in range(2))
    even_factors, odd_factors = ([ref.at[i] for ref in outs[5:8]] for i in range(2))
    length = smem[0][order[pl.program_id(0)]]
    state = held[...]
    corrected[...] = state
    context, hidden = linearize_rows(state, even, length, even_saved, even_factors)
    value = dot(context, even.get(OUT)[...]) + dot(hidden, even.get(DOWN)[...])
    middle = state + STEP * value
    middles[...] = middle
    settle(odd)
    linearize_rows(middle, odd, length, odd_saved, odd_factors)


def all_back_kernel(order, smem, ins, moving, outs, layers, held):
    del smem
    blocks = [ins[i : i + PIECES] for i in range(0, len(ins), PIECES)]
    pick(order[pl.program_id(0)], blocks, held)
    even, odd = layers
    fetch((odd, even))
    corrected, middles = (ref[...] for ref in moving[0:2])
    even_saved, odd_saved = ([[ref.at[i] for ref in moving[2:5]]] for i in range(2))
    even_right, odd_right = ([ref.at[i] for ref in outs] for i in range(2))
    state = held[...]
    change = backward_rows(state, middles, odd, odd_saved, right=odd_right)
    state = state + STEP * change
    settle(even)
    backward_rows(state, corrected, even, even_saved, right=even_right)


def gradient_kernel(count, steps, *refs):
    (normed, context, hidden), (d_packed, d_up, low) = refs[0:3], refs[3:6]
    outs, sums, sems = refs[6:10], refs[10:14], refs[14]
    layer, k = pl.program_id(0), pl.program_id(1)
    pairs = ((normed, d_packed), (context, low), (normed, d_up), (hidden, low))
    total = jnp.zeros((1, TILE), F32)
    for (left, right), held in zip(pairs, sums):
        for i in range(right.shape[2] // TILE):
            cols = at(i, TILE)
            value = STEP * dot(left[...], right[:, :, cols].reshape(left.shape[1], TILE))
            if steps > 1:
                value = jnp.where(k == 0, value, held[layer, :, cols] + value)
            held[layer, :, cols] = value
            total = total + jnp.sum(value * value, axis=0, keepdims=True)

    def copies(index):
        return [
            pltpu.make_async_copy(held.at[index], out.at[index], sems.at[i])
            for i, (held, out) in enumerate(zip(sums, outs))
        ]

    @pl.when(k == pl.num_programs(1) - 1)
    def _():
        square = jnp.sum(total, axis=1, keepdims=True)
        inverse = 1.0 / jnp.sqrt(square / count + 1e-06)

        @pl.when(layer == 1)
        def _():
            for copy in copies(0):
                copy.wait()

        for held, copy in zip(sums, copies(layer)):
            held[layer] = held[layer] * inverse
            copy.start()

        @pl.when(layer == 1)
        def _():
            for copy in copies(1):
                copy.wait()


def gradients(lefts, rights, weights):
    _, count, rows, _ = rights[0].shape
    group = min(count, 4)
    sizes = [w.shape[1:] for w in weights]
    blocks = [(2, x.shape[1] * group * rows) for x in lefts]
    blocks += [(2, group * rows * x.shape[3]) for x in rights]
    return pl.pallas_call(
        functools.partial(
            gradient_kernel, float(sum(math.prod(size) for size in sizes)), count // group
        ),
        grid=(2, count // group),
        in_specs=[
            pl.BlockSpec((None, x.shape[1], group * rows), lambda i, k: (i, 0, k)) for x in lefts
        ]
        + [
            pl.BlockSpec((None, group, rows, x.shape[3]), lambda i, k: (i, k, 0, 0))
            for x in rights
        ],
        out_specs=tuple(pl.BlockSpec(memory_space=pl.ANY) for _ in sizes),
        out_shape=tuple(jax.ShapeDtypeStruct((2, *size), F32) for size in sizes),
        scratch_shapes=[pltpu.VMEM((2, *size), F32) for size in sizes]
        + [pltpu.SemaphoreType.DMA((len(sizes),))],
        cost_estimate=pl.CostEstimate(
            flops=4 * count * rows * sum(math.prod(size) for size in sizes),
            bytes_accessed=0,
            transcendentals=0,
        ),
        compiler_params=room(
            [(block, BF) for block in blocks] + [((2, *size), F32) for size in sizes], [None], 8
        ),
    )(*lefts, *rights)


def nothing_kernel(*refs):
    del refs


def scratch(weights, layers):
    shapes = [pltpu.VMEM(w.shape[1:], w.dtype) for _ in layers for w in weights]
    return shapes + [pltpu.SemaphoreType.DMA((len(layers), len(weights)))]


def room(shapes, scratches, spare=10):
    total = sum(math.prod(shape) * jnp.dtype(kind).itemsize for shape, kind in shapes)
    for item in scratches[:-1]:
        total += math.prod(item.shape) * jnp.dtype(item.dtype).itemsize
    return pltpu.CompilerParams(vmem_limit_bytes=int(total * 1.1) + spare * 1024 * 1024)


def unpack(refs, sources, layers, when=None):
    count = len(sources)
    refs, sems = refs[:-1], refs[-1]
    return [
        Layer(index, sources, refs[i * count : (i + 1) * count], sems.at[i], when)
        for i, index in enumerate(layers)
    ]


def cost(rows, weights, layers):
    flops = 2 * rows * sum(math.prod(w.shape[1:]) for w in weights) * layers
    return pl.CostEstimate(flops=6 * flops, bytes_accessed=0, transcendentals=0)


def call(kernel, outs, smem, weights, layers, ins, rows, passes=1, limit=None):
    counts = [len(smem), len(ins), len(weights), len(outs)]
    held = scratch(weights, layers)

    def body(*refs):
        cuts = [sum(counts[:i]) for i in range(5)]
        parts = [refs[cuts[i] : cuts[i + 1]] for i in range(4)]
        kernel(parts[0], parts[1], parts[3], unpack(refs[cuts[4] :], parts[2], layers))

    return pl.pallas_call(
        body,
        out_shape=tuple(jax.ShapeDtypeStruct(shape, kind) for shape, kind in outs),
        in_specs=[pl.BlockSpec(memory_space=pltpu.SMEM)] * len(smem)
        + [pl.BlockSpec(memory_space=pltpu.VMEM)] * len(ins)
        + [pl.BlockSpec(memory_space=pl.ANY)] * len(weights),
        out_specs=tuple(pl.BlockSpec(memory_space=pltpu.VMEM) for _ in outs),
        scratch_shapes=held,
        cost_estimate=cost(rows, weights, passes),
        compiler_params=pltpu.CompilerParams(vmem_limit_bytes=limit)
        if limit
        else room([*((x.shape, x.dtype) for x in ins), *outs], held),
    )(*smem, *ins, *weights)


def call_each(kernel, outs, order, smem, gathered, weights, moving=(), limit=None, reused=()):
    rows = sum(x.shape[0] for x in gathered) // order.shape[0]
    width = gathered[0].shape[1]
    specs = [pl.BlockSpec(shape, index) for _, _, shape, index in outs]
    sizes = [[size for size in shape if size] for _, _, shape, _ in outs]
    outs = [(shape, kind) for shape, kind, _, _ in outs]
    held = scratch(weights, (0, 1))
    counts = [len(smem), len(gathered), len(weights), len(moving), len(outs)]

    before = 1 + len(smem) + len(gathered) + len(weights)
    moving_specs = [pl.BlockSpec(shape, index) for _, shape, index in moving]
    moving = [array for array, _, _ in moving]

    def body(order_ref, *refs):
        cuts = [sum(counts[:i]) for i in range(6)]
        parts = [refs[cuts[i] : cuts[i + 1]] for i in range(5)]
        first = pl.program_id(0) == 0
        layers = unpack(refs[cuts[5] : -1], parts[2], (0, 1), first)
        kernel(order_ref, parts[0], parts[1], parts[3], parts[4], layers, refs[-1])

    return pl.pallas_call(
        body,
        grid_spec=pltpu.PrefetchScalarGridSpec(
            num_scalar_prefetch=1,
            grid=order.shape,
            in_specs=[pl.BlockSpec(memory_space=pltpu.SMEM)] * len(smem)
            + [pl.BlockSpec(memory_space=pltpu.VMEM)] * len(gathered)
            + [pl.BlockSpec(memory_space=pl.ANY)] * len(weights)
            + moving_specs,
            out_specs=tuple(specs),
            scratch_shapes=held + [pltpu.VMEM((rows, width), F32)],
        ),
        out_shape=tuple(jax.ShapeDtypeStruct(shape, kind) for shape, kind in outs),
        cost_estimate=cost(rows, weights, 4 * order.shape[0]),
        input_output_aliases={before + i: o for i, o in reused},
        compiler_params=pltpu.CompilerParams(vmem_limit_bytes=limit)
        if limit
        else room(
            [(x.shape, x.dtype) for x in gathered]
            + 2 * [(shape, kind) for shape, (_, kind) in zip(sizes, outs)],
            held,
        ),
    )(order, *smem, *gathered, *weights, *moving)


def unwritten(outs):
    return pl.pallas_call(
        nothing_kernel,
        out_shape=tuple(jax.ShapeDtypeStruct(shape, kind) for shape, kind in outs),
        out_specs=tuple(pl.BlockSpec(memory_space=pl.ANY) for _ in outs),
    )()


def gather_dp(block, then=None):
    count = lax.axis_size("dp")
    if count == 1:
        return [block]
    swap = [(i, i ^ 1) for i in range(count)]
    mine = [block]
    for turn in range(1, count // 2):
        route = [(i, (i + 2 * turn) % count) for i in range(count)]
        mine.append(lax.ppermute(block, "dp", route))
    theirs = [lax.ppermute(block, "dp", swap)]
    if then is not None:
        mine, _ = lax.optimization_barrier((mine, then))
    theirs += [lax.ppermute(own, "dp", swap) for own in mine[1:]]
    return [x for pair in zip(mine, theirs) for x in pair]


def joined(chunks):
    size = len(chunks) // PIECES
    return [jnp.concatenate(chunks[i : i + size], axis=0) for i in range(0, len(chunks), size)]


def gathered_order():
    count = lax.axis_size("dp")
    place = lax.axis_index("dp")
    other = jnp.arange(count, dtype=jnp.int32)
    turn = (place // 2 - other // 2) % max(count // 2, 1)
    return (2 * turn + (place + other) % 2).astype(jnp.int32) if count > 1 else other


def on_device(states, target, lengths, qkv_weight, out_weight, up_weight, down_weight):
    layer_count = lax.axis_size("layer")
    device = lax.axis_index("layer")
    weights = (qkv_weight, out_weight, up_weight, down_weight)
    starts, goal = states[0, 0], target[0]
    rows, width = starts.shape
    hidden = up_weight.shape[2]
    part = rows // CHUNKS
    full = ((rows, width), F32)
    piece = ((part, width), F32)
    saved = (((rows, 3 * width), BF), ((HEADS, rows, rows), BF), ((rows, hidden), BF))
    sizes = jnp.concatenate(gather_dp(lengths))
    both, first_layer = (0, 1), (0,)
    order = gathered_order()
    count = order.shape[0]
    is_first = (device == 0).astype(jnp.int32).reshape(1)
    is_last = (device == layer_count - 1).astype(jnp.int32).reshape(1)

    (first_end,) = call(relax_kernel, (full,), (lengths,), weights, both, (starts,), rows, 2)
    received = lax.ppermute(
        first_end, "layer", [(i, i + 1) for i in range(layer_count - 1)]
    )
    received, sizes = lax.optimization_barrier((received, sizes))
    got = call(
        fine_kernel, (piece,) * (4 * CHUNKS), (lengths, is_first), weights, both,
        (starts, received), rows, 2,
    )
    corrected, middles, ends, defect = (
        list(got[i * CHUNKS : (i + 1) * CHUNKS]) for i in range(4)
    )
    stores = [jnp.zeros((c * part, 2 * width), BF) for c in range(1, CHUNKS)]
    for block in range(2, layer_count):
        incoming = [lax.ppermute(ends[c], "layer", [(block - 1, block)]) for c in range(CHUNKS)]
        for c in range(CHUNKS):
            outs = (piece, piece, piece)
            kept = (corrected[c], middles[c], ends[c])
            if c < CHUNKS - 1:
                outs += (((((c + 1) * part), 2 * width), BF),)
                kept += (stores[c],)
            old = () if c == 0 else (stores[c - 1],)
            got = lax.cond(
                device == block,
                functools.partial(
                    call, functools.partial(coarse_kernel, c), outs, (lengths,), weights,
                    first_layer, (incoming[c], defect[c], *old), part,
                ),
                lambda kept=kept: kept,
            )
            corrected[c], middles[c], ends[c] = got[0:3]
            if c < CHUNKS - 1:
                stores[c] = got[3]
    chunks = corrected
    *kept, guess, turned, corrected, middles, ends = call(
        turn_kernel, (*saved, *saved, full, full, full, full, full), (lengths,), weights, both,
        (*corrected, *middles, *ends, goal), rows, 6,
    )
    even_saved = kept[0:3]
    received = lax.ppermute(
        turned, "layer", [(i + 1, i) for i in range(layer_count - 1)]
    )
    linear_outs = [
        ((count, rows, width), F32, (None, rows, width), lambda i, order: (i, 0, 0))
    ] * 2 + [
        ((2, count, *shape), kind, (2, None, *shape), lambda i, order, n=len(shape): (0, i) + (0,) * n)
        for shape, kind in saved
    ]
    linear_outs += [
        ((2, columns, count * rows), BF, (2, columns, rows), lambda i, order: (0, 0, i))
        for columns in (width, width, hidden)
    ]
    gathered = [gather_dp(piece, turned) for piece in joined(chunks)]
    every = [piece[i] for i in range(count) for piece in gathered]

    def all_linear():
        return tuple(
            call_each(
                all_linear_kernel, linear_outs, order, (sizes,), every, weights
            )
        )

    linear = lax.cond(device < layer_count - 2, all_linear, lambda: tuple(unwritten([out[0:2] for out in linear_outs])))
    received, linear = lax.optimization_barrier((received, linear))
    got = call(
        back_kernel, (piece,) * (2 * CHUNKS), (is_last,), weights, both,
        (guess, received, corrected, middles, *kept), rows, 4, WHOLE_LIMIT,
    )
    relaxed, fine = got[0:CHUNKS], got[CHUNKS:]
    adjoint_ends, adjoint_out = list(relaxed), list(fine)
    carried = [jnp.zeros((c * part, 2 * width), F32) for c in range(1, CHUNKS)]
    for block in range(layer_count - 3, -1, -1):
        incoming = [
            lax.ppermute(adjoint_out[c], "layer", [(block + 1, block)])
            for c in range(CHUNKS - 1, -1, -1)
        ][::-1]
        if block == 0:
            adjoint_ends = [
                jnp.where(device == 0, new, old) for new, old in zip(incoming, adjoint_ends)
            ]
            gathered = [gather_dp(piece) for piece in joined(adjoint_ends)[::-1]][::-1]
            adjoint_out = lax.cond(
                device == 0,
                functools.partial(
                    call, first_block_kernel, (piece,) * CHUNKS, (), weights, first_layer,
                    (*incoming, *relaxed, *fine, corrected, *even_saved), rows, 2,
                ),
                lambda adjoint_out=adjoint_out: tuple(adjoint_out),
            )
            break
        for c in range(CHUNKS - 1, -1, -1):
            outs = (piece, piece)
            old = (adjoint_ends[c], adjoint_out[c])
            if c > 0:
                outs += (((c * part, 2 * width), F32),)
                old += (carried[c - 1],)
            later = () if c == CHUNKS - 1 else (carried[c],)
            got = lax.cond(
                device == block,
                functools.partial(
                    call, functools.partial(adjoint_kernel, c), outs, (), weights,
                    first_layer, (incoming[c], relaxed[c], fine[c], corrected, *even_saved, *later),
                    part, 2,
                ),
                lambda old=old: old,
            )
            adjoint_ends[c], adjoint_out[c] = got[0:2]
            if c > 0:
                carried[c - 1] = got[2]
    linear, adjoint_out = lax.optimization_barrier((linear, adjoint_out))
    linear = lax.cond(device < layer_count - 2, lambda: linear, all_linear)
    every_adjoint = [piece[i] for i in range(count) for piece in gathered]
    moving = [(array, *out[2:4]) for array, out in zip(linear[0:5], linear_outs)]
    rights = [linear_outs[2], linear_outs[4]]
    rights += [
        ((2, count, rows, width), BF, (2, None, rows, width), lambda i, order: (0, i, 0, 0))
    ]
    got = call_each(
        all_back_kernel, rights, order, (), every_adjoint, weights, moving, WHOLE_LIMIT,
        ((2, 0), (4, 1)),
    )
    results = gradients(linear[5:8], got, weights)
    adjoint_out = jnp.concatenate(adjoint_out, axis=0)
    return (ends[None, None], adjoint_out[None, None], *results)


def solution(mesh):
    in_specs = (
        P("layer", "dp", None, None),
        P("dp", None, None),
        P("dp"),
        P("layer", None, None),
        P("layer", None, None),
        P("layer", None, None),
        P("layer", None, None),
    )
    out_specs = (
        P("layer", "dp", None, None),
        P("layer", "dp", None, None),
        P("layer", None, None),
        P("layer", None, None),
        P("layer", None, None),
        P("layer", None, None),
    )
    return jax.shard_map(
        on_device, mesh=mesh, in_specs=in_specs, out_specs=out_specs, check_vma=False
    )
```
